128 devices in a mesh: row: 16 (over z, x), col: 2 (over y_hi), edge: 4 (over y_lo, core).
Axes of the slice: x: 4, y: 4 (y_hi: 2, y_lo: 2; y = y_hi * 2 + y_lo), z: 4, core: 2. Of those that a mesh axis runs over, the one named last changes fastest.
Arguments:
- features: bfloat16 [65536, 256], P('row', 'col'), may hold values from -6 to 6
- tiles: bfloat16 [45056, 128, 128], P(('row', 'edge')), may hold values from -0.078125 to 0.078125
- tile_rows: int32 [45056], P(('row', 'edge')), may hold values from 0 to 31
- tile_cols: int32 [45056], P(('row', 'edge')), may hold values from 0 to 95
- tile_count: int32 [64], P(('row', 'edge')), may hold values from 88 to 704, as said below
- w_self: bfloat16 [256, 256], P(None, 'col'), may hold values from -0.375 to 0.375
- w_neigh: bfloat16 [256, 256], P(None, 'col'), may hold values from -0.375 to 0.375
- bias: float32 [256], P('col'), may hold values from -3 to 3
- cotangent: bfloat16 [65536, 256], P(('row', 'edge'), 'col'), may hold values from -6 to 6
Outputs:
- output: bfloat16 [65536, 256], P(('row', 'edge'), 'col')
- features_grad: float32 [65536, 256], P(('row', 'edge'), 'col')
- w_self_grad: float32 [256, 256], P(None, 'col')
- w_neigh_grad: float32 [256, 256], P(None, 'col')
- bias_grad: float32 [256], P('col')
The draws below stay inside these ranges and needn't reach their ends.
Inputs may be any that keep to these rules, and one draw needn't show every extreme that they name: `tile_count`: some list uses all 704 slots in every draw.
All inputs are finite; a program needn't handle non-finite values.
Results may differ from the reference program's by a relative error of at most 0.012.
Values may be sent and summed in bfloat16 or wider, within the bound.
A program may use at most 128 MiB of HBM per device.

```python
import math
import jax
import jax.numpy as jnp
from jax import lax

F = 256
TILE = 128
ROW_BLOCKS = 32
TILES_DEV = 704
NODES = 65536
LISTS = 64
SLOTS = 45056
N_ROW = 16
N_EDGE = 4


def draw_tile_count(key, part):
    key = jax.random.fold_in(key, 11)
    first, second, third = jax.random.split(key, 3)
    lowest = max(1, TILES_DEV // 8)
    base = jax.random.randint(first, (LISTS,), lowest, TILES_DEV // 2 + 1)
    heavy = jax.random.randint(second, (LISTS,), 0, 8) == 0
    chosen = jax.random.randint(third, (), 0, LISTS)
    heavy = heavy | (jnp.arange(LISTS) == chosen)
    return jnp.where(heavy, TILES_DEV, base).astype(jnp.int32)


def plant(entries, rng, least, largest):
    dims = entries.shape
    place = [jax.random.randint(jax.random.fold_in(rng, axis), (), 0, dims[axis]) for axis in range(len(dims))]
    entries = entries.at[tuple(place)].set(least)
    longest = dims.index(max(dims))
    place[longest] = (place[longest] + 1) % dims[longest]
    return entries.at[tuple(place)].set(largest)


def block_scale(stream_key, dims, cuts, smallest, top_value):
    level = 1.0
    for dim, blocks in cuts:
        steps = jax.random.uniform(jax.random.fold_in(jax.random.fold_in(stream_key, 6), dim), (blocks,), jnp.float32, smallest / len(cuts), top_value / len(cuts))
        level = level * jnp.repeat(jnp.exp(steps), dims[dim] // blocks).reshape((-1,) + (1,) * (len(dims) - 1 - dim))
    return level


def centred(own_key, extent, spread, limit, cuts=(), kind=jnp.bfloat16):
    values = spread * jax.random.normal(own_key, extent, jnp.float32)
    if cuts:
        values = values * block_scale(own_key, extent, cuts, -0.22, 0.18)
    return jnp.clip(values, -limit, limit).astype(kind)


def setup_inputs(seed: int = 0) -> dict:
    seeds = jax.random.split(jax.random.key(seed), 10)
    return {
        "features": centred(seeds[0], (NODES, F), 1.0, 6.0, ((0, 16), (1, 2))),
        "tiles": centred(seeds[1], (SLOTS, TILE, TILE), (TILES_DEV * TILE * 2 // ROW_BLOCKS) ** -0.5, 0.078125, ((0, 64),)),
        "tile_rows": plant(jax.random.randint(seeds[2], (SLOTS,), 0, ROW_BLOCKS), jax.random.fold_in(seeds[2], 1), 0, ROW_BLOCKS - 1).astype(jnp.int32),
        "tile_cols": plant(jax.random.randint(seeds[3], (SLOTS,), 0, 3 * ROW_BLOCKS), jax.random.fold_in(seeds[3], 1), 0, (3 * ROW_BLOCKS) - 1).astype(jnp.int32),
        "tile_count": draw_tile_count(jax.random.fold_in(seeds[9], 71), 0),
        "w_self": centred(seeds[5], (F, F), F ** -0.5, 0.375, ((1, 2),)),
        "w_neigh": centred(seeds[6], (F, F), F ** -0.5, 0.375, ((1, 2),)),
        "bias": centred(seeds[7], (F,), 0.5, 3.0, ((0, 2),), jnp.float32),
        "cotangent": centred(seeds[8], (NODES, F), 1.0, 6.0, ((0, 64), (1, 2))),
    }


def reference(features, tiles, tile_rows, tile_cols, tile_count, w_self, w_neigh, bias, cotangent):
    f32 = jnp.float32
    nodes, width = features.shape
    rows_dev = nodes // N_ROW
    blocks = rows_dev // TILE
    per_row = N_EDGE * TILES_DEV
    group = 64 if per_row % 64 == 0 else per_row
    live = (jnp.arange(TILES_DEV, dtype=jnp.int32)[None, :] < tile_count[:, None]).astype(f32)
    live = live.reshape(N_ROW, per_row // group, group)
    tile_by_row = tiles.reshape(N_ROW, per_row // group, group, TILE, TILE)
    rows_by_row = tile_rows.reshape(N_ROW, per_row // group, group)
    cols_by_row = tile_cols.reshape(N_ROW, per_row // group, group)
    wrapped = jnp.concatenate([features[nodes - rows_dev:], features, features[:rows_dev]], axis=0)

    def forward_one(index):
        window = lax.dynamic_slice_in_dim(wrapped, index * rows_dev, 3 * rows_dev, 0)
        window = window.reshape(3 * blocks, TILE, width)

        def step(total, items):
            tile_grp, row_grp, col_grp, live_grp = items
            picked = window[col_grp].astype(f32)
            prod = jnp.einsum('gij,gjf->gif', tile_grp.astype(f32), picked) * live_grp[:, None, None]
            return (total.at[row_grp].add(prod), None)
        initial = jnp.zeros((blocks, TILE, width), f32)
        total, _ = lax.scan(step, initial, (tile_by_row[index], rows_by_row[index], cols_by_row[index], live[index]))
        return total.reshape(rows_dev, width)
    agg_sum = lax.map(forward_one, jnp.arange(N_ROW, dtype=jnp.int32)).reshape(nodes, width)
    aggregated = agg_sum.astype(jnp.bfloat16)
    pre = jnp.dot(features, w_self, preferred_element_type=f32) + jnp.dot(aggregated, w_neigh, preferred_element_type=f32) + bias[None, :]
    sigm = jax.nn.sigmoid(pre)
    output = (pre * sigm).astype(jnp.bfloat16)
    grad_pre = cotangent.astype(f32) * sigm * (1.0 + pre * (1.0 - sigm))
    grad_low = grad_pre.astype(jnp.bfloat16)
    scale = 1.0 / math.sqrt(nodes)
    w_self_grad = jnp.dot(features.T, grad_low, preferred_element_type=f32) * scale
    w_neigh_grad = jnp.dot(aggregated.T, grad_low, preferred_element_type=f32) * scale
    bias_grad = lax.optimization_barrier(jnp.sum(grad_pre, axis=0)) * scale
    self_back = jnp.dot(grad_low, w_self.T, preferred_element_type=f32)
    agg_back = jnp.dot(grad_low, w_neigh.T, preferred_element_type=f32).astype(jnp.bfloat16)

    def backward_one(padded, index):
        own = lax.dynamic_slice_in_dim(agg_back, index * rows_dev, rows_dev, 0).reshape(blocks, TILE, width)

        def step(total, items):
            tile_grp, row_grp, col_grp, live_grp = items
            picked = own[row_grp].astype(f32)
            prod = jnp.einsum('gji,gjf->gif', tile_grp.astype(f32), picked) * live_grp[:, None, None]
            return (total.at[col_grp].add(prod), None)
        initial = jnp.zeros((3 * blocks, TILE, width), f32)
        part, _ = lax.scan(step, initial, (tile_by_row[index], rows_by_row[index], cols_by_row[index], live[index]))
        current = lax.dynamic_slice_in_dim(padded, index * rows_dev, 3 * rows_dev, 0)
        padded = lax.dynamic_update_slice_in_dim(padded, current + part.reshape(3 * rows_dev, width), index * rows_dev, 0)
        return (padded, None)
    padded, _ = lax.scan(backward_one, jnp.zeros((nodes + 2 * rows_dev, width), f32), jnp.arange(N_ROW, dtype=jnp.int32))
    neigh_back = padded[rows_dev:rows_dev + nodes]
    neigh_back = neigh_back.at[:rows_dev].add(padded[nodes + rows_dev:])
    neigh_back = neigh_back.at[nodes - rows_dev:].add(padded[:rows_dev])
    features_grad = self_back + neigh_back
    return (output, features_grad, w_self_grad, w_neigh_grad, bias_grad)
```

```python
import functools
import math

import jax
import jax.numpy as jnp
from jax import lax
from jax.experimental import pallas as pl
from jax.experimental.pallas import tpu as pltpu
from jax.sharding import PartitionSpec as P

F32 = jnp.float32
BF16 = jnp.bfloat16
UNROLL = 16
CHUNK = 176
MIB = 1024 * 1024


def passed_along(array, axis, by):
    size = lax.axis_size(axis)
    return lax.ppermute(array, axis, [(i, (i + by) % size) for i in range(size)])


def tile_loop(count, rows, cols, tiles, ring, sems, total, product, target):
    chunks = lax.div(count + CHUNK - 1, CHUNK)

    def fetch(c):
        return pltpu.make_async_copy(tiles.at[pl.ds(c * CHUNK, CHUNK)], ring.at[lax.rem(c, 2)], sems.at[lax.rem(c, 2)])

    spare = total.shape[0] - 1

    def chunk_step(c, carry):
        fetch(c).wait()

        @pl.when(c + 1 < chunks)
        def _():
            fetch(c + 1).start()

        base = c * CHUNK
        limit = jnp.minimum(count - base, CHUNK)

        def group_step(g, inner):
            start = g * UNROLL
            products = [
                product(base + start + u, ring[lax.rem(c, 2), start + u]) for u in range(UNROLL)
            ]
            for u in range(UNROLL):
                slot = base + start + u
                total[jnp.where(slot < count, target(slot), spare)] += products[u]
            return inner

        return lax.fori_loop(0, lax.div(limit + UNROLL - 1, UNROLL), group_step, carry)

    return fetch, chunks, chunk_step


def forward_kernel(rows, cols, count_ref, before, own, after, tiles, out, window, ring, total, sems, halo_sems):
    blocks = own.shape[0]
    count = count_ref[0]
    fetch, chunks, chunk_step = tile_loop(
        count, rows, cols, tiles, ring, sems, total,
        lambda slot, tile: jnp.dot(tile, window[cols[slot]], preferred_element_type=F32),
        lambda slot: rows[slot],
    )
    copies = [
        pltpu.make_async_copy(part, window.at[pl.ds(k * blocks, blocks)], halo_sems.at[k])
        for k, part in enumerate((before, own, after))
    ]
    fetch(0).start()
    for copy in copies:
        copy.start()
    total[...] = jnp.zeros_like(total)
    for copy in copies:
        copy.wait()
    lax.fori_loop(0, chunks, chunk_step, 0)
    out[...] = total[:blocks].astype(BF16)


def backward_kernel(rows, cols, count_ref, grads, tiles, out, ring, total, sems):
    count = count_ref[0]
    fetch, chunks, chunk_step = tile_loop(
        count, rows, cols, tiles, ring, sems, total,
        lambda slot, tile: jnp.dot(grads[rows[slot]], tile, preferred_element_type=F32),
        lambda slot: cols[slot],
    )
    fetch(0).start()
    total[...] = jnp.zeros_like(total)
    lax.fori_loop(0, chunks, chunk_step, 0)
    out[...] = total[: out.shape[0]].astype(BF16)


SMEM = pl.BlockSpec(memory_space=pltpu.SMEM)
VMEM = pl.BlockSpec(memory_space=pltpu.VMEM)
ANY = pl.BlockSpec(memory_space=pl.ANY)


def forward_sum(tile_rows, tile_cols, tile_count, before, own, after, tiles):
    blocks, size, half = own.shape
    return pl.pallas_call(
        forward_kernel,
        out_shape=jax.ShapeDtypeStruct((blocks, size, half), BF16),
        in_specs=[SMEM] * 3 + [ANY] * 4,
        out_specs=VMEM,
        scratch_shapes=[
            pltpu.VMEM((3 * blocks, size, half), BF16),
            pltpu.VMEM((2, CHUNK, size, size), BF16),
            pltpu.VMEM((blocks + 1, size, half), F32),
            pltpu.SemaphoreType.DMA((2,)),
            pltpu.SemaphoreType.DMA((3,)),
        ],
        compiler_params=pltpu.CompilerParams(vmem_limit_bytes=48 * MIB),
        cost_estimate=pl.CostEstimate(flops=2 * 704 * 128**3, bytes_accessed=704 * 32768, transcendentals=0),
        name="forward_sum",
    )(tile_rows, tile_cols, tile_count, before, own, after, tiles)


def backward_sum(tile_rows, tile_cols, tile_count, grads, tiles):
    blocks, half, size = grads.shape
    return pl.pallas_call(
        backward_kernel,
        out_shape=jax.ShapeDtypeStruct((3 * blocks, half, size), BF16),
        in_specs=[SMEM] * 3 + [VMEM, ANY],
        out_specs=VMEM,
        scratch_shapes=[
            pltpu.VMEM((2, CHUNK, size, size), BF16),
            pltpu.VMEM((3 * blocks + 1, half, size), F32),
            pltpu.SemaphoreType.DMA((2,)),
        ],
        compiler_params=pltpu.CompilerParams(vmem_limit_bytes=48 * MIB),
        cost_estimate=pl.CostEstimate(flops=2 * 704 * 128**3, bytes_accessed=704 * 32768, transcendentals=0),
        name="backward_sum",
    )(tile_rows, tile_cols, tile_count, grads, tiles)


def local(features, tiles, tile_rows, tile_cols, tile_count, w_self, w_neigh, bias, cotangent):
    rows_dev, half = features.shape
    size = tiles.shape[1]
    blocks = rows_dev // size
    share = rows_dev // lax.axis_size("edge")
    nodes = rows_dev * lax.axis_size("row")

    own_blocks = features.reshape(blocks, size, half)
    before = passed_along(own_blocks, "row", 1)
    after = passed_along(own_blocks, "row", -1)
    own = lax.dynamic_slice_in_dim(features, lax.axis_index("edge") * share, share, 0)
    own_full = lax.all_gather(own, "col", axis=1, tiled=True)
    partial = forward_sum(tile_rows, tile_cols, tile_count, before, own_blocks, after, tiles)
    agg = lax.psum_scatter(partial.reshape(rows_dev, half), "edge", scatter_dimension=0, tiled=True)
    agg_full = lax.all_gather(agg, "col", axis=1, tiled=True)
    pre = (
        jnp.dot(own_full, w_self, preferred_element_type=F32)
        + jnp.dot(agg_full, w_neigh, preferred_element_type=F32)
        + bias[None, :]
    )
    sigm = jax.nn.sigmoid(pre)
    output = (pre * sigm).astype(BF16)
    grad_pre = cotangent.astype(F32) * sigm * (1.0 + pre * (1.0 - sigm))
    grad_low = grad_pre.astype(BF16)
    over_rows = (((0,), (0,)), ((), ()))
    self_weight = lax.dot_general(own_full, grad_low, over_rows, preferred_element_type=F32)
    neigh_weight = lax.dot_general(agg_full, grad_low, over_rows, preferred_element_type=F32)
    bias_part = jnp.sum(grad_pre, axis=0)
    self_weight, neigh_weight, bias_total = lax.psum(
        (self_weight, neigh_weight, bias_part), ("row", "edge")
    )
    scale = 1.0 / math.sqrt(nodes)
    over_cols = (((1,), (1,)), ((), ()))
    self_back = lax.dot_general(grad_low, w_self, over_cols, preferred_element_type=F32)
    agg_back = lax.dot_general(grad_low, w_neigh, over_cols, preferred_element_type=F32)
    self_back, agg_back = (
        lax.psum_scatter(self_back, "col", scatter_dimension=1, tiled=True),
        lax.psum_scatter(agg_back, "col", scatter_dimension=1, tiled=True),
    )
    flipped = agg_back.astype(BF16).reshape(share // size, size, half).swapaxes(1, 2)
    grads = lax.all_gather(flipped, "edge", axis=0, tiled=True)
    parts = backward_sum(tile_rows, tile_cols, tile_count, grads, tiles).reshape(3, blocks, half, size)
    from_after = passed_along(parts[0], "row", -1)
    from_before = passed_along(parts[2], "row", 1)
    joined = (parts[1].astype(F32) + from_after.astype(F32) + from_before.astype(F32)).astype(BF16)
    neigh_back = lax.psum_scatter(joined, "edge", scatter_dimension=0, tiled=True)
    neigh_back = neigh_back.astype(F32).swapaxes(1, 2).reshape(share, half)
    features_grad = self_back + neigh_back
    return (output, features_grad, self_weight * scale, neigh_weight * scale, bias_total * scale)


def solution(mesh):
    return jax.shard_map(
        local,
        mesh=mesh,
        in_specs=(
            P("row", "col"),
            P(("row", "edge"), None, None),
            P(("row", "edge")),
            P(("row", "edge")),
            P(("row", "edge")),
            P(None, "col"),
            P(None, "col"),
            P("col"),
            P(("row", "edge"), "col"),
        ),
        out_specs=(
            P(("row", "edge"), "col"),
            P(("row", "edge"), "col"),
            P(None, "col"),
            P(None, "col"),
            P("col"),
        ),
        check_vma=False,
    )
```

```python
import functools
import math

import jax
import jax.numpy as jnp
from jax import lax
from jax.experimental import pallas as pl
from jax.experimental.pallas import tpu as pltpu
from jax.sharding import PartitionSpec as P

F32 = jnp.float32
BF16 = jnp.bfloat16
UNROLL = 16
CHUNK = 176
MIB = 1024 * 1024


MESH = pl.DeviceIdType.MESH


def place():
    row, col, edge = (lax.axis_index(name) for name in ("row", "col", "edge"))
    return row, col, edge, lax.rem(edge, 2), lax.div(edge, 2)


def greet(peers):
    barrier = pltpu.get_barrier_semaphore()
    for peer in peers:
        pl.semaphore_signal(barrier, inc=1, device_id=peer, device_id_type=MESH)
    pl.semaphore_wait(barrier, len(peers))


class Sender:
    def __init__(self, send_sems, recv_sems):
        self.send_sems, self.recv_sems, self.used = send_sems, recv_sems, []

    def __call__(self, src, dst, peer):
        index = len(self.used)
        copy = pltpu.make_async_remote_copy(
            src_ref=src,
            dst_ref=dst,
            send_sem=self.send_sems.at[index],
            recv_sem=self.recv_sems.at[index],
            device_id=peer,
            device_id_type=MESH,
        )
        copy.start()
        self.used.append(copy)
        return copy

    def finish(self):
        for copy in self.used:
            copy.wait_send()


def tile_loop(count, rows, cols, tiles, ring, sems, total, product, target):
    chunks = lax.div(count + CHUNK - 1, CHUNK)

    def fetch(c):
        return pltpu.make_async_copy(tiles.at[pl.ds(c * CHUNK, CHUNK)], ring.at[lax.rem(c, 2)], sems.at[lax.rem(c, 2)])

    spare = total.shape[0] - 1

    def chunk_step(c, carry):
        fetch(c).wait()

        @pl.when(c + 1 < chunks)
        def _():
            fetch(c + 1).start()

        base = c * CHUNK
        limit = jnp.minimum(count - base, CHUNK)

        def group_step(g, inner):
            start = g * UNROLL
            products = [
                product(base + start + u, ring[lax.rem(c, 2), start + u]) for u in range(UNROLL)
            ]
            for u in range(UNROLL):
                slot = base + start + u
                total[jnp.where(slot < count, target(slot), spare)] += products[u]
            return inner

        return lax.fori_loop(0, lax.div(limit + UNROLL - 1, UNROLL), group_step, carry)

    return fetch, chunks, chunk_step


def forward_kernel(rows, cols, count_ref, before, own, after, tiles, out, window, ring, total, sems, halo_sems):
    blocks = own.shape[0]
    count = count_ref[0]
    fetch, chunks, chunk_step = tile_loop(
        count, rows, cols, tiles, ring, sems, total,
        lambda slot, tile: jnp.dot(tile, window[cols[slot]], preferred_element_type=F32),
        lambda slot: rows[slot],
    )
    copies = [
        pltpu.make_async_copy(part, window.at[pl.ds(k * blocks, blocks)], halo_sems.at[k])
        for k, part in enumerate((before, own, after))
    ]
    fetch(0).start()
    for copy in copies:
        copy.start()
    total[...] = jnp.zeros_like(total)
    for copy in copies:
        copy.wait()
    lax.fori_loop(0, chunks, chunk_step, 0)
    out[...] = total[:blocks].astype(BF16)


def backward_kernel(rows, cols, count_ref, grads, tiles, out, ring, total, sems):
    count = count_ref[0]
    fetch, chunks, chunk_step = tile_loop(
        count, rows, cols, tiles, ring, sems, total,
        lambda slot, tile: jnp.dot(grads[rows[slot]], tile, preferred_element_type=F32),
        lambda slot: cols[slot],
    )
    fetch(0).start()
    total[...] = jnp.zeros_like(total)
    lax.fori_loop(0, chunks, chunk_step, 0)
    out[...] = total[: out.shape[0]].astype(BF16)


SMEM = pl.BlockSpec(memory_space=pltpu.SMEM)
VMEM = pl.BlockSpec(memory_space=pltpu.VMEM)
ANY = pl.BlockSpec(memory_space=pl.ANY)


def forward_sum(tile_rows, tile_cols, tile_count, before, own, after, tiles):
    blocks, size, half = own.shape
    return pl.pallas_call(
        forward_kernel,
        out_shape=jax.ShapeDtypeStruct((blocks, size, half), BF16),
        in_specs=[SMEM] * 3 + [ANY] * 4,
        out_specs=VMEM,
        scratch_shapes=[
            pltpu.VMEM((3 * blocks, size, half), BF16),
            pltpu.VMEM((2, CHUNK, size, size), BF16),
            pltpu.VMEM((blocks + 1, size, half), F32),
            pltpu.SemaphoreType.DMA((2,)),
            pltpu.SemaphoreType.DMA((3,)),
        ],
        compiler_params=pltpu.CompilerParams(vmem_limit_bytes=48 * MIB),
        cost_estimate=pl.CostEstimate(flops=2 * 704 * 128**3, bytes_accessed=704 * 32768, transcendentals=0),
        name="forward_sum",
    )(tile_rows, tile_cols, tile_count, before, own, after, tiles)


def backward_sum(tile_rows, tile_cols, tile_count, grads, tiles):
    blocks, half, size = grads.shape
    return pl.pallas_call(
        backward_kernel,
        out_shape=jax.ShapeDtypeStruct((3 * blocks, half, size), BF16),
        in_specs=[SMEM] * 3 + [VMEM, ANY],
        out_specs=VMEM,
        scratch_shapes=[
            pltpu.VMEM((2, CHUNK, size, size), BF16),
            pltpu.VMEM((3 * blocks + 1, half, size), F32),
            pltpu.SemaphoreType.DMA((2,)),
        ],
        compiler_params=pltpu.CompilerParams(vmem_limit_bytes=48 * MIB),
        cost_estimate=pl.CostEstimate(flops=2 * 704 * 128**3, bytes_accessed=704 * 32768, transcendentals=0),
        name="backward_sum",
    )(tile_rows, tile_cols, tile_count, grads, tiles)


HALO_CHUNKS = 4


def halo_kernel(
    features, cotangent, w_self, w_neigh, bias,
    before, after, own_far, cot_far, w_self_far, w_neigh_far, bias_far,
    send_sems, recv_sems,
):
    row, col, edge, core, _ = place()
    rows = lax.axis_size("row")
    up, down = {"row": lax.rem(row + 1, rows)}, {"row": lax.rem(row + rows - 1, rows)}
    twin, partner = {"edge": edge + 1 - 2 * core}, {"col": 1 - col}
    blocks = features.shape[0]
    share = blocks // 8
    greet([up, down, twin, partner])
    send = Sender(send_sems, recv_sems)
    step = blocks // 2 // HALO_CHUNKS
    parts = [pl.ds(core * (blocks // 2) + i * step, step) for i in range(HALO_CHUNKS)]
    arriving = []
    for part in parts:
        arriving.append(
            (part, before, send(features.at[part], before.at[part], up))
        )
        arriving.append(
            (part, after, send(features.at[part], after.at[part], down))
        )
    theirs = pl.ds(edge * 2 * share + (1 - col) * share, share)
    theirs_cot = pl.ds((1 - col) * share, share)
    swaps = [
        send(features.at[theirs], own_far, partner),
        send(cotangent.at[theirs_cot], cot_far, partner),
        send(w_self, w_self_far, partner),
        send(w_neigh, w_neigh_far, partner),
        send(bias, bias_far, partner),
    ]
    handed = []
    for part, side, copy in arriving:
        copy.wait_recv()
        handed.append(send(side.at[part], side.at[part], twin))
    for copy in swaps + handed:
        copy.wait_recv()
    send.finish()


def exchange_inputs(features, cotangent, w_self, w_neigh, bias):
    blocks, size, half = features.shape
    share = blocks // 8
    shapes = [features, features] + [
        jax.ShapeDtypeStruct((share, size, half), BF16),
        jax.ShapeDtypeStruct((share, size, half), BF16),
        w_self, w_neigh, bias,
    ]
    copies = 4 * HALO_CHUNKS + 5
    return pl.pallas_call(
        halo_kernel,
        out_shape=[jax.ShapeDtypeStruct(s.shape, s.dtype) for s in shapes],
        in_specs=[ANY] * 5,
        out_specs=[ANY] * 7,
        scratch_shapes=[pltpu.SemaphoreType.DMA((copies,)), pltpu.SemaphoreType.DMA((copies,))],
        compiler_params=pltpu.CompilerParams(collective_id=1, has_side_effects=True),
        name="exchange_inputs",
    )(features, cotangent, w_self, w_neigh, bias)


def mid_kernel(
    partial, features, own_far, cotangent, cot_far, w_self, w_neigh, w_self_far, w_neigh_far, bias, bias_far,
    grads, out_near, self_near, weight_near, bias_near, far,
    got_core, sent_pair, kept, got_pair, sent_col, got_col, own, cot, weights, sent_grads,
    local_sems, send_sems, recv_sems,
):
    row, col, edge, core, pair_side = place()
    other = 1 - col
    twin, pair, partner = {"edge": edge + 1 - 2 * core}, {"edge": lax.rem(edge + 2, 4)}, {"col": other}
    diagonal = {"edge": lax.rem(edge + 2, 4), "col": other}
    blocks, size, half = partial.shape
    share = blocks // 8
    near_rows = own_far.shape[0] * size
    local = [
        pltpu.make_async_copy(features.at[pl.ds(edge * 2 * share + col * share, share)], own, local_sems.at[0]),
        pltpu.make_async_copy(cotangent.at[pl.ds(col * share, share)], cot, local_sems.at[1]),
    ]
    for copy in local:
        copy.start()
    greet([twin, pair, partner, diagonal])
    send = Sender(send_sems, recv_sems)

    def piece(side, on_core, column):
        return pl.ds((2 * side + on_core) * 2 * share + column * share, share)

    order = [(1 - pair_side, other), (1 - pair_side, col), (pair_side, other), (pair_side, col)]
    to_twin = [
        send(partial.at[piece(side, 1 - core, column)], got_core.at[i], twin)
        for i, (side, column) in enumerate(order)
    ]
    near_w, far_w = pl.ds(pl.multiple_of(col * half, half), half), pl.ds(pl.multiple_of(other * half, half), half)
    for k, (near, away) in enumerate(((w_self, w_self_far), (w_neigh, w_neigh_far))):
        for j, rows in enumerate((near_w, far_w)):
            at = pl.ds((2 * k + j) * half, half)
            weights[at, :half] = near[rows, :]
            weights[at, half:] = away[rows, :]

    def summed(i):
        to_twin[i].wait_recv()
        side, column = order[i]
        return partial[piece(side, core, column)].astype(F32) + got_core[i].astype(F32)

    to_pair = []
    for i in range(2):
        sent_pair[i] = summed(i).astype(BF16)
        to_pair.append(send(sent_pair.at[i], got_pair.at[i], pair))
    for i in range(2):
        kept[i] = summed(2 + i)
    to_pair[0].wait_recv()
    sent_col[...] = (kept[0] + got_pair[0].astype(F32)).astype(BF16)
    to_partner = send(sent_col, got_col, partner)
    for copy in local:
        copy.wait()
    to_pair[1].wait_recv()
    agg_near = (kept[1] + got_pair[1].astype(F32)).astype(BF16)
    to_partner.wait_recv()

    def flat(blocks_of):
        return blocks_of.reshape(near_rows, half)

    mixed = jnp.concatenate(
        [flat(own[...]), flat(own_far[...]), flat(agg_near), flat(got_col[...])], axis=1
    )
    pre = jnp.dot(mixed, weights[...], preferred_element_type=F32) + jnp.concatenate(
        [bias[...], bias_far[...]], axis=1
    )
    sigm = jax.nn.sigmoid(pre)
    cot_full = jnp.concatenate([flat(cot[...]), flat(cot_far[...])], axis=1).astype(F32)
    grad_pre = cot_full * sigm * (1.0 + pre * (1.0 - sigm))
    grad_low = grad_pre.astype(BF16)
    over_cols = (((1,), (1,)), ((), ()))
    agg_back = lax.dot_general(
        weights[2 * half :, :], grad_low, over_cols, preferred_element_type=F32
    ).astype(BF16)
    mine = pl.ds(edge * 2 * share + col * share, share)
    for b in range(share):
        grads[edge * 2 * share + col * share + b] = agg_back[:half, b * size : (b + 1) * size]
        sent_grads[b] = agg_back[half:, b * size : (b + 1) * size]
    crossing = [
        send(sent_grads, grads.at[mine], diagonal),
        send(sent_grads, grads.at[mine], partner),
        send(grads.at[mine], grads.at[mine], pair),
    ]
    handed = [send(grads.at[mine], grads.at[mine], twin)]

    output = (pre * sigm).astype(BF16)
    out_near[...] = output[:, :half]
    far[:near_rows] = output[:, half:]
    self_back = lax.dot_general(grad_low, weights[: 2 * half, :], over_cols, preferred_element_type=F32)
    self_near[...] = self_back[:, :half]
    far[near_rows : 2 * near_rows] = self_back[:, half:].astype(BF16)
    parts = lax.dot_general(mixed, grad_low, (((0,), (0,)), ((), ())), preferred_element_type=F32)
    for k in range(2):
        for j, start in enumerate((col * half, other * half)):
            at = (2 * k + j) * half
            weight_near[pl.ds(pl.multiple_of(2 * k * half + start, half), half), :] = parts[at : at + half, :half]
            far[pl.ds(pl.multiple_of(2 * near_rows + 2 * k * half + start, half), half), :] = (
                parts[at : at + half, half:].astype(BF16)
            )
    bias_parts = jnp.sum(grad_pre.reshape(near_rows // 16, 16, 2 * half), axis=0)
    bias_near[...] = bias_parts[:, :half]
    far[2 * near_rows + 4 * half :] = bias_parts[:, half:].astype(BF16)

    far_edge = lax.rem(edge + 2, 4)
    homes = [
        pl.ds(far_edge * 2 * share + other * share, share),
        pl.ds(edge * 2 * share + other * share, share),
        pl.ds(far_edge * 2 * share + col * share, share),
    ]
    for k in (1, 2, 0):
        crossing[k].wait_recv()
        handed.append(send(grads.at[homes[k]], grads.at[homes[k]], twin))
    for copy in handed:
        copy.wait_recv()
    send.finish()


def middle(partial, features, own_far, cotangent, cot_far, w_self, w_neigh, w_self_far, w_neigh_far, bias, bias_far):
    blocks, size, half = partial.shape
    share = blocks // 8
    rows = share * size
    copies = 4 + 2 + 1 + 3 + 4
    piece = (share, size, half)
    return pl.pallas_call(
        mid_kernel,
        out_shape=[
            jax.ShapeDtypeStruct((blocks, half, size), BF16),
            jax.ShapeDtypeStruct((rows, half), BF16),
            jax.ShapeDtypeStruct((rows, half), F32),
            jax.ShapeDtypeStruct((4 * half, half), F32),
            jax.ShapeDtypeStruct((16, half), F32),
            jax.ShapeDtypeStruct((2 * rows + 4 * half + 16, half), BF16),
        ],
        in_specs=[VMEM, ANY, VMEM, ANY] + [VMEM] * 7,
        out_specs=[VMEM] * 6,
        scratch_shapes=[
            pltpu.VMEM((4,) + piece, BF16),
            pltpu.VMEM((2,) + piece, BF16),
            pltpu.VMEM((2,) + piece, F32),
            pltpu.VMEM((2,) + piece, BF16),
            pltpu.VMEM(piece, BF16),
            pltpu.VMEM(piece, BF16),
            pltpu.VMEM(piece, BF16),
            pltpu.VMEM(piece, BF16),
            pltpu.VMEM((4 * half, 2 * half), BF16),
            pltpu.VMEM((share, half, size), BF16),
            pltpu.SemaphoreType.DMA((2,)),
            pltpu.SemaphoreType.DMA((copies,)),
            pltpu.SemaphoreType.DMA((copies,)),
        ],
        compiler_params=pltpu.CompilerParams(collective_id=2, has_side_effects=True, vmem_limit_bytes=40 * MIB),
        name="middle",
    )(partial, features, own_far, cotangent, cot_far, w_self, w_neigh, w_self_far, w_neigh_far, bias, bias_far)


def final_kernel(
    scale, back, out_near, self_near, weight_near, bias_near, far,
    output, features_grad, w_self_grad, w_neigh_grad, bias_grad,
    got_core, sent_row, kept, got_row, sent_pair, got_pair,
    w_all, w_sent0, w_got0, w_sent1, w_got1, w_sent2, w_got2, w_sent3, w_got3, w_total, bias_sum,
    send_sems, recv_sems,
):
    row, col, edge, core, side = place()
    rows = lax.axis_size("row")
    x, z = lax.rem(row, 4), lax.div(row, 4)
    twin, pair = {"edge": edge + 1 - 2 * core}, {"edge": lax.rem(edge + 2, 4)}
    up, down = {"row": lax.rem(row + 1, rows)}, {"row": lax.rem(row + rows - 1, rows)}
    along_x = [lax.rem(x + j, 4) for j in (1, 2, 3)]
    along_z = [lax.rem(z + j, 4) for j in (1, 2, 3)]
    x_peers = [{"row": z * 4 + to} for to in along_x]
    z_peers = [{"row": to * 4 + x} for to in along_z]
    greet([twin, pair, up, down] + x_peers + z_peers)
    send = Sender(send_sems, recv_sems)
    share = back.shape[0] // 3 // 4
    near_rows, half = out_near.shape
    blocks = back.shape[0] // 3

    def piece(part, at_side, on_core):
        return pl.ds(part * blocks + (2 * at_side + on_core) * share, share)

    order = [(0, 1 - side), (2, 1 - side), (0, side), (2, side), (1, 1 - side), (1, side)]
    to_twin = [
        send(back.at[piece(part, at, 1 - core)], got_core.at[i], twin) for i, (part, at) in enumerate(order)
    ]

    top = 4 * half
    w_all[...] = weight_near[...] + far[2 * near_rows : 2 * near_rows + top].astype(F32)
    bias_sum[...] = bias_near[...] + far[2 * near_rows + top :].astype(F32)
    w_sent0[: top // 2] = w_all[pl.ds(pl.multiple_of((1 - core) * (top // 2), 8), top // 2), :]
    w_sent0[top // 2 :] = bias_sum[...]
    w_step = send(w_sent0, w_got0, twin)

    def summed(i):
        to_twin[i].wait_recv()
        part, at = order[i]
        return back[piece(part, at, core)].astype(F32) + got_core[i].astype(F32)

    to_row = []
    for i in range(4):
        sent_row[i] = summed(i).astype(BF16)
        to_row.append(send(sent_row.at[i], got_row.at[i], down if i % 2 == 0 else up))

    w_step.wait_recv()
    start = pl.multiple_of(core * (top // 2), 8)
    w_all[pl.ds(start, top // 2), :] += w_got0[: top // 2]
    bias_sum[...] += w_got0[top // 2 :]
    w_sent1[: top // 4] = w_all[pl.ds(pl.multiple_of(start + (1 - side) * (top // 4), 8), top // 4), :]
    w_sent1[top // 4 :] = bias_sum[...]
    w_step = send(w_sent1, w_got1, pair)
    for i in range(2):
        kept[i] = summed(4 + i)

    w_step.wait_recv()
    start = pl.multiple_of(start + side * (top // 4), 8)
    w_all[pl.ds(start, top // 4), :] += w_got1[: top // 4]
    bias_sum[...] += w_got1[top // 4 :]

    def spread(start, many, sent, got, targets, peers):
        steps = []
        for j in range(3):
            sent[j, :many] = w_all[pl.ds(pl.multiple_of(start + targets[j] * many, 8), many), :]
            sent[j, many:] = bias_sum[...]
            steps.append(send(sent.at[j], got.at[j], peers[j]))
        return steps

    def collect(start, many, got, steps):
        for j in range(3):
            steps[j].wait_recv()
        at = pl.ds(start, many)
        w_all[at, :] += got[0, :many] + got[1, :many] + got[2, :many]
        bias_sum[...] += got[0, many:] + got[1, many:] + got[2, many:]

    many = top // 16
    steps = spread(start, many, w_sent2, w_got2, along_x, x_peers)
    start = pl.multiple_of(start + x * many, 8)
    collect(start, many, w_got2, steps)
    many = top // 64
    steps = spread(start, many, w_sent3, w_got3, along_z, z_peers)
    start = pl.multiple_of(start + z * many, 8)
    collect(start, many, w_got3, steps)
    w_total[pl.ds(start, many), :] = w_all[pl.ds(start, many), :]
    bias_grad[...] = jnp.sum(bias_sum[...], axis=0, keepdims=True) * scale
    at = pl.ds(start, many)
    steps = [send(w_total.at[at], w_total.at[at], peer) for peer in z_peers]

    for i in range(2):
        to_row[i].wait_recv()
    sent_pair[...] = (kept[0] + got_row[0].astype(F32) + got_row[1].astype(F32)).astype(BF16)
    to_pair = send(sent_pair, got_pair, pair)

    for step in steps:
        step.wait_recv()
    start = pl.multiple_of(start - z * many, 8)
    many = top // 16
    at = pl.ds(start, many)
    steps = [send(w_total.at[at], w_total.at[at], peer) for peer in x_peers]
    for step in steps:
        step.wait_recv()
    start = pl.multiple_of(start - x * many, 8)
    at = pl.ds(start, top // 4)
    step = send(w_total.at[at], w_total.at[at], pair)

    near, away = pl.multiple_of(col * near_rows, 8), pl.multiple_of((1 - col) * near_rows, 8)
    output[pl.ds(pl.multiple_of(near, 16), near_rows), :] = out_near[...]
    output[pl.ds(pl.multiple_of(away, 16), near_rows), :] = far[:near_rows]
    features_grad[pl.ds(near, near_rows), :] = self_near[...]
    features_grad[pl.ds(away, near_rows), :] = far[near_rows : 2 * near_rows].astype(F32)

    step.wait_recv()
    start = pl.multiple_of(start - side * (top // 4), 8)
    at = pl.ds(start, top // 2)
    step = send(w_total.at[at], w_total.at[at], twin)

    for i in range(2, 4):
        to_row[i].wait_recv()
    kept[1] += got_row[2].astype(F32) + got_row[3].astype(F32)
    to_pair.wait_recv()
    size = back.shape[2]
    for b in range(share):
        features_grad[b * size : (b + 1) * size, :] += (kept[1, b] + got_pair[b].astype(F32)).T
    step.wait_recv()
    w_self_grad[...] = w_total[: top // 2] * scale
    w_neigh_grad[...] = w_total[top // 2 :] * scale
    send.finish()


def finish(scale, back, out_near, self_near, weight_near, bias_near, far):
    share, half, size = back.shape[0] // 12, back.shape[1], back.shape[2]
    rows = out_near.shape[0]
    top = weight_near.shape[0]
    copies = 6 + 4 + 1 + 2 + 12 + 2
    piece = (share, half, size)

    def sent(lead, many):
        return [pltpu.VMEM(lead + (many + 16, half), F32)] * 2

    return pl.pallas_call(
        functools.partial(final_kernel, scale),
        out_shape=[
            jax.ShapeDtypeStruct((2 * rows, half), BF16),
            jax.ShapeDtypeStruct((2 * rows, half), F32),
            jax.ShapeDtypeStruct((top // 2, half), F32),
            jax.ShapeDtypeStruct((top // 2, half), F32),
            jax.ShapeDtypeStruct((1, half), F32),
        ],
        in_specs=[VMEM] * 6,
        out_specs=[VMEM] * 5,
        scratch_shapes=[
            pltpu.VMEM((6,) + piece, BF16),
            pltpu.VMEM((4,) + piece, BF16),
            pltpu.VMEM((2,) + piece, F32),
            pltpu.VMEM((4,) + piece, BF16),
            pltpu.VMEM(piece, BF16),
            pltpu.VMEM(piece, BF16),
            pltpu.VMEM((top, half), F32),
            *sent((), top // 2),
            *sent((), top // 4),
            *sent((3,), top // 16),
            *sent((3,), top // 64),
            pltpu.VMEM((top, half), F32),
            pltpu.VMEM((16, half), F32),
            pltpu.SemaphoreType.DMA((copies,)),
            pltpu.SemaphoreType.DMA((copies,)),
        ],
        compiler_params=pltpu.CompilerParams(collective_id=3, has_side_effects=True, vmem_limit_bytes=40 * MIB),
        name="finish",
    )(back, out_near, self_near, weight_near, bias_near, far)


def local(features, tiles, tile_rows, tile_cols, tile_count, w_self, w_neigh, bias, cotangent):
    rows_dev, half = features.shape
    size = tiles.shape[1]
    blocks = rows_dev // size
    nodes = rows_dev * lax.axis_size("row")
    scale = 1.0 / math.sqrt(nodes)

    own = features.reshape(blocks, size, half)
    cot = cotangent.reshape(-1, size, half)
    bias_row = bias.reshape(1, half)
    before, after, own_far, cot_far, w_self_far, w_neigh_far, bias_far = exchange_inputs(
        own, cot, w_self, w_neigh, bias_row
    )
    partial = forward_sum(tile_rows, tile_cols, tile_count, before, own, after, tiles)
    grads, out_near, self_near, weight_near, bias_near, far = middle(
        partial, own, own_far, cot, cot_far, w_self, w_neigh, w_self_far, w_neigh_far, bias_row, bias_far
    )
    far = lax.ppermute(far, "col", [(0, 1), (1, 0)])
    back = backward_sum(tile_rows, tile_cols, tile_count, grads, tiles)
    output, features_grad, w_self_grad, w_neigh_grad, bias_grad = finish(
        scale, back, out_near, self_near, weight_near, bias_near, far
    )
    return (output, features_grad, w_self_grad, w_neigh_grad, bias_grad.reshape(half))


def solution(mesh):
    return jax.shard_map(
        local,
        mesh=mesh,
        in_specs=(
            P("row", "col"),
            P(("row", "edge"), None, None),
            P(("row", "edge")),
            P(("row", "edge")),
            P(("row", "edge")),
            P(None, "col"),
            P(None, "col"),
            P("col"),
            P(("row", "edge"), "col"),
        ),
        out_specs=(
            P(("row", "edge"), "col"),
            P(("row", "edge"), "col"),
            P(None, "col"),
            P(None, "col"),
            P("col"),
        ),
        check_vma=False,
    )
```

```python
import functools
import math

import jax
import jax.numpy as jnp
from jax import lax
from jax.experimental import pallas as pl
from jax.experimental.pallas import tpu as pltpu
from jax.sharding import PartitionSpec as P

F32 = jnp.float32
BF16 = jnp.bfloat16
UNROLL = 88
LAG = 4
LOADS = 16
MIB = 1024 * 1024


MESH = pl.DeviceIdType.MESH


def place():
    row, col, edge = (lax.axis_index(name) for name in ("row", "col", "edge"))
    return row, col, edge, lax.rem(edge, 2), lax.div(edge, 2)


def greet(peers):
    barrier = pltpu.get_barrier_semaphore()
    for peer in peers:
        pl.semaphore_signal(barrier, inc=1, device_id=peer, device_id_type=MESH)
    pl.semaphore_wait(barrier, len(peers))


class Sender:
    def __init__(self, send_sems, recv_sems):
        self.send_sems, self.recv_sems, self.used = send_sems, recv_sems, []

    def __call__(self, src, dst, peer):
        index = len(self.used)
        copy = pltpu.make_async_remote_copy(
            src_ref=src,
            dst_ref=dst,
            send_sem=self.send_sems.at[index],
            recv_sem=self.recv_sems.at[index],
            device_id=peer,
            device_id_type=MESH,
        )
        copy.start()
        self.used.append(copy)
        return copy

    def finish(self):
        for copy in self.used:
            copy.wait_send()


def add_tiles(count, tiles, total, product, target, fetched=lambda g: None):
    spare = total.shape[0] - 1
    total[...] = jnp.zeros_like(total)

    def group_step(g, carry):
        fetched(g)
        start = g * UNROLL
        waiting = {}
        for u in range(UNROLL + LAG):
            if u < UNROLL:
                waiting[u] = product(start + u, tiles[start + u])
            if u >= LAG:
                slot = start + u - LAG
                total[jnp.where(slot < count, target(slot), spare)] += waiting.pop(u - LAG)
        return carry

    lax.fori_loop(0, groups(count), group_step, 0)


def groups(count):
    return lax.div(count + UNROLL - 1, UNROLL)


def forward_kernel(rows, cols, count_ref, window, tiles, out, total):
    add_tiles(
        count_ref[0], tiles, total,
        lambda slot, tile: jnp.dot(tile, window[cols[slot]], preferred_element_type=F32),
        lambda slot: rows[slot],
    )
    out[...] = total[: out.shape[0]].astype(BF16)


def backward_kernel(rows, cols, count_ref, grads, tiles, out, held, total, sems):
    def fetch(g):
        at = pl.ds(g * UNROLL, UNROLL)
        return pltpu.make_async_copy(tiles.at[at], held.at[at], sems.at[g])

    def start(g, carry):
        fetch(g).start()
        return carry

    lax.fori_loop(0, groups(count_ref[0]), start, 0)
    add_tiles(
        count_ref[0], held, total,
        lambda slot, tile: jnp.dot(grads[rows[slot]], tile, preferred_element_type=F32),
        lambda slot: cols[slot],
        lambda g: fetch(g).wait(),
    )
    out[...] = total[: out.shape[0]].astype(BF16)


SMEM = pl.BlockSpec(memory_space=pltpu.SMEM)
VMEM = pl.BlockSpec(memory_space=pltpu.VMEM)
HBM = pl.BlockSpec(memory_space=pltpu.HBM)


def tile_sum(kernel, blocks, tile_rows, tile_cols, tile_count, source, tiles, tiles_spec, scratch, limit):
    slots, size, _ = tiles.shape
    return pl.pallas_call(
        kernel,
        out_shape=pltpu.VMEM((blocks, size, size), BF16),
        in_specs=[SMEM] * 3 + [VMEM, tiles_spec],
        out_specs=VMEM,
        scratch_shapes=scratch,
        compiler_params=pltpu.CompilerParams(vmem_limit_bytes=limit),
        cost_estimate=pl.CostEstimate(flops=2 * slots * size**3, bytes_accessed=slots * 2 * size**2, transcendentals=0),
        name=kernel.__name__.replace("kernel", "sum"),
    )(tile_rows, tile_cols, tile_count, source, tiles)


def forward_sum(tile_rows, tile_cols, tile_count, window, held):
    blocks, size, half = window.shape
    scratch = [pltpu.VMEM((blocks // 3 + 1, size, half), F32)]
    return tile_sum(forward_kernel, blocks // 3, tile_rows, tile_cols, tile_count, window, held, VMEM, scratch, 24 * MIB)


def backward_sum(tile_rows, tile_cols, tile_count, grads, tiles):
    blocks, half, size = grads.shape
    scratch = [
        pltpu.VMEM(tiles.shape, BF16),
        pltpu.VMEM((3 * blocks + 1, half, size), F32),
        pltpu.SemaphoreType.DMA((tiles.shape[0] // UNROLL,)),
    ]
    return tile_sum(backward_kernel, 3 * blocks, tile_rows, tile_cols, tile_count, grads, tiles, HBM, scratch, 50 * MIB)


HALO_CHUNKS = 4


def halo_kernel(
    features, cotangent, w_self, w_neigh, bias, tiles,
    window, held, own_far, cot_far, w_self_far, w_neigh_far, bias_far,
    load_sems, send_sems, recv_sems,
):
    row, col, edge, core, _ = place()
    rows = lax.axis_size("row")
    up, down = {"row": lax.rem(row + 1, rows)}, {"row": lax.rem(row + rows - 1, rows)}
    twin, partner = {"edge": edge + 1 - 2 * core}, {"col": 1 - col}
    blocks = features.shape[0]
    share = blocks // 8
    greet([up, down, twin, partner])
    send = Sender(send_sems, recv_sems)
    step = blocks // 2 // HALO_CHUNKS
    parts = [pl.ds(core * (blocks // 2) + i * step, step) for i in range(HALO_CHUNKS)]
    arriving = []
    for part in parts:
        for side, peer in ((0, up), (2, down)):
            landing = pl.ds(side * blocks + core * (blocks // 2) + (len(arriving) // 2) * step, step)
            arriving.append((landing, send(features.at[part], window.at[landing], peer)))
    theirs = pl.ds(edge * 2 * share + (1 - col) * share, share)
    theirs_cot = pl.ds((1 - col) * share, share)
    swaps = [
        send(features.at[theirs], own_far, partner),
        send(cotangent.at[theirs_cot], cot_far, partner),
        send(w_self, w_self_far, partner),
        send(w_neigh, w_neigh_far, partner),
        send(bias, bias_far, partner),
    ]
    many = tiles.shape[0] // LOADS
    loads = [pltpu.make_async_copy(features, window.at[pl.ds(blocks, blocks)], load_sems.at[LOADS])]
    for i in range(LOADS):
        at = pl.ds(i * many, many)
        loads.append(pltpu.make_async_copy(tiles.at[at], held.at[at], load_sems.at[i]))
    for load in loads:
        load.start()
    handed = []
    for landing, copy in arriving:
        copy.wait_recv()
        handed.append(send(window.at[landing], window.at[landing], twin))
    for copy in swaps + handed:
        copy.wait_recv()
    for load in loads:
        load.wait()
    send.finish()


def exchange_inputs(features, cotangent, w_self, w_neigh, bias, tiles):
    blocks, size, half = features.shape
    share = blocks // 8
    shapes = [
        jax.ShapeDtypeStruct((3 * blocks, size, half), BF16),
        tiles,
        jax.ShapeDtypeStruct((share, size, half), BF16),
        jax.ShapeDtypeStruct((share, size, half), BF16),
        w_self, w_neigh, bias,
    ]
    copies = 4 * HALO_CHUNKS + 5
    return pl.pallas_call(
        halo_kernel,
        out_shape=[pltpu.VMEM(s.shape, s.dtype) for s in shapes],
        in_specs=[HBM] * 6,
        out_specs=[VMEM] * 7,
        scratch_shapes=[
            pltpu.SemaphoreType.DMA((LOADS + 1,)),
            pltpu.SemaphoreType.DMA((copies,)),
            pltpu.SemaphoreType.DMA((copies,)),
        ],
        compiler_params=pltpu.CompilerParams(collective_id=1, has_side_effects=True, vmem_limit_bytes=24 * MIB),
        name="exchange_inputs",
    )(features, cotangent, w_self, w_neigh, bias, tiles)


def mid_kernel(
    partial, features, own_far, cotangent, cot_far, w_self, w_neigh, w_self_far, w_neigh_far, bias, bias_far,
    grads, out_near, self_near, weight_sum, far,
    got_core, sent_pair, kept, got_pair, sent_col, got_col, own, cot, weights, sent_grads,
    w_all, w_bias, w_sent_x, w_got_x, w_sent_z, w_got_z, w_sent_e, w_got_e,
    local_sems, send_sems, recv_sems,
):
    row, col, edge, core, pair_side = place()
    other = 1 - col
    twin, pair, partner = {"edge": edge + 1 - 2 * core}, {"edge": lax.rem(edge + 2, 4)}, {"col": other}
    diagonal = {"edge": lax.rem(edge + 2, 4), "col": other}
    x, z = lax.rem(row, 4), lax.div(row, 4)
    along_x = [lax.rem(x + j, 4) for j in (1, 2, 3)]
    along_z = [lax.rem(z + j, 4) for j in (1, 2, 3)]
    along_e = [lax.rem(edge + j, 4) for j in (1, 2, 3)]
    x_peers = [{"row": z * 4 + to} for to in along_x]
    z_peers = [{"row": to * 4 + x} for to in along_z]
    e_peers = [{"edge": to} for to in along_e]
    blocks, size, half = partial.shape
    share = blocks // 8
    near_rows = own_far.shape[0] * size
    local = [
        pltpu.make_async_copy(features.at[pl.ds(edge * 2 * share + col * share, share)], own, local_sems.at[0]),
        pltpu.make_async_copy(cotangent.at[pl.ds(col * share, share)], cot, local_sems.at[1]),
    ]
    for copy in local:
        copy.start()
    greet([partner, diagonal] + e_peers + x_peers + z_peers)
    send = Sender(send_sems, recv_sems)

    def piece(side, on_core, column):
        return pl.ds((2 * side + on_core) * 2 * share + column * share, share)

    order = [(1 - pair_side, other), (1 - pair_side, col), (pair_side, other), (pair_side, col)]
    to_twin = [
        send(partial.at[piece(side, 1 - core, column)], got_core.at[i], twin)
        for i, (side, column) in enumerate(order)
    ]
    near_w, far_w = pl.ds(pl.multiple_of(col * half, half), half), pl.ds(pl.multiple_of(other * half, half), half)
    for k, (near, away) in enumerate(((w_self, w_self_far), (w_neigh, w_neigh_far))):
        for j, rows in enumerate((near_w, far_w)):
            at = pl.ds((2 * k + j) * half, half)
            weights[at, :half] = near[rows, :]
            weights[at, half:] = away[rows, :]

    def summed(i):
        to_twin[i].wait_recv()
        side, column = order[i]
        return partial[piece(side, core, column)].astype(F32) + got_core[i].astype(F32)

    to_pair = []
    for i in range(2):
        sent_pair[i] = summed(i).astype(BF16)
        to_pair.append(send(sent_pair.at[i], got_pair.at[i], pair))
    for i in range(2):
        kept[i] = summed(2 + i)
    to_pair[0].wait_recv()
    sent_col[...] = (kept[0] + got_pair[0].astype(F32)).astype(BF16)
    to_partner = send(sent_col, got_col, partner)
    for copy in local:
        copy.wait()
    to_pair[1].wait_recv()
    agg_near = (kept[1] + got_pair[1].astype(F32)).astype(BF16)
    to_partner.wait_recv()

    def flat(blocks_of):
        return blocks_of.reshape(near_rows, half)

    mixed = jnp.concatenate(
        [flat(own[...]), flat(own_far[...]), flat(agg_near), flat(got_col[...])], axis=1
    )
    pre = jnp.dot(mixed, weights[...], preferred_element_type=F32) + jnp.concatenate(
        [bias[...], bias_far[...]], axis=1
    )
    sigm = jax.nn.sigmoid(pre)
    cot_full = jnp.concatenate([flat(cot[...]), flat(cot_far[...])], axis=1).astype(F32)
    grad_pre = cot_full * sigm * (1.0 + pre * (1.0 - sigm))
    grad_low = grad_pre.astype(BF16)
    over_cols = (((1,), (1,)), ((), ()))
    agg_back = lax.dot_general(
        weights[2 * half :, :], grad_low, over_cols, preferred_element_type=F32
    ).astype(BF16)
    mine = pl.ds(edge * 2 * share + col * share, share)
    for b in range(share):
        grads[edge * 2 * share + col * share + b] = agg_back[:half, b * size : (b + 1) * size]
        sent_grads[b] = agg_back[half:, b * size : (b + 1) * size]
    crossing = [
        send(sent_grads, grads.at[mine], diagonal),
        send(sent_grads, grads.at[mine], partner),
        send(grads.at[mine], grads.at[mine], pair),
    ]
    handed = [send(grads.at[mine], grads.at[mine], twin)]

    parts = lax.dot_general(mixed, grad_low, (((0,), (0,)), ((), ())), preferred_element_type=F32)
    for k in range(2):
        for j, start in enumerate((col * half, other * half)):
            at = (2 * k + j) * half
            w_all[pl.ds(pl.multiple_of(2 * k * half + start, half), half), :] = parts[at : at + half, :]
    w_bias[...] = jnp.sum(grad_pre.reshape(near_rows // 16, 16, 2 * half), axis=0)

    def spread(start, many, sent, got, targets, peers):
        steps = []
        for j in range(3):
            sent[j, :many] = w_all[pl.ds(pl.multiple_of(start + targets[j] * many, 8), many), :].astype(sent.dtype)
            sent[j, many:] = w_bias[...].astype(sent.dtype)
            steps.append(send(sent.at[j], got.at[j], peers[j]))
        return steps

    def collect(start, many, got, steps):
        for j in range(3):
            steps[j].wait_recv()
        at = pl.ds(start, many)
        got3 = got[...].astype(F32)
        w_all[at, :] += got3[0, :many] + got3[1, :many] + got3[2, :many]
        w_bias[...] += got3[0, many:] + got3[1, many:] + got3[2, many:]

    x_many, z_many, e_many = 4 * half // 4, 4 * half // 16, 4 * half // 64
    x_start = pl.multiple_of(x * x_many, 8)
    z_start = pl.multiple_of(x_start + z * z_many, 8)
    e_start = pl.multiple_of(z_start + edge * e_many, 8)
    steps = spread(0, x_many, w_sent_x, w_got_x, along_x, x_peers)

    output = (pre * sigm).astype(BF16)
    out_near[...] = output[:, :half]
    far[:near_rows] = output[:, half:]
    self_back = lax.dot_general(grad_low, weights[: 2 * half, :], over_cols, preferred_element_type=F32)
    self_near[...] = self_back[:, :half]
    far[near_rows:] = self_back[:, half:].astype(BF16)

    collect(x_start, x_many, w_got_x, steps)
    steps = spread(x_start, z_many, w_sent_z, w_got_z, along_z, z_peers)

    far_edge = lax.rem(edge + 2, 4)
    homes = [
        pl.ds(far_edge * 2 * share + other * share, share),
        pl.ds(edge * 2 * share + other * share, share),
        pl.ds(far_edge * 2 * share + col * share, share),
    ]
    for k in (1, 2, 0):
        crossing[k].wait_recv()
        handed.append(send(grads.at[homes[k]], grads.at[homes[k]], twin))
    collect(z_start, z_many, w_got_z, steps)
    steps = spread(z_start, e_many, w_sent_e, w_got_e, along_e, e_peers)
    collect(e_start, e_many, w_got_e, steps)
    for j in range(2):
        weight_sum[j, :e_many] = w_all[pl.ds(e_start, e_many), j * half : (j + 1) * half]
        weight_sum[j, e_many:] = w_bias[:, j * half : (j + 1) * half]
    for copy in handed:
        copy.wait_recv()
    send.finish()


def middle(partial, features, own_far, cotangent, cot_far, w_self, w_neigh, w_self_far, w_neigh_far, bias, bias_far):
    blocks, size, half = partial.shape
    share = blocks // 8
    rows = share * size
    copies = 4 + 2 + 1 + 3 + 4 + 9
    top = 4 * half
    piece = (share, size, half)
    return pl.pallas_call(
        mid_kernel,
        out_shape=[
            pltpu.VMEM((blocks, half, size), BF16),
            pltpu.VMEM((rows, half), BF16),
            pltpu.VMEM((rows, half), F32),
            pltpu.VMEM((2, top // 64 + 16, half), F32),
            jax.ShapeDtypeStruct((2 * rows, half), BF16),
        ],
        in_specs=[VMEM, HBM, VMEM, HBM] + [VMEM] * 7,
        out_specs=[VMEM] * 5,
        scratch_shapes=[
            pltpu.VMEM((4,) + piece, BF16),
            pltpu.VMEM((2,) + piece, BF16),
            pltpu.VMEM((2,) + piece, F32),
            pltpu.VMEM((2,) + piece, BF16),
            pltpu.VMEM(piece, BF16),
            pltpu.VMEM(piece, BF16),
            pltpu.VMEM(piece, BF16),
            pltpu.VMEM(piece, BF16),
            pltpu.VMEM((4 * half, 2 * half), BF16),
            pltpu.VMEM((share, half, size), BF16),
            pltpu.VMEM((top, 2 * half), F32),
            pltpu.VMEM((16, 2 * half), F32),
            *[pltpu.VMEM((3, top // 4 + 16, 2 * half), BF16)] * 2,
            *[pltpu.VMEM((3, top // 16 + 16, 2 * half), F32)] * 2,
            *[pltpu.VMEM((3, top // 64 + 16, 2 * half), F32)] * 2,
            pltpu.SemaphoreType.DMA((2,)),
            pltpu.SemaphoreType.DMA((copies,)),
            pltpu.SemaphoreType.DMA((copies,)),
        ],
        compiler_params=pltpu.CompilerParams(collective_id=2, has_side_effects=True, vmem_limit_bytes=8 * MIB),
        name="middle",
    )(partial, features, own_far, cotangent, cot_far, w_self, w_neigh, w_self_far, w_neigh_far, bias, bias_far)


def final_kernel(
    back, weight_sum,
    sums, weights, bias_total,
    got_core, sent_row, kept, got_row, sent_pair, got_pair, got_col,
    send_sems, recv_sems,
):
    row, col, edge, core, side = place()
    rows = lax.axis_size("row")
    x, z = lax.rem(row, 4), lax.div(row, 4)
    twin, pair, partner = {"edge": edge + 1 - 2 * core}, {"edge": lax.rem(edge + 2, 4)}, {"col": 1 - col}
    up, down = {"row": lax.rem(row + 1, rows)}, {"row": lax.rem(row + rows - 1, rows)}
    x_peers = [{"row": z * 4 + lax.rem(x + j, 4)} for j in (1, 2, 3)]
    z_peers = [{"row": lax.rem(z + j, 4) * 4 + x} for j in (1, 2, 3)]
    e_peers = [{"edge": lax.rem(edge + j, 4)} for j in (1, 2, 3)]
    greet([partner, up, down] + e_peers + x_peers + z_peers)
    send = Sender(send_sems, recv_sems)
    blocks = back.shape[0] // 3
    share = blocks // 4

    def piece(part, at_side, on_core):
        return pl.ds(part * blocks + (2 * at_side + on_core) * share, share)

    order = [(0, 1 - side), (2, 1 - side), (0, side), (2, side), (1, 1 - side), (1, side)]
    to_twin = [
        send(back.at[piece(part, at, 1 - core)], got_core.at[i], twin) for i, (part, at) in enumerate(order)
    ]
    to_partner = send(weight_sum.at[1], got_col, partner)

    def summed(i):
        to_twin[i].wait_recv()
        part, at = order[i]
        return back[piece(part, at, core)].astype(F32) + got_core[i].astype(F32)

    to_row = []
    for i in range(4):
        sent_row[i] = summed(i).astype(BF16)
        to_row.append(send(sent_row.at[i], got_row.at[i], down if i % 2 == 0 else up))

    top = weights.shape[0]
    many = top // 64
    to_partner.wait_recv()
    start = pl.multiple_of(x * (top // 4) + z * (top // 16) + edge * many, 8)
    weights[pl.ds(start, many), :] = weight_sum[0, :many] + got_col[:many]
    bias_total[...] = weight_sum[0, many:] + got_col[many:]

    def gathered(start, many, peers):
        at = pl.ds(pl.multiple_of(start, 8), many)
        return [send(weights.at[at], weights.at[at], peer) for peer in peers]

    steps = gathered(start, many, e_peers)
    for i in range(2):
        kept[i] = summed(4 + i)
    for step in steps:
        step.wait_recv()
    steps = gathered(x * (top // 4) + z * (top // 16), top // 16, z_peers)
    for i in range(2):
        to_row[i].wait_recv()
    sent_pair[...] = (kept[0] + got_row[0].astype(F32) + got_row[1].astype(F32)).astype(BF16)
    to_pair = send(sent_pair, got_pair, pair)
    for step in steps:
        step.wait_recv()
    steps = gathered(x * (top // 4), top // 4, x_peers)
    for i in range(2, 4):
        to_row[i].wait_recv()
    kept[1] += got_row[2].astype(F32) + got_row[3].astype(F32)
    to_pair.wait_recv()
    sums[...] = kept[1] + got_pair[...].astype(F32)
    for step in steps:
        step.wait_recv()
    send.finish()


def finish(back, weight_sum):
    share, half, size = back.shape[0] // 12, back.shape[1], back.shape[2]
    unit = weight_sum.shape[1]
    copies = 6 + 4 + 1 + 1 + 9
    piece = (share, half, size)
    return pl.pallas_call(
        final_kernel,
        out_shape=[
            pltpu.VMEM(piece, F32),
            pltpu.VMEM((4 * half, half), F32),
            pltpu.VMEM((16, half), F32),
        ],
        in_specs=[VMEM] * 2,
        out_specs=[VMEM] * 3,
        scratch_shapes=[
            pltpu.VMEM((6,) + piece, BF16),
            pltpu.VMEM((4,) + piece, BF16),
            pltpu.VMEM((2,) + piece, F32),
            pltpu.VMEM((4,) + piece, BF16),
            pltpu.VMEM(piece, BF16),
            pltpu.VMEM(piece, BF16),
            pltpu.VMEM((unit, half), F32),
            pltpu.SemaphoreType.DMA((copies,)),
            pltpu.SemaphoreType.DMA((copies,)),
        ],
        compiler_params=pltpu.CompilerParams(collective_id=3, has_side_effects=True, vmem_limit_bytes=8 * MIB),
        name="finish",
    )(back, weight_sum)


def writing_kernel(
    scale, out_near, self_near, far, sums, weights, bias_total,
    output, features_grad, w_self_grad, w_neigh_grad, bias_grad,
):
    col = lax.axis_index("col")
    rows, half = out_near.shape
    near, away = pl.multiple_of(col * rows, 16), pl.multiple_of((1 - col) * rows, 16)
    output[pl.ds(near, rows), :] = out_near[...]
    output[pl.ds(away, rows), :] = far[:rows]
    features_grad[pl.ds(near, rows), :] = self_near[...]
    features_grad[pl.ds(away, rows), :] = far[rows:].astype(F32)
    share, _, size = sums.shape
    for b in range(share):
        features_grad[b * size : (b + 1) * size, :] += sums[b].T
    top = weights.shape[0]
    w_self_grad[...] = weights[: top // 2] * scale
    w_neigh_grad[...] = weights[top // 2 :] * scale
    bias_grad[...] = jnp.sum(bias_total[...], axis=0, keepdims=True) * scale


def written(scale, out_near, self_near, far, sums, weights, bias_total):
    rows, half = out_near.shape
    top = weights.shape[0]
    return pl.pallas_call(
        functools.partial(writing_kernel, scale),
        out_shape=[
            jax.ShapeDtypeStruct((2 * rows, half), BF16),
            jax.ShapeDtypeStruct((2 * rows, half), F32),
            jax.ShapeDtypeStruct((top // 2, half), F32),
            jax.ShapeDtypeStruct((top // 2, half), F32),
            jax.ShapeDtypeStruct((1, half), F32),
        ],
        in_specs=[VMEM] * 6,
        out_specs=[VMEM] * 5,
        compiler_params=pltpu.CompilerParams(vmem_limit_bytes=4 * MIB),
        name="written",
    )(out_near, self_near, far, sums, weights, bias_total)


def local(features, tiles, tile_rows, tile_cols, tile_count, w_self, w_neigh, bias, cotangent):
    rows_dev, half = features.shape
    size = tiles.shape[1]
    blocks = rows_dev // size
    nodes = rows_dev * lax.axis_size("row")
    scale = 1.0 / math.sqrt(nodes)

    own = features.reshape(blocks, size, half)
    cot = cotangent.reshape(-1, size, half)
    bias_row = bias.reshape(1, half)
    window, held, own_far, cot_far, w_self_far, w_neigh_far, bias_far = exchange_inputs(
        own, cot, w_self, w_neigh, bias_row, tiles
    )
    partial = forward_sum(tile_rows, tile_cols, tile_count, window, held)
    grads, out_near, self_near, weight_sum, far = middle(
        partial, own, own_far, cot, cot_far, w_self, w_neigh, w_self_far, w_neigh_far, bias_row, bias_far
    )
    far = lax.ppermute(far, "col", [(0, 1), (1, 0)])
    back = backward_sum(tile_rows, tile_cols, tile_count, grads, tiles)
    sums, weights, bias_total = finish(back, weight_sum)
    output, features_grad, w_self_grad, w_neigh_grad, bias_grad = written(
        scale, out_near, self_near, far, sums, weights, bias_total
    )
    return (output, features_grad, w_self_grad, w_neigh_grad, bias_grad.reshape(half))


def solution(mesh):
    return jax.shard_map(
        local,
        mesh=mesh,
        in_specs=(
            P("row", "col"),
            P(("row", "edge"), None, None),
            P(("row", "edge")),
            P(("row", "edge")),
            P(("row", "edge")),
            P(None, "col"),
            P(None, "col"),
            P("col"),
            P(("row", "edge"), "col"),
        ),
        out_specs=(
            P(("row", "edge"), "col"),
            P(("row", "edge"), "col"),
            P(None, "col"),
            P(None, "col"),
            P("col"),
        ),
        check_vma=False,
    )
```

```python
import functools
import math

import jax
import jax.numpy as jnp
from jax import lax
from jax.experimental import pallas as pl
from jax.experimental.pallas import tpu as pltpu
from jax.sharding import PartitionSpec as P

F32 = jnp.float32
BF16 = jnp.bfloat16
UNROLL = 88
LAG = 4
MIB = 1024 * 1024


MESH = pl.DeviceIdType.MESH


def place():
    row, col, edge = (lax.axis_index(name) for name in ("row", "col", "edge"))
    return row, col, edge, lax.rem(edge, 2), lax.div(edge, 2)


def greet(peers):
    barrier = pltpu.get_barrier_semaphore()
    for peer in peers:
        pl.semaphore_signal(barrier, inc=1, device_id=peer, device_id_type=MESH)
    pl.semaphore_wait(barrier, len(peers))


class Sender:
    def __init__(self, send_sems, recv_sems):
        self.send_sems, self.recv_sems, self.used = send_sems, recv_sems, []

    def __call__(self, src, dst, peer):
        index = len(self.used)
        copy = pltpu.make_async_remote_copy(
            src_ref=src,
            dst_ref=dst,
            send_sem=self.send_sems.at[index],
            recv_sem=self.recv_sems.at[index],
            device_id=peer,
            device_id_type=MESH,
        )
        copy.start()
        self.used.append(copy)
        return copy

    def finish(self):
        for copy in self.used:
            copy.wait_send()


def add_tiles(count, tiles, held, sems, total, product, target):
    spare = total.shape[0] - 1
    groups = lax.div(count + UNROLL - 1, UNROLL)

    def fetch(g):
        at = pl.ds(g * UNROLL, UNROLL)
        return pltpu.make_async_copy(tiles.at[at], held.at[at], sems.at[g])

    def start_step(g, carry):
        fetch(g).start()
        return carry

    lax.fori_loop(0, groups, start_step, 0)
    total[...] = jnp.zeros_like(total)

    def group_step(g, carry):
        fetch(g).wait()
        start = g * UNROLL
        waiting = {}
        for u in range(UNROLL + LAG):
            if u < UNROLL:
                waiting[u] = product(start + u, held[start + u])
            if u >= LAG:
                slot = start + u - LAG
                total[jnp.where(slot < count, target(slot), spare)] += waiting.pop(u - LAG)
        return carry

    lax.fori_loop(0, groups, group_step, 0)


def forward_kernel(rows, cols, count_ref, window, tiles, out, held, total, sems):
    add_tiles(
        count_ref[0], tiles, held, sems, total,
        lambda slot, tile: jnp.dot(tile, window[cols[slot]], preferred_element_type=F32),
        lambda slot: rows[slot],
    )
    out[...] = total[: out.shape[0]].astype(BF16)


def backward_kernel(rows, cols, count_ref, grads, tiles, out, held, total, sems):
    add_tiles(
        count_ref[0], tiles, held, sems, total,
        lambda slot, tile: jnp.dot(grads[rows[slot]], tile, preferred_element_type=F32),
        lambda slot: cols[slot],
    )
    out[...] = total[: out.shape[0]].astype(BF16)


SMEM = pl.BlockSpec(memory_space=pltpu.SMEM)
VMEM = pl.BlockSpec(memory_space=pltpu.VMEM)
HBM = pl.BlockSpec(memory_space=pltpu.HBM)


def tile_sum(kernel, blocks, tile_rows, tile_cols, tile_count, source, tiles):
    slots, size, _ = tiles.shape
    return pl.pallas_call(
        kernel,
        out_shape=pltpu.VMEM((blocks, size, size), BF16),
        in_specs=[SMEM] * 3 + [VMEM, HBM],
        out_specs=VMEM,
        scratch_shapes=[
            pltpu.VMEM(tiles.shape, BF16),
            pltpu.VMEM((blocks + 1, size, size), F32),
            pltpu.SemaphoreType.DMA((slots // UNROLL,)),
        ],
        compiler_params=pltpu.CompilerParams(vmem_limit_bytes=32 * MIB),
        cost_estimate=pl.CostEstimate(flops=2 * slots * size**3, bytes_accessed=slots * 2 * size**2, transcendentals=0),
        name=kernel.__name__.replace("kernel", "sum"),
    )(tile_rows, tile_cols, tile_count, source, tiles)


HALO_CHUNKS = 4


def halo_kernel(
    features, cotangent, w_self, w_neigh, bias,
    window, own_far, cot_far, w_self_far, w_neigh_far, bias_far,
    load_sem, send_sems, recv_sems,
):
    row, col, edge, core, _ = place()
    rows = lax.axis_size("row")
    up, down = {"row": lax.rem(row + 1, rows)}, {"row": lax.rem(row + rows - 1, rows)}
    twin, partner = {"edge": edge + 1 - 2 * core}, {"col": 1 - col}
    blocks = features.shape[0]
    share = blocks // 8
    greet([up, down, twin, partner])
    send = Sender(send_sems, recv_sems)
    step = blocks // 2 // HALO_CHUNKS
    parts = [pl.ds(core * (blocks // 2) + i * step, step) for i in range(HALO_CHUNKS)]
    arriving = []
    for part in parts:
        for side, peer in ((0, up), (2, down)):
            landing = pl.ds(side * blocks + core * (blocks // 2) + (len(arriving) // 2) * step, step)
            arriving.append((landing, send(features.at[part], window.at[landing], peer)))
    theirs = pl.ds(edge * 2 * share + (1 - col) * share, share)
    theirs_cot = pl.ds((1 - col) * share, share)
    swaps = [
        send(features.at[theirs], own_far, partner),
        send(cotangent.at[theirs_cot], cot_far, partner),
        send(w_self, w_self_far, partner),
        send(w_neigh, w_neigh_far, partner),
        send(bias, bias_far, partner),
    ]
    load = pltpu.make_async_copy(features, window.at[pl.ds(blocks, blocks)], load_sem)
    load.start()
    handed = []
    for landing, copy in arriving:
        copy.wait_recv()
        handed.append(send(window.at[landing], window.at[landing], twin))
    for copy in swaps + handed:
        copy.wait_recv()
    load.wait()
    send.finish()


def exchange_inputs(features, cotangent, w_self, w_neigh, bias):
    blocks, size, half = features.shape
    share = blocks // 8
    shapes = [
        jax.ShapeDtypeStruct((3 * blocks, size, half), BF16),
        jax.ShapeDtypeStruct((share, size, half), BF16),
        jax.ShapeDtypeStruct((share, size, half), BF16),
        w_self, w_neigh, bias,
    ]
    copies = 4 * HALO_CHUNKS + 5
    return pl.pallas_call(
        halo_kernel,
        out_shape=[pltpu.VMEM(s.shape, s.dtype) for s in shapes],
        in_specs=[HBM] * 5,
        out_specs=[VMEM] * 6,
        scratch_shapes=[
            pltpu.SemaphoreType.DMA,
            pltpu.SemaphoreType.DMA((copies,)),
            pltpu.SemaphoreType.DMA((copies,)),
        ],
        compiler_params=pltpu.CompilerParams(collective_id=1, has_side_effects=True, vmem_limit_bytes=32 * MIB),
        name="exchange_inputs",
    )(features, cotangent, w_self, w_neigh, bias)


def mid_kernel(
    partial, features, own_far, cotangent, cot_far, w_self, w_neigh, w_self_far, w_neigh_far, bias, bias_far,
    grads, out_near, self_near, weight_sum, far,
    got_core, sent_pair, kept, got_pair, sent_col, got_col, own, cot, weights, sent_grads,
    w_all, w_bias, w_sent_x, w_got_x, w_sent_z, w_got_z, w_sent_e, w_got_e,
    local_sems, send_sems, recv_sems,
):
    row, col, edge, core, pair_side = place()
    other = 1 - col
    twin, pair, partner = {"edge": edge + 1 - 2 * core}, {"edge": lax.rem(edge + 2, 4)}, {"col": other}
    diagonal = {"edge": lax.rem(edge + 2, 4), "col": other}
    x, z = lax.rem(row, 4), lax.div(row, 4)
    along_x = [lax.rem(x + j, 4) for j in (1, 2, 3)]
    along_z = [lax.rem(z + j, 4) for j in (1, 2, 3)]
    along_e = [lax.rem(edge + j, 4) for j in (1, 2, 3)]
    x_peers = [{"row": z * 4 + to} for to in along_x]
    z_peers = [{"row": to * 4 + x} for to in along_z]
    e_peers = [{"edge": to} for to in along_e]
    blocks, size, half = partial.shape
    share = blocks // 8
    near_rows = own_far.shape[0] * size
    local = [
        pltpu.make_async_copy(features.at[pl.ds(edge * 2 * share + col * share, share)], own, local_sems.at[0]),
        pltpu.make_async_copy(cotangent.at[pl.ds(col * share, share)], cot, local_sems.at[1]),
    ]
    for copy in local:
        copy.start()
    greet([partner, diagonal] + e_peers + x_peers + z_peers)
    send = Sender(send_sems, recv_sems)

    def piece(side, on_core, column):
        return pl.ds((2 * side + on_core) * 2 * share + column * share, share)

    order = [(1 - pair_side, other), (1 - pair_side, col), (pair_side, other), (pair_side, col)]
    to_twin = [
        send(partial.at[piece(side, 1 - core, column)], got_core.at[i], twin)
        for i, (side, column) in enumerate(order)
    ]
    near_w, far_w = pl.ds(pl.multiple_of(col * half, half), half), pl.ds(pl.multiple_of(other * half, half), half)
    for k, (near, away) in enumerate(((w_self, w_self_far), (w_neigh, w_neigh_far))):
        for j, rows in enumerate((near_w, far_w)):
            at = pl.ds((2 * k + j) * half, half)
            weights[at, :half] = near[rows, :]
            weights[at, half:] = away[rows, :]

    def summed(i):
        to_twin[i].wait_recv()
        side, column = order[i]
        return partial[piece(side, core, column)].astype(F32) + got_core[i].astype(F32)

    to_pair = []
    for i in range(2):
        sent_pair[i] = summed(i).astype(BF16)
        to_pair.append(send(sent_pair.at[i], got_pair.at[i], pair))
    for i in range(2):
        kept[i] = summed(2 + i)
    to_pair[0].wait_recv()
    sent_col[...] = (kept[0] + got_pair[0].astype(F32)).astype(BF16)
    to_partner = send(sent_col, got_col, partner)
    for copy in local:
        copy.wait()
    to_pair[1].wait_recv()
    agg_near = (kept[1] + got_pair[1].astype(F32)).astype(BF16)
    to_partner.wait_recv()

    def flat(blocks_of):
        return blocks_of.reshape(near_rows, half)

    mixed = jnp.concatenate(
        [flat(own[...]), flat(own_far[...]), flat(agg_near), flat(got_col[...])], axis=1
    )
    pre = jnp.dot(mixed, weights[...], preferred_element_type=F32) + jnp.concatenate(
        [bias[...], bias_far[...]], axis=1
    )
    sigm = jax.nn.sigmoid(pre)
    cot_full = jnp.concatenate([flat(cot[...]), flat(cot_far[...])], axis=1).astype(F32)
    grad_pre = cot_full * sigm * (1.0 + pre * (1.0 - sigm))
    grad_low = grad_pre.astype(BF16)
    over_cols = (((1,), (1,)), ((), ()))
    agg_back = lax.dot_general(
        weights[2 * half :, :], grad_low, over_cols, preferred_element_type=F32
    ).astype(BF16)
    mine = pl.ds(edge * 2 * share + col * share, share)
    for b in range(share):
        grads[edge * 2 * share + col * share + b] = agg_back[:half, b * size : (b + 1) * size]
        sent_grads[b] = agg_back[half:, b * size : (b + 1) * size]
    crossing = [
        send(sent_grads, grads.at[mine], diagonal),
        send(sent_grads, grads.at[mine], partner),
        send(grads.at[mine], grads.at[mine], pair),
    ]
    handed = [send(grads.at[mine], grads.at[mine], twin)]

    parts = lax.dot_general(mixed, grad_low, (((0,), (0,)), ((), ())), preferred_element_type=F32)
    for k in range(2):
        for j, start in enumerate((col * half, other * half)):
            at = (2 * k + j) * half
            w_all[pl.ds(pl.multiple_of(2 * k * half + start, half), half), :] = parts[at : at + half, :]
    w_bias[...] = jnp.sum(grad_pre.reshape(near_rows // 16, 16, 2 * half), axis=0)

    def spread(start, many, sent, got, targets, peers):
        steps = []
        for j in range(3):
            sent[j, :many] = w_all[pl.ds(pl.multiple_of(start + targets[j] * many, 8), many), :].astype(sent.dtype)
            sent[j, many:] = w_bias[...].astype(sent.dtype)
            steps.append(send(sent.at[j], got.at[j], peers[j]))
        return steps

    def collect(start, many, got, steps):
        for j in range(3):
            steps[j].wait_recv()
        at = pl.ds(start, many)
        got3 = got[...].astype(F32)
        w_all[at, :] += got3[0, :many] + got3[1, :many] + got3[2, :many]
        w_bias[...] += got3[0, many:] + got3[1, many:] + got3[2, many:]

    x_many, z_many, e_many = 4 * half // 4, 4 * half // 16, 4 * half // 64
    x_start = pl.multiple_of(x * x_many, 8)
    z_start = pl.multiple_of(x_start + z * z_many, 8)
    e_start = pl.multiple_of(z_start + edge * e_many, 8)
    steps = spread(0, x_many, w_sent_x, w_got_x, along_x, x_peers)

    output = (pre * sigm).astype(BF16)
    out_near[...] = output[:, :half]
    far[:near_rows] = output[:, half:]
    self_back = lax.dot_general(grad_low, weights[: 2 * half, :], over_cols, preferred_element_type=F32)
    self_near[...] = self_back[:, :half]
    far[near_rows:] = self_back[:, half:].astype(BF16)

    collect(x_start, x_many, w_got_x, steps)
    steps = spread(x_start, z_many, w_sent_z, w_got_z, along_z, z_peers)

    far_edge = lax.rem(edge + 2, 4)
    homes = [
        pl.ds(far_edge * 2 * share + other * share, share),
        pl.ds(edge * 2 * share + other * share, share),
        pl.ds(far_edge * 2 * share + col * share, share),
    ]
    for k in (1, 2, 0):
        crossing[k].wait_recv()
        handed.append(send(grads.at[homes[k]], grads.at[homes[k]], twin))
    collect(z_start, z_many, w_got_z, steps)
    steps = spread(z_start, e_many, w_sent_e, w_got_e, along_e, e_peers)
    collect(e_start, e_many, w_got_e, steps)
    for j in range(2):
        weight_sum[j, :e_many] = w_all[pl.ds(e_start, e_many), j * half : (j + 1) * half]
        weight_sum[j, e_many:] = w_bias[:, j * half : (j + 1) * half]
    for copy in handed:
        copy.wait_recv()
    send.finish()


def middle(partial, features, own_far, cotangent, cot_far, w_self, w_neigh, w_self_far, w_neigh_far, bias, bias_far):
    blocks, size, half = partial.shape
    share = blocks // 8
    rows = share * size
    copies = 4 + 2 + 1 + 3 + 4 + 9
    top = 4 * half
    piece = (share, size, half)
    return pl.pallas_call(
        mid_kernel,
        out_shape=[
            pltpu.VMEM((blocks, half, size), BF16),
            pltpu.VMEM((rows, half), BF16),
            pltpu.VMEM((rows, half), F32),
            pltpu.VMEM((2, top // 64 + 16, half), F32),
            jax.ShapeDtypeStruct((2 * rows, half), BF16),
        ],
        in_specs=[VMEM, HBM, VMEM, HBM] + [VMEM] * 7,
        out_specs=[VMEM] * 5,
        scratch_shapes=[
            pltpu.VMEM((4,) + piece, BF16),
            pltpu.VMEM((2,) + piece, BF16),
            pltpu.VMEM((2,) + piece, F32),
            pltpu.VMEM((2,) + piece, BF16),
            pltpu.VMEM(piece, BF16),
            pltpu.VMEM(piece, BF16),
            pltpu.VMEM(piece, BF16),
            pltpu.VMEM(piece, BF16),
            pltpu.VMEM((4 * half, 2 * half), BF16),
            pltpu.VMEM((share, half, size), BF16),
            pltpu.VMEM((top, 2 * half), F32),
            pltpu.VMEM((16, 2 * half), F32),
            *[pltpu.VMEM((3, top // 4 + 16, 2 * half), BF16)] * 2,
            *[pltpu.VMEM((3, top // 16 + 16, 2 * half), F32)] * 2,
            *[pltpu.VMEM((3, top // 64 + 16, 2 * half), F32)] * 2,
            pltpu.SemaphoreType.DMA((2,)),
            pltpu.SemaphoreType.DMA((copies,)),
            pltpu.SemaphoreType.DMA((copies,)),
        ],
        compiler_params=pltpu.CompilerParams(collective_id=2, has_side_effects=True, vmem_limit_bytes=32 * MIB),
        name="middle",
    )(partial, features, own_far, cotangent, cot_far, w_self, w_neigh, w_self_far, w_neigh_far, bias, bias_far)


def final_kernel(
    back, weight_sum,
    sums, weights, bias_total,
    got_core, sent_row, kept, got_row, sent_pair, got_pair, got_col,
    send_sems, recv_sems,
):
    row, col, edge, core, side = place()
    rows = lax.axis_size("row")
    x, z = lax.rem(row, 4), lax.div(row, 4)
    twin, pair, partner = {"edge": edge + 1 - 2 * core}, {"edge": lax.rem(edge + 2, 4)}, {"col": 1 - col}
    up, down = {"row": lax.rem(row + 1, rows)}, {"row": lax.rem(row + rows - 1, rows)}
    x_peers = [{"row": z * 4 + lax.rem(x + j, 4)} for j in (1, 2, 3)]
    z_peers = [{"row": lax.rem(z + j, 4) * 4 + x} for j in (1, 2, 3)]
    e_peers = [{"edge": lax.rem(edge + j, 4)} for j in (1, 2, 3)]
    greet([partner, up, down] + e_peers + x_peers + z_peers)
    send = Sender(send_sems, recv_sems)
    blocks = back.shape[0] // 3
    share = blocks // 4

    def piece(part, at_side, on_core):
        return pl.ds(part * blocks + (2 * at_side + on_core) * share, share)

    order = [(0, 1 - side), (2, 1 - side), (0, side), (2, side), (1, 1 - side), (1, side)]
    to_twin = [
        send(back.at[piece(part, at, 1 - core)], got_core.at[i], twin) for i, (part, at) in enumerate(order)
    ]
    to_partner = send(weight_sum.at[1], got_col, partner)

    def summed(i):
        to_twin[i].wait_recv()
        part, at = order[i]
        return back[piece(part, at, core)].astype(F32) + got_core[i].astype(F32)

    to_row = []
    for i in range(4):
        sent_row[i] = summed(i).astype(BF16)
        to_row.append(send(sent_row.at[i], got_row.at[i], down if i % 2 == 0 else up))

    top = weights.shape[0]
    many = top // 64
    to_partner.wait_recv()
    start = pl.multiple_of(x * (top // 4) + z * (top // 16) + edge * many, 8)
    weights[pl.ds(start, many), :] = weight_sum[0, :many] + got_col[:many]
    bias_total[...] = weight_sum[0, many:] + got_col[many:]

    def gathered(start, many, peers):
        at = pl.ds(pl.multiple_of(start, 8), many)
        return [send(weights.at[at], weights.at[at], peer) for peer in peers]

    steps = gathered(start, many, e_peers)
    for i in range(2):
        kept[i] = summed(4 + i)
    for step in steps:
        step.wait_recv()
    steps = gathered(x * (top // 4) + z * (top // 16), top // 16, z_peers)
    for i in range(2):
        to_row[i].wait_recv()
    sent_pair[...] = (kept[0] + got_row[0].astype(F32) + got_row[1].astype(F32)).astype(BF16)
    to_pair = send(sent_pair, got_pair, pair)
    for step in steps:
        step.wait_recv()
    steps = gathered(x * (top // 4), top // 4, x_peers)
    for i in range(2, 4):
        to_row[i].wait_recv()
    kept[1] += got_row[2].astype(F32) + got_row[3].astype(F32)
    to_pair.wait_recv()
    sums[...] = kept[1] + got_pair[...].astype(F32)
    for step in steps:
        step.wait_recv()
    send.finish()


def finish(back, weight_sum):
    share, half, size = back.shape[0] // 12, back.shape[1], back.shape[2]
    unit = weight_sum.shape[1]
    copies = 6 + 4 + 1 + 1 + 9
    piece = (share, half, size)
    return pl.pallas_call(
        final_kernel,
        out_shape=[
            pltpu.VMEM(piece, F32),
            pltpu.VMEM((4 * half, half), F32),
            pltpu.VMEM((16, half), F32),
        ],
        in_specs=[VMEM] * 2,
        out_specs=[VMEM] * 3,
        scratch_shapes=[
            pltpu.VMEM((6,) + piece, BF16),
            pltpu.VMEM((4,) + piece, BF16),
            pltpu.VMEM((2,) + piece, F32),
            pltpu.VMEM((4,) + piece, BF16),
            pltpu.VMEM(piece, BF16),
            pltpu.VMEM(piece, BF16),
            pltpu.VMEM((unit, half), F32),
            pltpu.SemaphoreType.DMA((copies,)),
            pltpu.SemaphoreType.DMA((copies,)),
        ],
        compiler_params=pltpu.CompilerParams(collective_id=3, has_side_effects=True, vmem_limit_bytes=32 * MIB),
        name="finish",
    )(back, weight_sum)


def writing_kernel(
    scale, out_near, self_near, far, sums, weights, bias_total,
    output, features_grad, w_self_grad, w_neigh_grad, bias_grad,
):
    col = lax.axis_index("col")
    rows, half = out_near.shape
    near, away = pl.multiple_of(col * rows, 16), pl.multiple_of((1 - col) * rows, 16)
    output[pl.ds(near, rows), :] = out_near[...]
    output[pl.ds(away, rows), :] = far[:rows]
    features_grad[pl.ds(near, rows), :] = self_near[...]
    features_grad[pl.ds(away, rows), :] = far[rows:].astype(F32)
    share, _, size = sums.shape
    for b in range(share):
        features_grad[b * size : (b + 1) * size, :] += sums[b].T
    top = weights.shape[0]
    w_self_grad[...] = weights[: top // 2] * scale
    w_neigh_grad[...] = weights[top // 2 :] * scale
    bias_grad[...] = jnp.sum(bias_total[...], axis=0, keepdims=True) * scale


def written(scale, out_near, self_near, far, sums, weights, bias_total):
    rows, half = out_near.shape
    top = weights.shape[0]
    return pl.pallas_call(
        functools.partial(writing_kernel, scale),
        out_shape=[
            jax.ShapeDtypeStruct((2 * rows, half), BF16),
            jax.ShapeDtypeStruct((2 * rows, half), F32),
            jax.ShapeDtypeStruct((top // 2, half), F32),
            jax.ShapeDtypeStruct((top // 2, half), F32),
            jax.ShapeDtypeStruct((1, half), F32),
        ],
        in_specs=[VMEM] * 6,
        out_specs=[VMEM] * 5,
        compiler_params=pltpu.CompilerParams(vmem_limit_bytes=4 * MIB),
        name="written",
    )(out_near, self_near, far, sums, weights, bias_total)


def local(features, tiles, tile_rows, tile_cols, tile_count, w_self, w_neigh, bias, cotangent):
    rows_dev, half = features.shape
    size = tiles.shape[1]
    blocks = rows_dev // size
    nodes = rows_dev * lax.axis_size("row")
    scale = 1.0 / math.sqrt(nodes)

    own = features.reshape(blocks, size, half)
    cot = cotangent.reshape(-1, size, half)
    bias_row = bias.reshape(1, half)
    own, cot, w_self, w_neigh, bias_row = (
        pltpu.with_memory_space_constraint(array, pltpu.HBM) for array in (own, cot, w_self, w_neigh, bias_row)
    )
    window, own_far, cot_far, w_self_far, w_neigh_far, bias_far = exchange_inputs(
        own, cot, w_self, w_neigh, bias_row
    )
    partial = tile_sum(forward_kernel, blocks, tile_rows, tile_cols, tile_count, window, tiles)
    grads, out_near, self_near, weight_sum, far = middle(
        partial, own, own_far, cot, cot_far, w_self, w_neigh, w_self_far, w_neigh_far, bias_row, bias_far
    )
    far = lax.ppermute(far, "col", [(0, 1), (1, 0)])
    back = tile_sum(backward_kernel, 3 * blocks, tile_rows, tile_cols, tile_count, grads, tiles)
    sums, weights, bias_total = finish(back, weight_sum)
    output, features_grad, w_self_grad, w_neigh_grad, bias_grad = written(
        scale, out_near, self_near, far, sums, weights, bias_total
    )
    return (output, features_grad, w_self_grad, w_neigh_grad, bias_grad.reshape(half))


def solution(mesh):
    return jax.shard_map(
        local,
        mesh=mesh,
        in_specs=(
            P("row", "col"),
            P(("row", "edge"), None, None),
            P(("row", "edge")),
            P(("row", "edge")),
            P(("row", "edge")),
            P(None, "col"),
            P(None, "col"),
            P("col"),
            P(("row", "edge"), "col"),
        ),
        out_specs=(
            P(("row", "edge"), "col"),
            P(("row", "edge"), "col"),
            P(None, "col"),
            P(None, "col"),
            P("col"),
        ),
        check_vma=False,
    )
```

```python
import functools
import math

import jax
import jax.numpy as jnp
from jax import lax
from jax.experimental import pallas as pl
from jax.experimental.pallas import tpu as pltpu
from jax.sharding import PartitionSpec as P

F32 = jnp.float32
BF16 = jnp.bfloat16
UNROLL = 88
LAG = 4
MIB = 1024 * 1024


MESH = pl.DeviceIdType.MESH


def place():
    row, col, edge = (lax.axis_index(name) for name in ("row", "col", "edge"))
    return row, col, edge, lax.rem(edge, 2), lax.div(edge, 2)


def greet(peers):
    barrier = pltpu.get_barrier_semaphore()
    for peer in peers:
        pl.semaphore_signal(barrier, inc=1, device_id=peer, device_id_type=MESH)
    pl.semaphore_wait(barrier, len(peers))


class Sender:
    def __init__(self, send_sems, recv_sems):
        self.send_sems, self.recv_sems, self.used = send_sems, recv_sems, []

    def __call__(self, src, dst, peer):
        index = len(self.used)
        copy = pltpu.make_async_remote_copy(
            src_ref=src,
            dst_ref=dst,
            send_sem=self.send_sems.at[index],
            recv_sem=self.recv_sems.at[index],
            device_id=peer,
            device_id_type=MESH,
        )
        copy.start()
        self.used.append(copy)
        return copy

    def finish(self):
        for copy in self.used:
            copy.wait_send()


def add_tiles(count, tiles, held, sems, total, product, target):
    spare = total.shape[0] - 1
    groups = lax.div(count + UNROLL - 1, UNROLL)

    def fetch(g):
        at = pl.ds(g * UNROLL, UNROLL)
        return pltpu.make_async_copy(tiles.at[at], held.at[at], sems.at[g])

    def start_step(g, carry):
        fetch(g).start()
        return carry

    lax.fori_loop(0, groups, start_step, 0)
    total[...] = jnp.zeros_like(total)

    def group_step(g, carry):
        fetch(g).wait()
        start = g * UNROLL
        waiting = {}
        for u in range(UNROLL + LAG):
            if u < UNROLL:
                waiting[u] = product(start + u, held[start + u])
            if u >= LAG:
                slot = start + u - LAG
                total[jnp.where(slot < count, target(slot), spare)] += waiting.pop(u - LAG)
        return carry

    lax.fori_loop(0, groups, group_step, 0)


def forward_kernel(rows, cols, count_ref, window, tiles, out, held, total, sems):
    add_tiles(
        count_ref[0], tiles, held, sems, total,
        lambda slot, tile: jnp.dot(tile, window[cols[slot]], preferred_element_type=F32),
        lambda slot: rows[slot],
    )
    out[...] = total[: out.shape[0]].astype(BF16)


def backward_kernel(rows, cols, count_ref, grads, tiles, out, held, total, sems):
    add_tiles(
        count_ref[0], tiles, held, sems, total,
        lambda slot, tile: jnp.dot(grads[rows[slot]], tile, preferred_element_type=F32),
        lambda slot: cols[slot],
    )
    out[...] = total[: out.shape[0]].astype(BF16)


SMEM = pl.BlockSpec(memory_space=pltpu.SMEM)
VMEM = pl.BlockSpec(memory_space=pltpu.VMEM)
HBM = pl.BlockSpec(memory_space=pltpu.HBM)


def tile_sum(kernel, blocks, tile_rows, tile_cols, tile_count, source, tiles):
    slots, size, _ = tiles.shape
    return pl.pallas_call(
        kernel,
        out_shape=pltpu.VMEM((blocks, size, size), BF16),
        in_specs=[SMEM] * 3 + [VMEM, HBM],
        out_specs=VMEM,
        scratch_shapes=[
            pltpu.VMEM(tiles.shape, BF16),
            pltpu.VMEM((blocks + 1, size, size), F32),
            pltpu.SemaphoreType.DMA((slots // UNROLL,)),
        ],
        compiler_params=pltpu.CompilerParams(vmem_limit_bytes=32 * MIB),
        cost_estimate=pl.CostEstimate(flops=2 * slots * size**3, bytes_accessed=slots * 2 * size**2, transcendentals=0),
        name=kernel.__name__.replace("kernel", "sum"),
    )(tile_rows, tile_cols, tile_count, source, tiles)


HALO_CHUNKS = 4


def halo_kernel(
    features, cotangent, w_self, w_neigh, bias,
    window, own_far, cot_far, w_self_far, w_neigh_far, bias_far,
    load_sem, send_sems, recv_sems,
):
    row, col, edge, core, _ = place()
    rows = lax.axis_size("row")
    up, down = {"row": lax.rem(row + 1, rows)}, {"row": lax.rem(row + rows - 1, rows)}
    twin, partner = {"edge": edge + 1 - 2 * core}, {"col": 1 - col}
    blocks = features.shape[0]
    share = blocks // 8
    greet([up, down, twin, partner])
    send = Sender(send_sems, recv_sems)
    step = blocks // 2 // HALO_CHUNKS
    parts = [pl.ds(core * (blocks // 2) + i * step, step) for i in range(HALO_CHUNKS)]
    arriving = []
    for part in parts:
        for side, peer in ((0, up), (2, down)):
            landing = pl.ds(side * blocks + core * (blocks // 2) + (len(arriving) // 2) * step, step)
            arriving.append((landing, send(features.at[part], window.at[landing], peer)))
    theirs = pl.ds(edge * 2 * share + (1 - col) * share, share)
    theirs_cot = pl.ds((1 - col) * share, share)
    swaps = [
        send(features.at[theirs], own_far, partner),
        send(cotangent.at[theirs_cot], cot_far, partner),
        send(w_self, w_self_far, partner),
        send(w_neigh, w_neigh_far, partner),
        send(bias, bias_far, partner),
    ]
    load = pltpu.make_async_copy(features, window.at[pl.ds(blocks, blocks)], load_sem)
    load.start()
    handed = []
    for landing, copy in arriving:
        copy.wait_recv()
        handed.append(send(window.at[landing], window.at[landing], twin))
    for copy in swaps + handed:
        copy.wait_recv()
    load.wait()
    send.finish()


def exchange_inputs(features, cotangent, w_self, w_neigh, bias):
    blocks, size, half = features.shape
    share = blocks // 8
    shapes = [
        jax.ShapeDtypeStruct((3 * blocks, size, half), BF16),
        jax.ShapeDtypeStruct((share, size, half), BF16),
        jax.ShapeDtypeStruct((share, size, half), BF16),
        w_self, w_neigh, bias,
    ]
    copies = 4 * HALO_CHUNKS + 5
    return pl.pallas_call(
        halo_kernel,
        out_shape=[pltpu.VMEM(s.shape, s.dtype) for s in shapes],
        in_specs=[HBM] * 5,
        out_specs=[VMEM] * 6,
        scratch_shapes=[
            pltpu.SemaphoreType.DMA,
            pltpu.SemaphoreType.DMA((copies,)),
            pltpu.SemaphoreType.DMA((copies,)),
        ],
        compiler_params=pltpu.CompilerParams(collective_id=1, has_side_effects=True, vmem_limit_bytes=32 * MIB),
        name="exchange_inputs",
    )(features, cotangent, w_self, w_neigh, bias)


def mid_kernel(
    partial, features, own_far, cotangent, cot_far, w_self, w_neigh, w_self_far, w_neigh_far, bias, bias_far,
    grads, out_near, self_near, weight_sum, far,
    got_core, sent, got, own, cot, weights, sent_grads,
    w_all, w_bias, w_sent_z, w_got_z, w_sent_x, w_got_x,
    local_sems, send_sems, recv_sems,
):
    row, col, edge, core, pair_side = place()
    other = 1 - col
    twin, pair, partner = {"edge": edge + 1 - 2 * core}, {"edge": lax.rem(edge + 2, 4)}, {"col": other}
    diagonal = {"edge": lax.rem(edge + 2, 4), "col": other}
    x, z = lax.rem(row, 4), lax.div(row, 4)
    along_x = [lax.rem(x + j, 4) for j in (1, 2, 3)]
    along_z = [lax.rem(z + j, 4) for j in (1, 2, 3)]
    x_peers = [{"row": z * 4 + to} for to in along_x]
    z_peers = [{"row": to * 4 + x} for to in along_z]
    blocks, size, half = partial.shape
    share = blocks // 8
    near_rows = own_far.shape[0] * size
    local = [
        pltpu.make_async_copy(features.at[pl.ds(edge * 2 * share + col * share, share)], own, local_sems.at[0]),
        pltpu.make_async_copy(cotangent.at[pl.ds(col * share, share)], cot, local_sems.at[1]),
    ]
    for copy in local:
        copy.start()
    greet([twin, pair, partner, diagonal] + x_peers + z_peers)
    send = Sender(send_sems, recv_sems)

    def piece(side, on_core, column):
        return pl.ds((2 * side + on_core) * 2 * share + column * share, share)

    order = [(pair_side, other), (1 - pair_side, other), (1 - pair_side, col), (pair_side, col)]
    to_twin = [
        send(partial.at[piece(side, 1 - core, column)], got_core.at[i], twin)
        for i, (side, column) in enumerate(order)
    ]
    near_w, far_w = pl.ds(pl.multiple_of(col * half, half), half), pl.ds(pl.multiple_of(other * half, half), half)
    for k, (near, away) in enumerate(((w_self, w_self_far), (w_neigh, w_neigh_far))):
        for j, rows in enumerate((near_w, far_w)):
            at = pl.ds((2 * k + j) * half, half)
            weights[at, :half] = near[rows, :]
            weights[at, half:] = away[rows, :]

    def summed(i):
        to_twin[i].wait_recv()
        side, column = order[i]
        return partial[piece(side, core, column)].astype(F32) + got_core[i].astype(F32)

    crossing = []
    for i, owner in enumerate((partner, diagonal, pair)):
        sent[i] = summed(i).astype(BF16)
        crossing.append(send(sent.at[i], got.at[i], owner))
    kept = summed(3)
    for copy in local:
        copy.wait()
    for copy in crossing:
        copy.wait_recv()
    agg_near = (kept + got[2].astype(F32)).astype(BF16)
    agg_far = (got[0].astype(F32) + got[1].astype(F32)).astype(BF16)

    def flat(blocks_of):
        return blocks_of.reshape(near_rows, half)

    mixed = jnp.concatenate(
        [flat(own[...]), flat(own_far[...]), flat(agg_near), flat(agg_far)], axis=1
    )
    pre = jnp.dot(mixed, weights[...], preferred_element_type=F32) + jnp.concatenate(
        [bias[...], bias_far[...]], axis=1
    )
    sigm = jax.nn.sigmoid(pre)
    cot_full = jnp.concatenate([flat(cot[...]), flat(cot_far[...])], axis=1).astype(F32)
    grad_pre = cot_full * sigm * (1.0 + pre * (1.0 - sigm))
    grad_low = grad_pre.astype(BF16)
    over_cols = (((1,), (1,)), ((), ()))
    agg_back = lax.dot_general(
        weights[2 * half :, :], grad_low, over_cols, preferred_element_type=F32
    ).astype(BF16)
    mine = pl.ds(edge * 2 * share + col * share, share)
    for b in range(share):
        grads[edge * 2 * share + col * share + b] = agg_back[:half, b * size : (b + 1) * size]
        sent_grads[b] = agg_back[half:, b * size : (b + 1) * size]
    crossing = [
        send(sent_grads, grads.at[mine], diagonal),
        send(sent_grads, grads.at[mine], partner),
        send(grads.at[mine], grads.at[mine], pair),
    ]
    handed = [send(grads.at[mine], grads.at[mine], twin)]

    parts = lax.dot_general(mixed, grad_low, (((0,), (0,)), ((), ())), preferred_element_type=F32)
    for k in range(2):
        for j, start in enumerate((col * half, other * half)):
            at = (2 * k + j) * half
            w_all[pl.ds(pl.multiple_of(2 * k * half + start, half), half), :] = parts[at : at + half, :]
    w_bias[...] = jnp.sum(grad_pre.reshape(near_rows // 16, 16, 2 * half), axis=0)

    def spread(start, many, sent, got, targets, peers):
        steps = []
        for j in range(3):
            sent[j, :many] = w_all[pl.ds(pl.multiple_of(start + targets[j] * many, 8), many), :].astype(sent.dtype)
            sent[j, many:] = w_bias[...].astype(sent.dtype)
            steps.append(send(sent.at[j], got.at[j], peers[j]))
        return steps

    def collect(start, many, got, steps):
        for j in range(3):
            steps[j].wait_recv()
        at = pl.ds(start, many)
        got3 = got[...].astype(F32)
        w_all[at, :] += got3[0, :many] + got3[1, :many] + got3[2, :many]
        w_bias[...] += got3[0, many:] + got3[1, many:] + got3[2, many:]

    z_many, x_many = 4 * half // 4, 4 * half // 16
    z_start = pl.multiple_of(z * z_many, 8)
    x_start = pl.multiple_of(z_start + x * x_many, 8)
    steps = spread(0, z_many, w_sent_z, w_got_z, along_z, z_peers)

    output = (pre * sigm).astype(BF16)
    out_near[...] = output[:, :half]
    far[:near_rows] = output[:, half:]
    self_back = lax.dot_general(grad_low, weights[: 2 * half, :], over_cols, preferred_element_type=F32)
    self_near[...] = self_back[:, :half]
    far[near_rows:] = self_back[:, half:].astype(BF16)

    collect(z_start, z_many, w_got_z, steps)
    steps = spread(z_start, x_many, w_sent_x, w_got_x, along_x, x_peers)

    far_edge = lax.rem(edge + 2, 4)
    homes = [
        pl.ds(far_edge * 2 * share + other * share, share),
        pl.ds(edge * 2 * share + other * share, share),
        pl.ds(far_edge * 2 * share + col * share, share),
    ]
    for k in (1, 2, 0):
        crossing[k].wait_recv()
        handed.append(send(grads.at[homes[k]], grads.at[homes[k]], twin))
    collect(x_start, x_many, w_got_x, steps)
    for j in range(2):
        weight_sum[j, :x_many] = w_all[pl.ds(x_start, x_many), j * half : (j + 1) * half]
        weight_sum[j, x_many:] = w_bias[:, j * half : (j + 1) * half]
    for copy in handed:
        copy.wait_recv()
    send.finish()


def middle(partial, features, own_far, cotangent, cot_far, w_self, w_neigh, w_self_far, w_neigh_far, bias, bias_far):
    blocks, size, half = partial.shape
    share = blocks // 8
    rows = share * size
    copies = 4 + 3 + 3 + 4 + 6
    top = 4 * half
    piece = (share, size, half)
    return pl.pallas_call(
        mid_kernel,
        out_shape=[
            pltpu.VMEM((blocks, half, size), BF16),
            pltpu.VMEM((rows, half), BF16),
            pltpu.VMEM((rows, half), F32),
            pltpu.VMEM((2, top // 16 + 16, half), F32),
            jax.ShapeDtypeStruct((2 * rows, half), BF16),
        ],
        in_specs=[VMEM, HBM, VMEM, HBM] + [VMEM] * 7,
        out_specs=[VMEM] * 5,
        scratch_shapes=[
            pltpu.VMEM((4,) + piece, BF16),
            pltpu.VMEM((3,) + piece, BF16),
            pltpu.VMEM((3,) + piece, BF16),
            pltpu.VMEM(piece, BF16),
            pltpu.VMEM(piece, BF16),
            pltpu.VMEM((4 * half, 2 * half), BF16),
            pltpu.VMEM((share, half, size), BF16),
            pltpu.VMEM((top, 2 * half), F32),
            pltpu.VMEM((16, 2 * half), F32),
            *[pltpu.VMEM((3, top // 4 + 16, 2 * half), BF16)] * 2,
            *[pltpu.VMEM((3, top // 16 + 16, 2 * half), F32)] * 2,
            pltpu.SemaphoreType.DMA((2,)),
            pltpu.SemaphoreType.DMA((copies,)),
            pltpu.SemaphoreType.DMA((copies,)),
        ],
        compiler_params=pltpu.CompilerParams(collective_id=2, has_side_effects=True, vmem_limit_bytes=32 * MIB),
        name="middle",
    )(partial, features, own_far, cotangent, cot_far, w_self, w_neigh, w_self_far, w_neigh_far, bias, bias_far)


def final_kernel(
    back, weight_sum,
    sums, weights, bias_total,
    got_core, sent_row, kept, got_row, sent_pair, got_pair, w_sent, w_got,
    send_sems, recv_sems,
):
    row, col, edge, core, side = place()
    rows = lax.axis_size("row")
    x, z = lax.rem(row, 4), lax.div(row, 4)
    twin, pair = {"edge": edge + 1 - 2 * core}, {"edge": lax.rem(edge + 2, 4)}
    up, down = {"row": lax.rem(row + 1, rows)}, {"row": lax.rem(row + rows - 1, rows)}
    x_peers = [{"row": z * 4 + lax.rem(x + j, 4)} for j in (1, 2, 3)]
    z_peers = [{"row": lax.rem(z + j, 4) * 4 + x} for j in (1, 2, 3)]
    e_peers = [{"edge": lax.rem(edge + j, 4)} for j in (1, 2, 3)]
    far_peers = [{"edge": lax.rem(edge + j, 4), "col": 1 - col} for j in range(4)]
    greet([up, down] + e_peers + far_peers + x_peers + z_peers)
    send = Sender(send_sems, recv_sems)
    blocks = back.shape[0] // 3
    share = blocks // 4

    def piece(part, at_side, on_core):
        return pl.ds(part * blocks + (2 * at_side + on_core) * share, share)

    order = [(0, 1 - side), (2, 1 - side), (0, side), (2, side), (1, 1 - side), (1, side)]
    to_twin = [
        send(back.at[piece(part, at, 1 - core)], got_core.at[i], twin) for i, (part, at) in enumerate(order)
    ]

    top = weights.shape[0]
    many, bias_at = top // 64, top // 16
    to_group = []
    for i, peer in enumerate(e_peers + far_peers):
        j, owner = (0, lax.rem(edge + 1 + i, 4)) if i < 3 else (1, lax.rem(edge + i - 3, 4))
        w_sent[i, :many] = weight_sum[j, pl.ds(pl.multiple_of(owner * many, 8), many), :]
        w_sent[i, many:] = weight_sum[j, bias_at:]
        to_group.append(send(w_sent.at[i], w_got.at[i], peer))

    def summed(i):
        to_twin[i].wait_recv()
        part, at = order[i]
        return back[piece(part, at, core)].astype(F32) + got_core[i].astype(F32)

    to_row = []
    for i in range(4):
        sent_row[i] = summed(i).astype(BF16)
        to_row.append(send(sent_row.at[i], got_row.at[i], down if i % 2 == 0 else up))

    for copy in to_group:
        copy.wait_recv()
    group_total = w_got[0]
    for i in range(1, 7):
        group_total += w_got[i]
    start = pl.multiple_of(z * (top // 4) + x * (top // 16) + edge * many, 8)
    weights[pl.ds(start, many), :] = weight_sum[0, pl.ds(pl.multiple_of(edge * many, 8), many), :] + group_total[:many]
    bias_total[...] = weight_sum[0, bias_at:] + group_total[many:]

    def gathered(start, many, peers):
        at = pl.ds(pl.multiple_of(start, 8), many)
        return [send(weights.at[at], weights.at[at], peer) for peer in peers]

    steps = gathered(start, many, e_peers)
    for i in range(2):
        kept[i] = summed(4 + i)
    for step in steps:
        step.wait_recv()
    steps = gathered(z * (top // 4) + x * (top // 16), top // 16, x_peers)
    for i in range(2):
        to_row[i].wait_recv()
    sent_pair[...] = (kept[0] + got_row[0].astype(F32) + got_row[1].astype(F32)).astype(BF16)
    to_pair = send(sent_pair, got_pair, pair)
    for step in steps:
        step.wait_recv()
    steps = gathered(z * (top // 4), top // 4, z_peers)
    for i in range(2, 4):
        to_row[i].wait_recv()
    kept[1] += got_row[2].astype(F32) + got_row[3].astype(F32)
    to_pair.wait_recv()
    sums[...] = kept[1] + got_pair[...].astype(F32)
    for step in steps:
        step.wait_recv()
    send.finish()


def finish(back, weight_sum):
    share, half, size = back.shape[0] // 12, back.shape[1], back.shape[2]
    unit = half // 16 + 16
    copies = 6 + 4 + 1 + 7 + 9
    piece = (share, half, size)
    return pl.pallas_call(
        final_kernel,
        out_shape=[
            pltpu.VMEM(piece, F32),
            pltpu.VMEM((4 * half, half), F32),
            pltpu.VMEM((16, half), F32),
        ],
        in_specs=[VMEM] * 2,
        out_specs=[VMEM] * 3,
        scratch_shapes=[
            pltpu.VMEM((6,) + piece, BF16),
            pltpu.VMEM((4,) + piece, BF16),
            pltpu.VMEM((2,) + piece, F32),
            pltpu.VMEM((4,) + piece, BF16),
            pltpu.VMEM(piece, BF16),
            pltpu.VMEM(piece, BF16),
            *[pltpu.VMEM((7, unit, half), F32)] * 2,
            pltpu.SemaphoreType.DMA((copies,)),
            pltpu.SemaphoreType.DMA((copies,)),
        ],
        compiler_params=pltpu.CompilerParams(collective_id=3, has_side_effects=True, vmem_limit_bytes=32 * MIB),
        name="finish",
    )(back, weight_sum)


def writing_kernel(
    scale, out_near, self_near, far, sums, weights, bias_total,
    output, features_grad, w_self_grad, w_neigh_grad, bias_grad,
):
    col = lax.axis_index("col")
    rows, half = out_near.shape
    near, away = pl.multiple_of(col * rows, 16), pl.multiple_of((1 - col) * rows, 16)
    output[pl.ds(near, rows), :] = out_near[...]
    output[pl.ds(away, rows), :] = far[:rows]
    features_grad[pl.ds(near, rows), :] = self_near[...]
    features_grad[pl.ds(away, rows), :] = far[rows:].astype(F32)
    share, _, size = sums.shape
    for b in range(share):
        features_grad[b * size : (b + 1) * size, :] += sums[b].T
    top = weights.shape[0]
    w_self_grad[...] = weights[: top // 2] * scale
    w_neigh_grad[...] = weights[top // 2 :] * scale
    bias_grad[...] = jnp.sum(bias_total[...], axis=0, keepdims=True) * scale


def written(scale, out_near, self_near, far, sums, weights, bias_total):
    rows, half = out_near.shape
    top = weights.shape[0]
    return pl.pallas_call(
        functools.partial(writing_kernel, scale),
        out_shape=[
            jax.ShapeDtypeStruct((2 * rows, half), BF16),
            jax.ShapeDtypeStruct((2 * rows, half), F32),
            jax.ShapeDtypeStruct((top // 2, half), F32),
            jax.ShapeDtypeStruct((top // 2, half), F32),
            jax.ShapeDtypeStruct((1, half), F32),
        ],
        in_specs=[VMEM] * 6,
        out_specs=[VMEM] * 5,
        compiler_params=pltpu.CompilerParams(vmem_limit_bytes=4 * MIB),
        name="written",
    )(out_near, self_near, far, sums, weights, bias_total)


def local(features, tiles, tile_rows, tile_cols, tile_count, w_self, w_neigh, bias, cotangent):
    rows_dev, half = features.shape
    size = tiles.shape[1]
    blocks = rows_dev // size
    nodes = rows_dev * lax.axis_size("row")
    scale = 1.0 / math.sqrt(nodes)

    own = features.reshape(blocks, size, half)
    cot = cotangent.reshape(-1, size, half)
    bias_row = bias.reshape(1, half)
    own, cot, w_self, w_neigh, bias_row = (
        pltpu.with_memory_space_constraint(array, pltpu.HBM) for array in (own, cot, w_self, w_neigh, bias_row)
    )
    window, own_far, cot_far, w_self_far, w_neigh_far, bias_far = exchange_inputs(
        own, cot, w_self, w_neigh, bias_row
    )
    partial = tile_sum(forward_kernel, blocks, tile_rows, tile_cols, tile_count, window, tiles)
    grads, out_near, self_near, weight_sum, far = middle(
        partial, own, own_far, cot, cot_far, w_self, w_neigh, w_self_far, w_neigh_far, bias_row, bias_far
    )
    far = lax.ppermute(far, "col", [(0, 1), (1, 0)])
    back = tile_sum(backward_kernel, 3 * blocks, tile_rows, tile_cols, tile_count, grads, tiles)
    sums, weights, bias_total = finish(back, weight_sum)
    output, features_grad, w_self_grad, w_neigh_grad, bias_grad = written(
        scale, out_near, self_near, far, sums, weights, bias_total
    )
    return (output, features_grad, w_self_grad, w_neigh_grad, bias_grad.reshape(half))


def solution(mesh):
    return jax.shard_map(
        local,
        mesh=mesh,
        in_specs=(
            P("row", "col"),
            P(("row", "edge"), None, None),
            P(("row", "edge")),
            P(("row", "edge")),
            P(("row", "edge")),
            P(None, "col"),
            P(None, "col"),
            P("col"),
            P(("row", "edge"), "col"),
        ),
        out_specs=(
            P(("row", "edge"), "col"),
            P(("row", "edge"), "col"),
            P(None, "col"),
            P(None, "col"),
            P("col"),
        ),
        check_vma=False,
    )
```

```python
import functools
import math

import jax
import jax.numpy as jnp
from jax import lax
from jax.experimental import pallas as pl
from jax.experimental.pallas import tpu as pltpu
from jax.sharding import PartitionSpec as P

F32 = jnp.float32
BF16 = jnp.bfloat16
UNROLL = 88
LAG = 4
MIB = 1024 * 1024


MESH = pl.DeviceIdType.MESH


def place():
    row, col, edge = (lax.axis_index(name) for name in ("row", "col", "edge"))
    return row, col, edge, lax.rem(edge, 2), lax.div(edge, 2)


def greet(peers):
    barrier = pltpu.get_barrier_semaphore()
    for peer in peers:
        pl.semaphore_signal(barrier, inc=1, device_id=peer, device_id_type=MESH)
    pl.semaphore_wait(barrier, len(peers))


class Sender:
    def __init__(self, send_sems, recv_sems):
        self.send_sems, self.recv_sems, self.used = send_sems, recv_sems, []

    def __call__(self, src, dst, peer):
        index = len(self.used)
        copy = pltpu.make_async_remote_copy(
            src_ref=src,
            dst_ref=dst,
            send_sem=self.send_sems.at[index],
            recv_sem=self.recv_sems.at[index],
            device_id=peer,
            device_id_type=MESH,
        )
        copy.start()
        self.used.append(copy)
        return copy

    def finish(self):
        for copy in self.used:
            copy.wait_send()


def add_tiles(count, tiles, held, sems, total, product, target):
    spare = total.shape[0] - 1
    groups = lax.div(count + UNROLL - 1, UNROLL)

    def fetch(g):
        at = pl.ds(g * UNROLL, UNROLL)
        return pltpu.make_async_copy(tiles.at[at], held.at[at], sems.at[g])

    def start_step(g, carry):
        fetch(g).start()
        return carry

    lax.fori_loop(0, groups, start_step, 0)
    total[...] = jnp.zeros_like(total)

    def group_step(g, carry):
        fetch(g).wait()
        start = g * UNROLL
        waiting = {}
        for u in range(UNROLL + LAG):
            if u < UNROLL:
                waiting[u] = product(start + u, held[start + u])
            if u >= LAG:
                slot = start + u - LAG
                total[jnp.where(slot < count, target(slot), spare)] += waiting.pop(u - LAG)
        return carry

    lax.fori_loop(0, groups, group_step, 0)


def forward_kernel(rows, cols, count_ref, window, tiles, out, held, total, sems):
    add_tiles(
        count_ref[0], tiles, held, sems, total,
        lambda slot, tile: jnp.dot(tile, window[cols[slot]], preferred_element_type=F32),
        lambda slot: rows[slot],
    )
    out[...] = total[: out.shape[0]].astype(BF16)


def backward_kernel(rows, cols, count_ref, grads, tiles, out, held, total, sems):
    add_tiles(
        count_ref[0], tiles, held, sems, total,
        lambda slot, tile: jnp.dot(grads[rows[slot]], tile, preferred_element_type=F32),
        lambda slot: cols[slot],
    )
    out[...] = total[: out.shape[0]].astype(BF16)


SMEM = pl.BlockSpec(memory_space=pltpu.SMEM)
VMEM = pl.BlockSpec(memory_space=pltpu.VMEM)
HBM = pl.BlockSpec(memory_space=pltpu.HBM)


def tile_sum(kernel, blocks, tile_rows, tile_cols, tile_count, source, tiles):
    slots, size, _ = tiles.shape
    return pl.pallas_call(
        kernel,
        out_shape=pltpu.VMEM((blocks, size, size), BF16),
        in_specs=[SMEM] * 3 + [VMEM, HBM],
        out_specs=VMEM,
        scratch_shapes=[
            pltpu.VMEM(tiles.shape, BF16),
            pltpu.VMEM((blocks + 1, size, size), F32),
            pltpu.SemaphoreType.DMA((slots // UNROLL,)),
        ],
        compiler_params=pltpu.CompilerParams(vmem_limit_bytes=32 * MIB),
        cost_estimate=pl.CostEstimate(flops=2 * slots * size**3, bytes_accessed=slots * 2 * size**2, transcendentals=0),
        name=kernel.__name__.replace("kernel", "sum"),
    )(tile_rows, tile_cols, tile_count, source, tiles)


HALO_CHUNKS = 4


def halo_kernel(
    features, cotangent, w_self, w_neigh, bias,
    window, own_far, cot_far, w_self_far, w_neigh_far, bias_far,
    load_sem, send_sems, recv_sems,
):
    row, col, edge, core, _ = place()
    rows = lax.axis_size("row")
    up, down = {"row": lax.rem(row + 1, rows)}, {"row": lax.rem(row + rows - 1, rows)}
    twin, partner = {"edge": edge + 1 - 2 * core}, {"col": 1 - col}
    blocks = features.shape[0]
    share = blocks // 8
    greet([up, down, twin, partner])
    send = Sender(send_sems, recv_sems)
    step = blocks // 2 // HALO_CHUNKS
    parts = [pl.ds(core * (blocks // 2) + i * step, step) for i in range(HALO_CHUNKS)]
    arriving = []
    for part in parts:
        for side, peer in ((0, up), (2, down)):
            landing = pl.ds(side * blocks + core * (blocks // 2) + (len(arriving) // 2) * step, step)
            arriving.append((landing, send(features.at[part], window.at[landing], peer)))
    theirs = pl.ds(edge * 2 * share + (1 - col) * share, share)
    theirs_cot = pl.ds((1 - col) * share, share)
    swaps = [
        send(features.at[theirs], own_far, partner),
        send(cotangent.at[theirs_cot], cot_far, partner),
        send(w_self, w_self_far, partner),
        send(w_neigh, w_neigh_far, partner),
        send(bias, bias_far, partner),
    ]
    load = pltpu.make_async_copy(features, window.at[pl.ds(blocks, blocks)], load_sem)
    load.start()
    handed = []
    for landing, copy in arriving:
        copy.wait_recv()
        handed.append(send(window.at[landing], window.at[landing], twin))
    for copy in swaps + handed:
        copy.wait_recv()
    load.wait()
    send.finish()


def exchange_inputs(features, cotangent, w_self, w_neigh, bias):
    blocks, size, half = features.shape
    share = blocks // 8
    shapes = [
        jax.ShapeDtypeStruct((3 * blocks, size, half), BF16),
        jax.ShapeDtypeStruct((share, size, half), BF16),
        jax.ShapeDtypeStruct((share, size, half), BF16),
        w_self, w_neigh, bias,
    ]
    copies = 4 * HALO_CHUNKS + 5
    return pl.pallas_call(
        halo_kernel,
        out_shape=[pltpu.VMEM(s.shape, s.dtype) for s in shapes],
        in_specs=[HBM] * 5,
        out_specs=[VMEM] * 6,
        scratch_shapes=[
            pltpu.SemaphoreType.DMA,
            pltpu.SemaphoreType.DMA((copies,)),
            pltpu.SemaphoreType.DMA((copies,)),
        ],
        compiler_params=pltpu.CompilerParams(collective_id=1, has_side_effects=True, vmem_limit_bytes=32 * MIB),
        name="exchange_inputs",
    )(features, cotangent, w_self, w_neigh, bias)


def mid_kernel(
    partial, features, own_far, cotangent, cot_far, w_self, w_neigh, w_self_far, w_neigh_far, bias, bias_far,
    grads, out_near, self_near, weight_sum, far,
    got_core, sent, got, own, cot, weights, sent_grads,
    w_all, w_bias, w_sent_z, w_got_z, w_got_x,
    local_sems, send_sems, recv_sems,
):
    row, col, edge, core, pair_side = place()
    other = 1 - col
    twin, pair, partner = {"edge": edge + 1 - 2 * core}, {"edge": lax.rem(edge + 2, 4)}, {"col": other}
    diagonal = {"edge": lax.rem(edge + 2, 4), "col": other}
    x, z = lax.rem(row, 4), lax.div(row, 4)
    along_z = [lax.rem(z + j, 4) for j in (1, 2, 3)]
    x_peers = [{"row": z * 4 + lax.rem(x + j, 4)} for j in (1, 2, 3)]
    z_peers = [{"row": to * 4 + x} for to in along_z]
    blocks, size, half = partial.shape
    share = blocks // 8
    near_rows = own_far.shape[0] * size
    local = [
        pltpu.make_async_copy(features.at[pl.ds(edge * 2 * share + col * share, share)], own, local_sems.at[0]),
        pltpu.make_async_copy(cotangent.at[pl.ds(col * share, share)], cot, local_sems.at[1]),
    ]
    for copy in local:
        copy.start()
    greet([twin, pair, partner, diagonal] + x_peers + z_peers)
    send = Sender(send_sems, recv_sems)

    def piece(side, on_core, column):
        return pl.ds((2 * side + on_core) * 2 * share + column * share, share)

    order = [(pair_side, other), (1 - pair_side, other), (1 - pair_side, col), (pair_side, col)]
    to_twin = [
        send(partial.at[piece(side, 1 - core, column)], got_core.at[i], twin)
        for i, (side, column) in enumerate(order)
    ]
    near_w, far_w = pl.ds(pl.multiple_of(col * half, half), half), pl.ds(pl.multiple_of(other * half, half), half)
    for k, (near, away) in enumerate(((w_self, w_self_far), (w_neigh, w_neigh_far))):
        for j, rows in enumerate((near_w, far_w)):
            at = pl.ds((2 * k + j) * half, half)
            weights[at, :half] = near[rows, :]
            weights[at, half:] = away[rows, :]

    def summed(i):
        to_twin[i].wait_recv()
        side, column = order[i]
        return partial[piece(side, core, column)].astype(F32) + got_core[i].astype(F32)

    crossing = []
    for i, owner in enumerate((partner, diagonal, pair)):
        sent[i] = summed(i).astype(BF16)
        crossing.append(send(sent.at[i], got.at[i], owner))
    kept = summed(3)
    for copy in local:
        copy.wait()
    for copy in crossing:
        copy.wait_recv()
    agg_near = (kept + got[2].astype(F32)).astype(BF16)
    agg_far = (got[0].astype(F32) + got[1].astype(F32)).astype(BF16)

    def flat(blocks_of):
        return blocks_of.reshape(near_rows, half)

    mixed = jnp.concatenate(
        [flat(own[...]), flat(own_far[...]), flat(agg_near), flat(agg_far)], axis=1
    )
    pre = jnp.dot(mixed, weights[...], preferred_element_type=F32) + jnp.concatenate(
        [bias[...], bias_far[...]], axis=1
    )
    sigm = jax.nn.sigmoid(pre)
    cot_full = jnp.concatenate([flat(cot[...]), flat(cot_far[...])], axis=1).astype(F32)
    grad_pre = cot_full * sigm * (1.0 + pre * (1.0 - sigm))
    grad_low = grad_pre.astype(BF16)
    over_cols = (((1,), (1,)), ((), ()))
    agg_back = lax.dot_general(
        weights[2 * half :, :], grad_low, over_cols, preferred_element_type=F32
    ).astype(BF16)
    mine = pl.ds(edge * 2 * share + col * share, share)
    for b in range(share):
        grads[edge * 2 * share + col * share + b] = agg_back[:half, b * size : (b + 1) * size]
        sent_grads[b] = agg_back[half:, b * size : (b + 1) * size]
    crossing = [
        send(sent_grads, grads.at[mine], diagonal),
        send(sent_grads, grads.at[mine], partner),
        send(grads.at[mine], grads.at[mine], pair),
    ]
    handed = [send(grads.at[mine], grads.at[mine], twin)]

    parts = lax.dot_general(mixed, grad_low, (((0,), (0,)), ((), ())), preferred_element_type=F32)
    for k in range(2):
        for j, start in enumerate((col * half, other * half)):
            at = (2 * k + j) * half
            w_all[pl.ds(pl.multiple_of(2 * k * half + start, half), half), :] = parts[at : at + half, :]
    w_bias[...] = jnp.sum(grad_pre.reshape(near_rows // 16, 16, 2 * half), axis=0)

    z_many = 4 * half // 4
    z_start = pl.multiple_of(z * z_many, 8)
    steps = []
    for j in range(3):
        w_sent_z[j, :z_many] = w_all[pl.ds(pl.multiple_of(along_z[j] * z_many, 8), z_many), :].astype(BF16)
        w_sent_z[j, z_many:] = w_bias[...].astype(BF16)
        steps.append(send(w_sent_z.at[j], w_got_z.at[z], z_peers[j]))
    w_got_z[z, z_many:] = w_bias[...].astype(BF16)

    output = (pre * sigm).astype(BF16)
    out_near[...] = output[:, :half]
    far[:near_rows] = output[:, half:]
    self_back = lax.dot_general(grad_low, weights[: 2 * half, :], over_cols, preferred_element_type=F32)
    self_near[...] = self_back[:, :half]
    far[near_rows:] = self_back[:, half:].astype(BF16)

    for step in steps:
        step.wait_recv()
    quarter = w_all[pl.ds(z_start, z_many), :]
    for j in range(3):
        quarter += w_got_z[along_z[j], :z_many].astype(F32)
    bias_sum = w_got_z[0, z_many:].astype(F32)
    for j in range(1, 4):
        bias_sum += w_got_z[j, z_many:].astype(F32)
    w_got_x[x, :z_many] = quarter.astype(BF16)
    w_got_x[x, z_many:] = bias_sum.astype(BF16)
    steps = [send(w_got_x.at[x], w_got_x.at[x], peer) for peer in x_peers]

    far_edge = lax.rem(edge + 2, 4)
    homes = [
        pl.ds(far_edge * 2 * share + other * share, share),
        pl.ds(edge * 2 * share + other * share, share),
        pl.ds(far_edge * 2 * share + col * share, share),
    ]
    for k in (1, 2, 0):
        crossing[k].wait_recv()
        handed.append(send(grads.at[homes[k]], grads.at[homes[k]], twin))
    for step in steps:
        step.wait_recv()
    x_total = w_got_x[0].astype(F32)
    for j in range(1, 4):
        x_total += w_got_x[j].astype(F32)
    for j in range(2):
        weight_sum[j] = x_total[:, j * half : (j + 1) * half]
    for copy in handed:
        copy.wait_recv()
    send.finish()


def middle(partial, features, own_far, cotangent, cot_far, w_self, w_neigh, w_self_far, w_neigh_far, bias, bias_far):
    blocks, size, half = partial.shape
    share = blocks // 8
    rows = share * size
    copies = 4 + 3 + 3 + 4 + 6
    top = 4 * half
    piece = (share, size, half)
    return pl.pallas_call(
        mid_kernel,
        out_shape=[
            pltpu.VMEM((blocks, half, size), BF16),
            pltpu.VMEM((rows, half), BF16),
            pltpu.VMEM((rows, half), F32),
            pltpu.VMEM((2, top // 4 + 16, half), F32),
            jax.ShapeDtypeStruct((2 * rows, half), BF16),
        ],
        in_specs=[VMEM, HBM, VMEM, HBM] + [VMEM] * 7,
        out_specs=[VMEM] * 5,
        scratch_shapes=[
            pltpu.VMEM((4,) + piece, BF16),
            pltpu.VMEM((3,) + piece, BF16),
            pltpu.VMEM((3,) + piece, BF16),
            pltpu.VMEM(piece, BF16),
            pltpu.VMEM(piece, BF16),
            pltpu.VMEM((4 * half, 2 * half), BF16),
            pltpu.VMEM((share, half, size), BF16),
            pltpu.VMEM((top, 2 * half), F32),
            pltpu.VMEM((16, 2 * half), F32),
            pltpu.VMEM((3, top // 4 + 16, 2 * half), BF16),
            pltpu.VMEM((4, top // 4 + 16, 2 * half), BF16),
            pltpu.VMEM((4, top // 4 + 16, 2 * half), BF16),
            pltpu.SemaphoreType.DMA((2,)),
            pltpu.SemaphoreType.DMA((copies,)),
            pltpu.SemaphoreType.DMA((copies,)),
        ],
        compiler_params=pltpu.CompilerParams(collective_id=2, has_side_effects=True, vmem_limit_bytes=32 * MIB),
        name="middle",
    )(partial, features, own_far, cotangent, cot_far, w_self, w_neigh, w_self_far, w_neigh_far, bias, bias_far)


def final_kernel(
    back, weight_sum,
    sums, weights, bias_total,
    got_core, sent_row, kept, got_row, sent_pair, got_pair, w_sent, w_got,
    send_sems, recv_sems,
):
    row, col, edge, core, side = place()
    rows = lax.axis_size("row")
    x, z = lax.rem(row, 4), lax.div(row, 4)
    twin, pair = {"edge": edge + 1 - 2 * core}, {"edge": lax.rem(edge + 2, 4)}
    up, down = {"row": lax.rem(row + 1, rows)}, {"row": lax.rem(row + rows - 1, rows)}
    z_peers = [{"row": lax.rem(z + j, 4) * 4 + x} for j in (1, 2, 3)]
    e_peers = [{"edge": lax.rem(edge + j, 4)} for j in (1, 2, 3)]
    far_peers = [{"edge": lax.rem(edge + j, 4), "col": 1 - col} for j in range(4)]
    greet([up, down] + e_peers + far_peers + z_peers)
    send = Sender(send_sems, recv_sems)
    blocks = back.shape[0] // 3
    share = blocks // 4

    def piece(part, at_side, on_core):
        return pl.ds(part * blocks + (2 * at_side + on_core) * share, share)

    order = [(0, 1 - side), (2, 1 - side), (0, side), (2, side), (1, 1 - side), (1, side)]
    to_twin = [
        send(back.at[piece(part, at, 1 - core)], got_core.at[i], twin) for i, (part, at) in enumerate(order)
    ]

    def summed(i):
        to_twin[i].wait_recv()
        part, at = order[i]
        return back[piece(part, at, core)].astype(F32) + got_core[i].astype(F32)

    to_row = []
    for i in range(4):
        sent_row[i] = summed(i).astype(BF16)
        to_row.append(send(sent_row.at[i], got_row.at[i], down if i % 2 == 0 else up))

    top = weights.shape[0]
    many, bias_at = top // 16, top // 4
    to_group = []
    for i, peer in enumerate(e_peers + far_peers):
        j, owner = (0, lax.rem(edge + 1 + i, 4)) if i < 3 else (1, lax.rem(edge + i - 3, 4))
        w_sent[i, :many] = weight_sum[j, pl.ds(pl.multiple_of(owner * many, 8), many), :]
        w_sent[i, many:] = weight_sum[j, bias_at:]
        to_group.append(send(w_sent.at[i], w_got.at[i], peer))

    for copy in to_group:
        copy.wait_recv()
    group_total = w_got[0]
    for i in range(1, 7):
        group_total += w_got[i]
    start = pl.multiple_of(z * (top // 4) + edge * many, 8)
    weights[pl.ds(start, many), :] = weight_sum[0, pl.ds(pl.multiple_of(edge * many, 8), many), :] + group_total[:many]
    bias_total[...] = weight_sum[0, bias_at:] + group_total[many:]

    def gathered(start, many, peers):
        at = pl.ds(pl.multiple_of(start, 8), many)
        return [send(weights.at[at], weights.at[at], peer) for peer in peers]

    steps = gathered(start, many, e_peers)
    for i in range(2):
        kept[i] = summed(4 + i)
    for step in steps:
        step.wait_recv()
    steps = gathered(z * (top // 4), top // 4, z_peers)
    for i in range(2):
        to_row[i].wait_recv()
    sent_pair[...] = (kept[0] + got_row[0].astype(F32) + got_row[1].astype(F32)).astype(BF16)
    to_pair = send(sent_pair, got_pair, pair)
    for i in range(2, 4):
        to_row[i].wait_recv()
    kept[1] += got_row[2].astype(F32) + got_row[3].astype(F32)
    to_pair.wait_recv()
    sums[...] = kept[1] + got_pair[...].astype(F32)
    for step in steps:
        step.wait_recv()
    send.finish()


def finish(back, weight_sum):
    share, half, size = back.shape[0] // 12, back.shape[1], back.shape[2]
    unit = half // 4 + 16
    copies = 6 + 4 + 1 + 7 + 6
    piece = (share, half, size)
    return pl.pallas_call(
        final_kernel,
        out_shape=[
            pltpu.VMEM(piece, F32),
            pltpu.VMEM((4 * half, half), F32),
            pltpu.VMEM((16, half), F32),
        ],
        in_specs=[VMEM] * 2,
        out_specs=[VMEM] * 3,
        scratch_shapes=[
            pltpu.VMEM((6,) + piece, BF16),
            pltpu.VMEM((4,) + piece, BF16),
            pltpu.VMEM((2,) + piece, F32),
            pltpu.VMEM((4,) + piece, BF16),
            pltpu.VMEM(piece, BF16),
            pltpu.VMEM(piece, BF16),
            *[pltpu.VMEM((7, unit, half), F32)] * 2,
            pltpu.SemaphoreType.DMA((copies,)),
            pltpu.SemaphoreType.DMA((copies,)),
        ],
        compiler_params=pltpu.CompilerParams(collective_id=3, has_side_effects=True, vmem_limit_bytes=32 * MIB),
        name="finish",
    )(back, weight_sum)


def writing_kernel(
    scale, out_near, self_near, far, sums, weights, bias_total,
    output, features_grad, w_self_grad, w_neigh_grad, bias_grad,
):
    col = lax.axis_index("col")
    rows, half = out_near.shape
    near, away = pl.multiple_of(col * rows, 16), pl.multiple_of((1 - col) * rows, 16)
    output[pl.ds(near, rows), :] = out_near[...]
    output[pl.ds(away, rows), :] = far[:rows]
    features_grad[pl.ds(near, rows), :] = self_near[...]
    features_grad[pl.ds(away, rows), :] = far[rows:].astype(F32)
    share, _, size = sums.shape
    for b in range(share):
        features_grad[b * size : (b + 1) * size, :] += sums[b].T
    top = weights.shape[0]
    w_self_grad[...] = weights[: top // 2] * scale
    w_neigh_grad[...] = weights[top // 2 :] * scale
    bias_grad[...] = jnp.sum(bias_total[...], axis=0, keepdims=True) * scale


def written(scale, out_near, self_near, far, sums, weights, bias_total):
    rows, half = out_near.shape
    top = weights.shape[0]
    return pl.pallas_call(
        functools.partial(writing_kernel, scale),
        out_shape=[
            jax.ShapeDtypeStruct((2 * rows, half), BF16),
            jax.ShapeDtypeStruct((2 * rows, half), F32),
            jax.ShapeDtypeStruct((top // 2, half), F32),
            jax.ShapeDtypeStruct((top // 2, half), F32),
            jax.ShapeDtypeStruct((1, half), F32),
        ],
        in_specs=[VMEM] * 6,
        out_specs=[VMEM] * 5,
        compiler_params=pltpu.CompilerParams(vmem_limit_bytes=4 * MIB),
        name="written",
    )(out_near, self_near, far, sums, weights, bias_total)


def local(features, tiles, tile_rows, tile_cols, tile_count, w_self, w_neigh, bias, cotangent):
    rows_dev, half = features.shape
    size = tiles.shape[1]
    blocks = rows_dev // size
    nodes = rows_dev * lax.axis_size("row")
    scale = 1.0 / math.sqrt(nodes)

    own = features.reshape(blocks, size, half)
    cot = cotangent.reshape(-1, size, half)
    bias_row = bias.reshape(1, half)
    own, cot, w_self, w_neigh, bias_row, tile_rows, tile_cols = (
        pltpu.with_memory_space_constraint(array, pltpu.HBM)
        for array in (own, cot, w_self, w_neigh, bias_row, tile_rows, tile_cols)
    )
    window, own_far, cot_far, w_self_far, w_neigh_far, bias_far = exchange_inputs(
        own, cot, w_self, w_neigh, bias_row
    )
    partial = tile_sum(forward_kernel, blocks, tile_rows, tile_cols, tile_count, window, tiles)
    grads, out_near, self_near, weight_sum, far = middle(
        partial, own, own_far, cot, cot_far, w_self, w_neigh, w_self_far, w_neigh_far, bias_row, bias_far
    )
    far = lax.ppermute(far, "col", [(0, 1), (1, 0)])
    back = tile_sum(backward_kernel, 3 * blocks, tile_rows, tile_cols, tile_count, grads, tiles)
    sums, weights, bias_total = finish(back, weight_sum)
    output, features_grad, w_self_grad, w_neigh_grad, bias_grad = written(
        scale, out_near, self_near, far, sums, weights, bias_total
    )
    return (output, features_grad, w_self_grad, w_neigh_grad, bias_grad.reshape(half))


def solution(mesh):
    return jax.shard_map(
        local,
        mesh=mesh,
        in_specs=(
            P("row", "col"),
            P(("row", "edge"), None, None),
            P(("row", "edge")),
            P(("row", "edge")),
            P(("row", "edge")),
            P(None, "col"),
            P(None, "col"),
            P("col"),
            P(("row", "edge"), "col"),
        ),
        out_specs=(
            P(("row", "edge"), "col"),
            P(("row", "edge"), "col"),
            P(None, "col"),
            P(None, "col"),
            P("col"),
        ),
        check_vma=False,
    )
```

```python
import functools
import math

import jax
import jax.numpy as jnp
from jax import lax
from jax.experimental import pallas as pl
from jax.experimental.pallas import tpu as pltpu
from jax.sharding import PartitionSpec as P

F32 = jnp.float32
BF16 = jnp.bfloat16
UNROLL = 88
LAG = 4
MIB = 1024 * 1024


MESH = pl.DeviceIdType.MESH


def place():
    row, col, edge = (lax.axis_index(name) for name in ("row", "col", "edge"))
    return row, col, edge, lax.rem(edge, 2), lax.div(edge, 2)


def greet(peers):
    barrier = pltpu.get_barrier_semaphore()
    for peer in peers:
        pl.semaphore_signal(barrier, inc=1, device_id=peer, device_id_type=MESH)
    pl.semaphore_wait(barrier, len(peers))


class Sender:
    def __init__(self, send_sems, recv_sems):
        self.send_sems, self.recv_sems, self.used = send_sems, recv_sems, []

    def __call__(self, src, dst, peer):
        index = len(self.used)
        copy = pltpu.make_async_remote_copy(
            src_ref=src,
            dst_ref=dst,
            send_sem=self.send_sems.at[index],
            recv_sem=self.recv_sems.at[index],
            device_id=peer,
            device_id_type=MESH,
        )
        copy.start()
        self.used.append(copy)
        return copy

    def finish(self):
        for copy in self.used:
            copy.wait_send()


def add_tiles(count, head, tiles, held, sems, total, product, target):
    spare = total.shape[0] - 1
    groups = lax.div(count + UNROLL - 1, UNROLL)

    def fetch(g):
        at = pl.ds(g * UNROLL, UNROLL)
        return pltpu.make_async_copy(tiles.at[at], held.at[pl.ds((g - 1) * UNROLL, UNROLL)], sems.at[g - 1])

    def start_step(g, carry):
        fetch(g).start()
        return carry

    lax.fori_loop(1, groups, start_step, 0)
    total[...] = jnp.zeros_like(total)

    def add_group(source, first, start):
        waiting = {}
        for u in range(UNROLL + LAG):
            if u < UNROLL:
                waiting[u] = product(start + u, source[first + u])
            if u >= LAG:
                slot = start + u - LAG
                total[jnp.where(slot < count, target(slot), spare)] += waiting.pop(u - LAG)

    add_group(head, 0, 0)

    def group_step(g, carry):
        fetch(g).wait()
        add_group(held, (g - 1) * UNROLL, g * UNROLL)
        return carry

    lax.fori_loop(1, groups, group_step, 0)


def forward_kernel(rows, cols, count_ref, window, head, tiles, out, held, total, sems):
    add_tiles(
        count_ref[0], head, tiles, held, sems, total,
        lambda slot, tile: jnp.dot(tile, window[cols[slot]], preferred_element_type=F32),
        lambda slot: rows[slot],
    )
    out[...] = total[: out.shape[0]].astype(BF16)


def backward_kernel(rows, cols, count_ref, grads, head, tiles, out, held, total, sems):
    add_tiles(
        count_ref[0], head, tiles, held, sems, total,
        lambda slot, tile: jnp.dot(grads[rows[slot]], tile, preferred_element_type=F32),
        lambda slot: cols[slot],
    )
    out[...] = total[: out.shape[0]].astype(BF16)


SMEM = pl.BlockSpec(memory_space=pltpu.SMEM)
VMEM = pl.BlockSpec(memory_space=pltpu.VMEM)
HBM = pl.BlockSpec(memory_space=pltpu.HBM)


def tile_sum(kernel, blocks, tile_rows, tile_cols, tile_count, source, head, tiles):
    slots, size, _ = tiles.shape
    return pl.pallas_call(
        kernel,
        out_shape=pltpu.VMEM((blocks, size, size), BF16),
        in_specs=[SMEM] * 3 + [VMEM, VMEM, HBM],
        out_specs=VMEM,
        scratch_shapes=[
            pltpu.VMEM((slots - UNROLL, size, size), BF16),
            pltpu.VMEM((blocks + 1, size, size), F32),
            pltpu.SemaphoreType.DMA((slots // UNROLL - 1,)),
        ],
        compiler_params=pltpu.CompilerParams(vmem_limit_bytes=32 * MIB),
        cost_estimate=pl.CostEstimate(flops=2 * slots * size**3, bytes_accessed=slots * 2 * size**2, transcendentals=0),
        name=kernel.__name__.replace("kernel", "sum"),
    )(tile_rows, tile_cols, tile_count, source, head, tiles)


HALO_CHUNKS = 4


def halo_kernel(
    features, cotangent, w_self, w_neigh, bias, tiles,
    window, head, own_far, cot_far, w_self_far, w_neigh_far, bias_far,
    load_sems, send_sems, recv_sems,
):
    row, col, edge, core, _ = place()
    rows = lax.axis_size("row")
    up, down = {"row": lax.rem(row + 1, rows)}, {"row": lax.rem(row + rows - 1, rows)}
    twin, partner = {"edge": edge + 1 - 2 * core}, {"col": 1 - col}
    blocks = features.shape[0]
    share = blocks // 8
    greet([up, down, twin, partner])
    send = Sender(send_sems, recv_sems)
    step = blocks // 2 // HALO_CHUNKS
    parts = [pl.ds(core * (blocks // 2) + i * step, step) for i in range(HALO_CHUNKS)]
    arriving = []
    for part in parts:
        for side, peer in ((0, up), (2, down)):
            landing = pl.ds(side * blocks + core * (blocks // 2) + (len(arriving) // 2) * step, step)
            arriving.append((landing, send(features.at[part], window.at[landing], peer)))
    theirs = pl.ds(edge * 2 * share + (1 - col) * share, share)
    theirs_cot = pl.ds((1 - col) * share, share)
    swaps = [
        send(features.at[theirs], own_far, partner),
        send(cotangent.at[theirs_cot], cot_far, partner),
        send(w_self, w_self_far, partner),
        send(w_neigh, w_neigh_far, partner),
        send(bias, bias_far, partner),
    ]
    loads = [
        pltpu.make_async_copy(features, window.at[pl.ds(blocks, blocks)], load_sems.at[0]),
        pltpu.make_async_copy(tiles.at[pl.ds(0, UNROLL)], head, load_sems.at[1]),
    ]
    for load in loads:
        load.start()
    handed = []
    for landing, copy in arriving:
        copy.wait_recv()
        handed.append(send(window.at[landing], window.at[landing], twin))
    for copy in swaps + handed:
        copy.wait_recv()
    for load in loads:
        load.wait()
    send.finish()


def exchange_inputs(features, cotangent, w_self, w_neigh, bias, tiles):
    blocks, size, half = features.shape
    share = blocks // 8
    shapes = [
        jax.ShapeDtypeStruct((3 * blocks, size, half), BF16),
        jax.ShapeDtypeStruct((UNROLL,) + tiles.shape[1:], BF16),
        jax.ShapeDtypeStruct((share, size, half), BF16),
        jax.ShapeDtypeStruct((share, size, half), BF16),
        w_self, w_neigh, bias,
    ]
    copies = 4 * HALO_CHUNKS + 5
    return pl.pallas_call(
        halo_kernel,
        out_shape=[pltpu.VMEM(s.shape, s.dtype) for s in shapes],
        in_specs=[HBM] * 6,
        out_specs=[VMEM] * 7,
        scratch_shapes=[
            pltpu.SemaphoreType.DMA((2,)),
            pltpu.SemaphoreType.DMA((copies,)),
            pltpu.SemaphoreType.DMA((copies,)),
        ],
        compiler_params=pltpu.CompilerParams(collective_id=1, has_side_effects=True, vmem_limit_bytes=32 * MIB),
        name="exchange_inputs",
    )(features, cotangent, w_self, w_neigh, bias, tiles)


def mid_kernel(
    partial, features, own_far, cotangent, cot_far, w_self, w_neigh, w_self_far, w_neigh_far, bias, bias_far, tiles,
    grads, out_near, self_near, weight_sum, far, head,
    got_core, sent, got, own, cot, weights, sent_grads,
    w_all, w_bias, w_sent_z, w_got_z, w_got_x,
    local_sems, send_sems, recv_sems,
):
    row, col, edge, core, pair_side = place()
    other = 1 - col
    twin, pair, partner = {"edge": edge + 1 - 2 * core}, {"edge": lax.rem(edge + 2, 4)}, {"col": other}
    diagonal = {"edge": lax.rem(edge + 2, 4), "col": other}
    x, z = lax.rem(row, 4), lax.div(row, 4)
    along_z = [lax.rem(z + j, 4) for j in (1, 2, 3)]
    x_peers = [{"row": z * 4 + lax.rem(x + j, 4)} for j in (1, 2, 3)]
    z_peers = [{"row": to * 4 + x} for to in along_z]
    blocks, size, half = partial.shape
    share = blocks // 8
    near_rows = own_far.shape[0] * size
    local = [
        pltpu.make_async_copy(features.at[pl.ds(edge * 2 * share + col * share, share)], own, local_sems.at[0]),
        pltpu.make_async_copy(cotangent.at[pl.ds(col * share, share)], cot, local_sems.at[1]),
    ]
    ahead = pltpu.make_async_copy(tiles.at[pl.ds(0, UNROLL)], head, local_sems.at[2])
    for copy in local:
        copy.start()
    ahead.start()
    greet([twin, pair, partner, diagonal] + x_peers + z_peers)
    send = Sender(send_sems, recv_sems)

    def piece(side, on_core, column):
        return pl.ds((2 * side + on_core) * 2 * share + column * share, share)

    order = [(pair_side, other), (1 - pair_side, other), (1 - pair_side, col), (pair_side, col)]
    to_twin = [
        send(partial.at[piece(side, 1 - core, column)], got_core.at[i], twin)
        for i, (side, column) in enumerate(order)
    ]
    near_w, far_w = pl.ds(pl.multiple_of(col * half, half), half), pl.ds(pl.multiple_of(other * half, half), half)
    for k, (near, away) in enumerate(((w_self, w_self_far), (w_neigh, w_neigh_far))):
        for j, rows in enumerate((near_w, far_w)):
            at = pl.ds((2 * k + j) * half, half)
            weights[at, :half] = near[rows, :]
            weights[at, half:] = away[rows, :]

    def summed(i):
        to_twin[i].wait_recv()
        side, column = order[i]
        return partial[piece(side, core, column)].astype(F32) + got_core[i].astype(F32)

    crossing = []
    for i, owner in enumerate((partner, diagonal, pair)):
        sent[i] = summed(i).astype(BF16)
        crossing.append(send(sent.at[i], got.at[i], owner))
    kept = summed(3)
    for copy in local:
        copy.wait()
    for copy in crossing:
        copy.wait_recv()
    agg_near = (kept + got[2].astype(F32)).astype(BF16)
    agg_far = (got[0].astype(F32) + got[1].astype(F32)).astype(BF16)

    def flat(blocks_of):
        return blocks_of.reshape(near_rows, half)

    mixed = jnp.concatenate(
        [flat(own[...]), flat(own_far[...]), flat(agg_near), flat(agg_far)], axis=1
    )
    pre = jnp.dot(mixed, weights[...], preferred_element_type=F32) + jnp.concatenate(
        [bias[...], bias_far[...]], axis=1
    )
    sigm = jax.nn.sigmoid(pre)
    cot_full = jnp.concatenate([flat(cot[...]), flat(cot_far[...])], axis=1).astype(F32)
    grad_pre = cot_full * sigm * (1.0 + pre * (1.0 - sigm))
    grad_low = grad_pre.astype(BF16)
    over_cols = (((1,), (1,)), ((), ()))
    agg_back = lax.dot_general(
        weights[2 * half :, :], grad_low, over_cols, preferred_element_type=F32
    ).astype(BF16)
    mine = pl.ds(edge * 2 * share + col * share, share)
    for b in range(share):
        grads[edge * 2 * share + col * share + b] = agg_back[:half, b * size : (b + 1) * size]
        sent_grads[b] = agg_back[half:, b * size : (b + 1) * size]
    crossing = [
        send(sent_grads, grads.at[mine], diagonal),
        send(sent_grads, grads.at[mine], partner),
        send(grads.at[mine], grads.at[mine], pair),
    ]
    handed = [send(grads.at[mine], grads.at[mine], twin)]

    parts = lax.dot_general(mixed, grad_low, (((0,), (0,)), ((), ())), preferred_element_type=F32)
    for k in range(2):
        for j, start in enumerate((col * half, other * half)):
            at = (2 * k + j) * half
            w_all[pl.ds(pl.multiple_of(2 * k * half + start, half), half), :] = parts[at : at + half, :]
    w_bias[...] = jnp.sum(grad_pre.reshape(near_rows // 16, 16, 2 * half), axis=0)

    z_many = 4 * half // 4
    z_start = pl.multiple_of(z * z_many, 8)
    steps = []
    for j in range(3):
        w_sent_z[j, :z_many] = w_all[pl.ds(pl.multiple_of(along_z[j] * z_many, 8), z_many), :].astype(BF16)
        w_sent_z[j, z_many:] = w_bias[...].astype(BF16)
        steps.append(send(w_sent_z.at[j], w_got_z.at[z], z_peers[j]))
    w_got_z[z, z_many:] = w_bias[...].astype(BF16)

    output = (pre * sigm).astype(BF16)
    out_near[...] = output[:, :half]
    far[:near_rows] = output[:, half:]
    self_back = lax.dot_general(grad_low, weights[: 2 * half, :], over_cols, preferred_element_type=F32)
    self_near[...] = self_back[:, :half]
    far[near_rows:] = self_back[:, half:].astype(BF16)

    for step in steps:
        step.wait_recv()
    quarter = w_all[pl.ds(z_start, z_many), :]
    for j in range(3):
        quarter += w_got_z[along_z[j], :z_many].astype(F32)
    bias_sum = w_got_z[0, z_many:].astype(F32)
    for j in range(1, 4):
        bias_sum += w_got_z[j, z_many:].astype(F32)
    w_got_x[x, :z_many] = quarter.astype(BF16)
    w_got_x[x, z_many:] = bias_sum.astype(BF16)
    steps = [send(w_got_x.at[x], w_got_x.at[x], peer) for peer in x_peers]

    far_edge = lax.rem(edge + 2, 4)
    homes = [
        pl.ds(far_edge * 2 * share + other * share, share),
        pl.ds(edge * 2 * share + other * share, share),
        pl.ds(far_edge * 2 * share + col * share, share),
    ]
    for k in (1, 2, 0):
        crossing[k].wait_recv()
        handed.append(send(grads.at[homes[k]], grads.at[homes[k]], twin))
    for step in steps:
        step.wait_recv()
    x_total = w_got_x[0].astype(F32)
    for j in range(1, 4):
        x_total += w_got_x[j].astype(F32)
    for j in range(2):
        weight_sum[j] = x_total[:, j * half : (j + 1) * half]
    for copy in handed:
        copy.wait_recv()
    ahead.wait()
    send.finish()


def middle(partial, features, own_far, cotangent, cot_far, w_self, w_neigh, w_self_far, w_neigh_far, bias, bias_far, tiles):
    blocks, size, half = partial.shape
    share = blocks // 8
    rows = share * size
    copies = 4 + 3 + 3 + 4 + 6
    top = 4 * half
    piece = (share, size, half)
    return pl.pallas_call(
        mid_kernel,
        out_shape=[
            pltpu.VMEM((blocks, half, size), BF16),
            pltpu.VMEM((rows, half), BF16),
            pltpu.VMEM((rows, half), F32),
            pltpu.VMEM((2, top // 4 + 16, half), F32),
            pltpu.VMEM((2 * rows, half), BF16),
            pltpu.VMEM((UNROLL,) + tiles.shape[1:], BF16),
        ],
        in_specs=[VMEM, HBM, VMEM, HBM] + [VMEM] * 7 + [HBM],
        out_specs=[VMEM] * 6,
        scratch_shapes=[
            pltpu.VMEM((4,) + piece, BF16),
            pltpu.VMEM((3,) + piece, BF16),
            pltpu.VMEM((3,) + piece, BF16),
            pltpu.VMEM(piece, BF16),
            pltpu.VMEM(piece, BF16),
            pltpu.VMEM((4 * half, 2 * half), BF16),
            pltpu.VMEM((share, half, size), BF16),
            pltpu.VMEM((top, 2 * half), F32),
            pltpu.VMEM((16, 2 * half), F32),
            pltpu.VMEM((3, top // 4 + 16, 2 * half), BF16),
            pltpu.VMEM((4, top // 4 + 16, 2 * half), BF16),
            pltpu.VMEM((4, top // 4 + 16, 2 * half), BF16),
            pltpu.SemaphoreType.DMA((3,)),
            pltpu.SemaphoreType.DMA((copies,)),
            pltpu.SemaphoreType.DMA((copies,)),
        ],
        compiler_params=pltpu.CompilerParams(collective_id=2, has_side_effects=True, vmem_limit_bytes=32 * MIB),
        name="middle",
    )(partial, features, own_far, cotangent, cot_far, w_self, w_neigh, w_self_far, w_neigh_far, bias, bias_far, tiles)


def final_kernel(
    back, weight_sum, far,
    sums, weights, bias_total, far_got,
    got_core, sent_row, kept, got_row, sent_pair, got_pair, w_sent, w_got,
    send_sems, recv_sems,
):
    row, col, edge, core, side = place()
    rows = lax.axis_size("row")
    x, z = lax.rem(row, 4), lax.div(row, 4)
    twin, pair = {"edge": edge + 1 - 2 * core}, {"edge": lax.rem(edge + 2, 4)}
    up, down = {"row": lax.rem(row + 1, rows)}, {"row": lax.rem(row + rows - 1, rows)}
    z_peers = [{"row": lax.rem(z + j, 4) * 4 + x} for j in (1, 2, 3)]
    e_peers = [{"edge": lax.rem(edge + j, 4)} for j in (1, 2, 3)]
    far_peers = [{"edge": lax.rem(edge + j, 4), "col": 1 - col} for j in range(4)]
    greet([up, down] + e_peers + far_peers + z_peers)
    send = Sender(send_sems, recv_sems)
    blocks = back.shape[0] // 3
    share = blocks // 4

    def piece(part, at_side, on_core):
        return pl.ds(part * blocks + (2 * at_side + on_core) * share, share)

    order = [(0, 1 - side), (2, 1 - side), (0, side), (2, side), (1, 1 - side), (1, side)]
    to_twin = [
        send(back.at[piece(part, at, 1 - core)], got_core.at[i], twin) for i, (part, at) in enumerate(order)
    ]

    to_partner = send(far, far_got, far_peers[0])

    def summed(i):
        to_twin[i].wait_recv()
        part, at = order[i]
        return back[piece(part, at, core)].astype(F32) + got_core[i].astype(F32)

    to_row = []
    for i in range(4):
        sent_row[i] = summed(i).astype(BF16)
        to_row.append(send(sent_row.at[i], got_row.at[i], down if i % 2 == 0 else up))

    top = weights.shape[0]
    many, bias_at = top // 16, top // 4
    to_group = []
    for i, peer in enumerate(e_peers + far_peers):
        j, owner = (0, lax.rem(edge + 1 + i, 4)) if i < 3 else (1, lax.rem(edge + i - 3, 4))
        w_sent[i, :many] = weight_sum[j, pl.ds(pl.multiple_of(owner * many, 8), many), :]
        w_sent[i, many:] = weight_sum[j, bias_at:]
        to_group.append(send(w_sent.at[i], w_got.at[i], peer))

    for copy in to_group:
        copy.wait_recv()
    group_total = w_got[0]
    for i in range(1, 7):
        group_total += w_got[i]
    start = pl.multiple_of(z * (top // 4) + edge * many, 8)
    weights[pl.ds(start, many), :] = weight_sum[0, pl.ds(pl.multiple_of(edge * many, 8), many), :] + group_total[:many]
    bias_total[...] = weight_sum[0, bias_at:] + group_total[many:]

    def gathered(start, many, peers):
        at = pl.ds(pl.multiple_of(start, 8), many)
        return [send(weights.at[at], weights.at[at], peer) for peer in peers]

    steps = gathered(start, many, e_peers)
    for i in range(2):
        kept[i] = summed(4 + i)
    for step in steps:
        step.wait_recv()
    steps = gathered(z * (top // 4), top // 4, z_peers)
    for i in range(2):
        to_row[i].wait_recv()
    sent_pair[...] = (kept[0] + got_row[0].astype(F32) + got_row[1].astype(F32)).astype(BF16)
    to_pair = send(sent_pair, got_pair, pair)
    for i in range(2, 4):
        to_row[i].wait_recv()
    kept[1] += got_row[2].astype(F32) + got_row[3].astype(F32)
    to_pair.wait_recv()
    sums[...] = kept[1] + got_pair[...].astype(F32)
    to_partner.wait_recv()
    for step in steps:
        step.wait_recv()
    send.finish()


def finish(back, weight_sum, far):
    share, half, size = back.shape[0] // 12, back.shape[1], back.shape[2]
    unit = half // 4 + 16
    copies = 6 + 1 + 4 + 1 + 7 + 6
    piece = (share, half, size)
    return pl.pallas_call(
        final_kernel,
        out_shape=[
            pltpu.VMEM(piece, F32),
            pltpu.VMEM((4 * half, half), F32),
            pltpu.VMEM((16, half), F32),
            pltpu.VMEM(far.shape, BF16),
        ],
        in_specs=[VMEM] * 3,
        out_specs=[VMEM] * 4,
        scratch_shapes=[
            pltpu.VMEM((6,) + piece, BF16),
            pltpu.VMEM((4,) + piece, BF16),
            pltpu.VMEM((2,) + piece, F32),
            pltpu.VMEM((4,) + piece, BF16),
            pltpu.VMEM(piece, BF16),
            pltpu.VMEM(piece, BF16),
            *[pltpu.VMEM((7, unit, half), F32)] * 2,
            pltpu.SemaphoreType.DMA((copies,)),
            pltpu.SemaphoreType.DMA((copies,)),
        ],
        compiler_params=pltpu.CompilerParams(collective_id=3, has_side_effects=True, vmem_limit_bytes=32 * MIB),
        name="finish",
    )(back, weight_sum, far)


def writing_kernel(
    scale, out_near, self_near, far, sums, weights, bias_total,
    output, features_grad, w_self_grad, w_neigh_grad, bias_grad,
):
    col = lax.axis_index("col")
    rows, half = out_near.shape
    near, away = pl.multiple_of(col * rows, 16), pl.multiple_of((1 - col) * rows, 16)
    output[pl.ds(near, rows), :] = out_near[...]
    output[pl.ds(away, rows), :] = far[:rows]
    features_grad[pl.ds(near, rows), :] = self_near[...]
    features_grad[pl.ds(away, rows), :] = far[rows:].astype(F32)
    share, _, size = sums.shape
    for b in range(share):
        features_grad[b * size : (b + 1) * size, :] += sums[b].T
    top = weights.shape[0]
    w_self_grad[...] = weights[: top // 2] * scale
    w_neigh_grad[...] = weights[top // 2 :] * scale
    bias_grad[...] = jnp.sum(bias_total[...], axis=0, keepdims=True) * scale


def written(scale, out_near, self_near, far, sums, weights, bias_total):
    rows, half = out_near.shape
    top = weights.shape[0]
    return pl.pallas_call(
        functools.partial(writing_kernel, scale),
        out_shape=[
            jax.ShapeDtypeStruct((2 * rows, half), BF16),
            jax.ShapeDtypeStruct((2 * rows, half), F32),
            jax.ShapeDtypeStruct((top // 2, half), F32),
            jax.ShapeDtypeStruct((top // 2, half), F32),
            jax.ShapeDtypeStruct((1, half), F32),
        ],
        in_specs=[VMEM] * 6,
        out_specs=[VMEM] * 5,
        compiler_params=pltpu.CompilerParams(vmem_limit_bytes=4 * MIB),
        name="written",
    )(out_near, self_near, far, sums, weights, bias_total)


def local(features, tiles, tile_rows, tile_cols, tile_count, w_self, w_neigh, bias, cotangent):
    rows_dev, half = features.shape
    size = tiles.shape[1]
    blocks = rows_dev // size
    nodes = rows_dev * lax.axis_size("row")
    scale = 1.0 / math.sqrt(nodes)

    own = features.reshape(blocks, size, half)
    cot = cotangent.reshape(-1, size, half)
    bias_row = bias.reshape(1, half)
    own, cot, w_self, w_neigh, bias_row, tile_rows, tile_cols, tiles = (
        pltpu.with_memory_space_constraint(array, pltpu.HBM)
        for array in (own, cot, w_self, w_neigh, bias_row, tile_rows, tile_cols, tiles)
    )
    window, head, own_far, cot_far, w_self_far, w_neigh_far, bias_far = exchange_inputs(
        own, cot, w_self, w_neigh, bias_row, tiles
    )
    partial = tile_sum(forward_kernel, blocks, tile_rows, tile_cols, tile_count, window, head, tiles)
    grads, out_near, self_near, weight_sum, far, head = middle(
        partial, own, own_far, cot, cot_far, w_self, w_neigh, w_self_far, w_neigh_far, bias_row, bias_far, tiles
    )
    back = tile_sum(backward_kernel, 3 * blocks, tile_rows, tile_cols, tile_count, grads, head, tiles)
    sums, weights, bias_total, far = finish(back, weight_sum, far)
    output, features_grad, w_self_grad, w_neigh_grad, bias_grad = written(
        scale, out_near, self_near, far, sums, weights, bias_total
    )
    return (output, features_grad, w_self_grad, w_neigh_grad, bias_grad.reshape(half))


def solution(mesh):
    return jax.shard_map(
        local,
        mesh=mesh,
        in_specs=(
            P("row", "col"),
            P(("row", "edge"), None, None),
            P(("row", "edge")),
            P(("row", "edge")),
            P(("row", "edge")),
            P(None, "col"),
            P(None, "col"),
            P("col"),
            P(("row", "edge"), "col"),
        ),
        out_specs=(
            P(("row", "edge"), "col"),
            P(("row", "edge"), "col"),
            P(None, "col"),
            P(None, "col"),
            P("col"),
        ),
        check_vma=False,
    )
```

```python
import functools
import math

import jax
import jax.numpy as jnp
from jax import lax
from jax.experimental import pallas as pl
from jax.experimental.pallas import tpu as pltpu
from jax.sharding import PartitionSpec as P

F32 = jnp.float32
BF16 = jnp.bfloat16
UNROLL = 88
LAG = 4
MIB = 1024 * 1024


MESH = pl.DeviceIdType.MESH


def place():
    row, col, edge = (lax.axis_index(name) for name in ("row", "col", "edge"))
    return row, col, edge, lax.rem(edge, 2), lax.div(edge, 2)


def greet(peers):
    barrier = pltpu.get_barrier_semaphore()
    for peer in peers:
        pl.semaphore_signal(barrier, inc=1, device_id=peer, device_id_type=MESH)
    pl.semaphore_wait(barrier, len(peers))


class Sender:
    def __init__(self, send_sems, recv_sems):
        self.send_sems, self.recv_sems, self.used = send_sems, recv_sems, []

    def __call__(self, src, dst, peer):
        index = len(self.used)
        copy = pltpu.make_async_remote_copy(
            src_ref=src,
            dst_ref=dst,
            send_sem=self.send_sems.at[index],
            recv_sem=self.recv_sems.at[index],
            device_id=peer,
            device_id_type=MESH,
        )
        copy.start()
        self.used.append(copy)
        return copy

    def finish(self):
        for copy in self.used:
            copy.wait_send()


def add_tiles(count, head, tiles, held, sems, total, product, target):
    spare = total.shape[0] - 1
    groups = lax.div(count + UNROLL - 1, UNROLL)

    def fetch(g):
        at = pl.ds(g * UNROLL, UNROLL)
        return pltpu.make_async_copy(tiles.at[at], held.at[pl.ds((g - 1) * UNROLL, UNROLL)], sems.at[g - 1])

    def start_step(g, carry):
        fetch(g).start()
        return carry

    lax.fori_loop(1, groups, start_step, 0)
    total[...] = jnp.zeros_like(total)

    def add_group(source, first, start):
        waiting = {}
        for u in range(UNROLL + LAG):
            if u < UNROLL:
                waiting[u] = product(start + u, source[first + u])
            if u >= LAG:
                slot = start + u - LAG
                total[jnp.where(slot < count, target(slot), spare)] += waiting.pop(u - LAG)

    add_group(head, 0, 0)

    def group_step(g, carry):
        fetch(g).wait()
        add_group(held, (g - 1) * UNROLL, g * UNROLL)
        return carry

    lax.fori_loop(1, groups, group_step, 0)


def forward_kernel(rows, cols, count_ref, window, head, tiles, out, held, total, sems):
    add_tiles(
        count_ref[0], head, tiles, held, sems, total,
        lambda slot, tile: jnp.dot(tile, window[cols[slot]], preferred_element_type=F32),
        lambda slot: rows[slot],
    )
    out[...] = total[: out.shape[0]].astype(BF16)


def backward_kernel(rows, cols, count_ref, grads, head, tiles, out, held, total, sems):
    add_tiles(
        count_ref[0], head, tiles, held, sems, total,
        lambda slot, tile: jnp.dot(grads[rows[slot]], tile, preferred_element_type=F32),
        lambda slot: cols[slot],
    )
    out[...] = total[: out.shape[0]].astype(BF16)


SMEM = pl.BlockSpec(memory_space=pltpu.SMEM)
VMEM = pl.BlockSpec(memory_space=pltpu.VMEM)
HBM = pl.BlockSpec(memory_space=pltpu.HBM)


def tile_sum(kernel, blocks, tile_rows, tile_cols, tile_count, source, head, tiles):
    slots, size, _ = tiles.shape
    return pl.pallas_call(
        kernel,
        out_shape=pltpu.VMEM((blocks, size, size), BF16),
        in_specs=[SMEM] * 3 + [VMEM, VMEM, HBM],
        out_specs=VMEM,
        scratch_shapes=[
            pltpu.VMEM((slots - UNROLL, size, size), BF16),
            pltpu.VMEM((blocks + 1, size, size), F32),
            pltpu.SemaphoreType.DMA((slots // UNROLL - 1,)),
        ],
        compiler_params=pltpu.CompilerParams(vmem_limit_bytes=32 * MIB),
        cost_estimate=pl.CostEstimate(flops=2 * slots * size**3, bytes_accessed=slots * 2 * size**2, transcendentals=0),
        name=kernel.__name__.replace("kernel", "sum"),
    )(tile_rows, tile_cols, tile_count, source, head, tiles)


HALO_CHUNKS = 4


def halo_kernel(
    features, cotangent, w_self, w_neigh, bias, tiles,
    window, head, own_far, cot_far, w_self_far, w_neigh_far, bias_far,
    load_sems, send_sems, recv_sems,
):
    row, col, edge, core, _ = place()
    rows = lax.axis_size("row")
    up, down = {"row": lax.rem(row + 1, rows)}, {"row": lax.rem(row + rows - 1, rows)}
    twin, partner = {"edge": edge + 1 - 2 * core}, {"col": 1 - col}
    blocks = features.shape[0]
    share = blocks // 8
    greet([up, down, twin, partner])
    send = Sender(send_sems, recv_sems)
    step = blocks // 2 // HALO_CHUNKS
    parts = [pl.ds(core * (blocks // 2) + i * step, step) for i in range(HALO_CHUNKS)]
    arriving = []
    for part in parts:
        for side, peer in ((0, up), (2, down)):
            landing = pl.ds(side * blocks + core * (blocks // 2) + (len(arriving) // 2) * step, step)
            arriving.append((landing, send(features.at[part], window.at[landing], peer)))
    theirs = pl.ds(edge * 2 * share + (1 - col) * share, share)
    theirs_cot = pl.ds((1 - col) * share, share)
    swaps = [
        send(features.at[theirs], own_far, partner),
        send(cotangent.at[theirs_cot], cot_far, partner),
        send(w_self, w_self_far, partner),
        send(w_neigh, w_neigh_far, partner),
        send(bias, bias_far, partner),
    ]
    loads = [
        pltpu.make_async_copy(features, window.at[pl.ds(blocks, blocks)], load_sems.at[0]),
        pltpu.make_async_copy(tiles.at[pl.ds(0, UNROLL)], head, load_sems.at[1]),
    ]
    for load in loads:
        load.start()
    handed = []
    for landing, copy in arriving:
        copy.wait_recv()
        handed.append(send(window.at[landing], window.at[landing], twin))
    for copy in swaps + handed:
        copy.wait_recv()
    for load in loads:
        load.wait()
    send.finish()


def exchange_inputs(features, cotangent, w_self, w_neigh, bias, tiles):
    blocks, size, half = features.shape
    share = blocks // 8
    shapes = [
        jax.ShapeDtypeStruct((3 * blocks, size, half), BF16),
        jax.ShapeDtypeStruct((UNROLL,) + tiles.shape[1:], BF16),
        jax.ShapeDtypeStruct((share, size, half), BF16),
        jax.ShapeDtypeStruct((share, size, half), BF16),
        w_self, w_neigh, bias,
    ]
    copies = 4 * HALO_CHUNKS + 5
    return pl.pallas_call(
        halo_kernel,
        out_shape=[pltpu.VMEM(s.shape, s.dtype) for s in shapes],
        in_specs=[HBM] * 6,
        out_specs=[VMEM] * 7,
        scratch_shapes=[
            pltpu.SemaphoreType.DMA((2,)),
            pltpu.SemaphoreType.DMA((copies,)),
            pltpu.SemaphoreType.DMA((copies,)),
        ],
        compiler_params=pltpu.CompilerParams(collective_id=1, has_side_effects=True, vmem_limit_bytes=32 * MIB),
        name="exchange_inputs",
    )(features, cotangent, w_self, w_neigh, bias, tiles)


def mid_kernel(
    partial, features, own_far, cotangent, cot_far, w_self, w_neigh, w_self_far, w_neigh_far, bias, bias_far, tiles,
    grads, out_near, self_near, weight_sum, far, head,
    got_core, sent, got, own, cot, weights, sent_grads,
    w_all, w_bias, w_sent_z, w_got_z, w_got_x,
    local_sems, send_sems, recv_sems,
):
    row, col, edge, core, pair_side = place()
    other = 1 - col
    twin, pair, partner = {"edge": edge + 1 - 2 * core}, {"edge": lax.rem(edge + 2, 4)}, {"col": other}
    diagonal = {"edge": lax.rem(edge + 2, 4), "col": other}
    x, z = lax.rem(row, 4), lax.div(row, 4)
    along_z = [lax.rem(z + j, 4) for j in (1, 2, 3)]
    x_peers = [{"row": z * 4 + lax.rem(x + j, 4)} for j in (1, 2, 3)]
    z_peers = [{"row": to * 4 + x} for to in along_z]
    blocks, size, half = partial.shape
    share = blocks // 8
    near_rows = own_far.shape[0] * size
    local = [
        pltpu.make_async_copy(features.at[pl.ds(edge * 2 * share + col * share, share)], own, local_sems.at[0]),
        pltpu.make_async_copy(cotangent.at[pl.ds(col * share, share)], cot, local_sems.at[1]),
    ]
    ahead = pltpu.make_async_copy(tiles.at[pl.ds(0, UNROLL)], head, local_sems.at[2])
    for copy in local:
        copy.start()
    ahead.start()
    greet([twin, pair, partner, diagonal] + x_peers + z_peers)
    send = Sender(send_sems, recv_sems)

    def piece(side, on_core, column):
        return pl.ds((2 * side + on_core) * 2 * share + column * share, share)

    order = [(pair_side, other), (1 - pair_side, other), (1 - pair_side, col), (pair_side, col)]
    to_twin = [
        send(partial.at[piece(side, 1 - core, column)], got_core.at[i], twin)
        for i, (side, column) in enumerate(order)
    ]
    near_w, far_w = pl.ds(pl.multiple_of(col * half, half), half), pl.ds(pl.multiple_of(other * half, half), half)
    for k, (near, away) in enumerate(((w_self, w_self_far), (w_neigh, w_neigh_far))):
        for j, rows in enumerate((near_w, far_w)):
            at = pl.ds((2 * k + j) * half, half)
            weights[at, :half] = near[rows, :]
            weights[at, half:] = away[rows, :]

    def summed(i):
        to_twin[i].wait_recv()
        side, column = order[i]
        return partial[piece(side, core, column)].astype(F32) + got_core[i].astype(F32)

    crossing = []
    for i, owner in enumerate((partner, diagonal, pair)):
        sent[i] = summed(i).astype(BF16)
        crossing.append(send(sent.at[i], got.at[i], owner))
    kept = summed(3)
    for copy in local:
        copy.wait()
    for copy in crossing:
        copy.wait_recv()
    agg_near = (kept + got[2].astype(F32)).astype(BF16)
    agg_far = (got[0].astype(F32) + got[1].astype(F32)).astype(BF16)

    def flat(blocks_of):
        return blocks_of.reshape(near_rows, half)

    mixed = jnp.concatenate(
        [flat(own[...]), flat(own_far[...]), flat(agg_near), flat(agg_far)], axis=1
    )
    pre = jnp.dot(mixed, weights[...], preferred_element_type=F32) + jnp.concatenate(
        [bias[...], bias_far[...]], axis=1
    )
    sigm = jax.nn.sigmoid(pre)
    cot_full = jnp.concatenate([flat(cot[...]), flat(cot_far[...])], axis=1).astype(F32)
    grad_pre = cot_full * sigm * (1.0 + pre * (1.0 - sigm))
    grad_low = grad_pre.astype(BF16)
    over_cols = (((1,), (1,)), ((), ()))
    agg_back = lax.dot_general(
        weights[2 * half :, :], grad_low, over_cols, preferred_element_type=F32
    ).astype(BF16)
    mine = pl.ds(edge * 2 * share + col * share, share)
    for b in range(share):
        grads[edge * 2 * share + col * share + b] = agg_back[:half, b * size : (b + 1) * size]
        sent_grads[b] = agg_back[half:, b * size : (b + 1) * size]
    crossing = [
        send(sent_grads, grads.at[mine], diagonal),
        send(sent_grads, grads.at[mine], partner),
        send(grads.at[mine], grads.at[mine], pair),
    ]
    handed = [send(grads.at[mine], grads.at[mine], twin)]

    parts = lax.dot_general(mixed, grad_low, (((0,), (0,)), ((), ())), preferred_element_type=F32)
    for k in range(2):
        for j, start in enumerate((col * half, other * half)):
            at = (2 * k + j) * half
            w_all[pl.ds(pl.multiple_of(2 * k * half + start, half), half), :] = parts[at : at + half, :]
    w_bias[...] = jnp.sum(grad_pre.reshape(near_rows // 16, 16, 2 * half), axis=0)

    z_many = 4 * half // 4
    z_start = pl.multiple_of(z * z_many, 8)
    steps = []
    for j in range(3):
        w_sent_z[j, :z_many] = w_all[pl.ds(pl.multiple_of(along_z[j] * z_many, 8), z_many), :].astype(BF16)
        w_sent_z[j, z_many:] = w_bias[...].astype(BF16)
        steps.append(send(w_sent_z.at[j], w_got_z.at[z], z_peers[j]))
    w_got_z[z, z_many:] = w_bias[...].astype(BF16)

    output = (pre * sigm).astype(BF16)
    out_near[...] = output[:, :half]
    far[:near_rows] = output[:, half:]
    self_back = lax.dot_general(grad_low, weights[: 2 * half, :], over_cols, preferred_element_type=F32)
    self_near[...] = self_back[:, :half]
    far[near_rows:] = self_back[:, half:].astype(BF16)

    for step in steps:
        step.wait_recv()
    quarter = w_all[pl.ds(z_start, z_many), :]
    for j in range(3):
        quarter += w_got_z[along_z[j], :z_many].astype(F32)
    bias_sum = w_got_z[0, z_many:].astype(F32)
    for j in range(1, 4):
        bias_sum += w_got_z[j, z_many:].astype(F32)
    w_got_x[x, :z_many] = quarter.astype(BF16)
    w_got_x[x, z_many:] = bias_sum.astype(BF16)
    steps = [send(w_got_x.at[x], w_got_x.at[x], peer) for peer in x_peers]

    far_edge = lax.rem(edge + 2, 4)
    homes = [
        pl.ds(far_edge * 2 * share + other * share, share),
        pl.ds(edge * 2 * share + other * share, share),
        pl.ds(far_edge * 2 * share + col * share, share),
    ]
    for k in (1, 2, 0):
        crossing[k].wait_recv()
        handed.append(send(grads.at[homes[k]], grads.at[homes[k]], twin))
    for step in steps:
        step.wait_recv()
    x_total = w_got_x[0].astype(F32)
    for j in range(1, 4):
        x_total += w_got_x[j].astype(F32)
    for j in range(2):
        weight_sum[j] = x_total[:, j * half : (j + 1) * half]
    for copy in handed:
        copy.wait_recv()
    ahead.wait()
    send.finish()


def middle(partial, features, own_far, cotangent, cot_far, w_self, w_neigh, w_self_far, w_neigh_far, bias, bias_far, tiles):
    blocks, size, half = partial.shape
    share = blocks // 8
    rows = share * size
    copies = 4 + 3 + 3 + 4 + 6
    top = 4 * half
    piece = (share, size, half)
    return pl.pallas_call(
        mid_kernel,
        out_shape=[
            pltpu.VMEM((blocks, half, size), BF16),
            pltpu.VMEM((rows, half), BF16),
            pltpu.VMEM((rows, half), F32),
            pltpu.VMEM((2, top // 4 + 16, half), F32),
            pltpu.VMEM((2 * rows, half), BF16),
            pltpu.VMEM((UNROLL,) + tiles.shape[1:], BF16),
        ],
        in_specs=[VMEM, HBM, VMEM, HBM] + [VMEM] * 7 + [HBM],
        out_specs=[VMEM] * 6,
        scratch_shapes=[
            pltpu.VMEM((4,) + piece, BF16),
            pltpu.VMEM((3,) + piece, BF16),
            pltpu.VMEM((3,) + piece, BF16),
            pltpu.VMEM(piece, BF16),
            pltpu.VMEM(piece, BF16),
            pltpu.VMEM((4 * half, 2 * half), BF16),
            pltpu.VMEM((share, half, size), BF16),
            pltpu.VMEM((top, 2 * half), F32),
            pltpu.VMEM((16, 2 * half), F32),
            pltpu.VMEM((3, top // 4 + 16, 2 * half), BF16),
            pltpu.VMEM((4, top // 4 + 16, 2 * half), BF16),
            pltpu.VMEM((4, top // 4 + 16, 2 * half), BF16),
            pltpu.SemaphoreType.DMA((3,)),
            pltpu.SemaphoreType.DMA((copies,)),
            pltpu.SemaphoreType.DMA((copies,)),
        ],
        compiler_params=pltpu.CompilerParams(collective_id=2, has_side_effects=True, vmem_limit_bytes=32 * MIB),
        name="middle",
    )(partial, features, own_far, cotangent, cot_far, w_self, w_neigh, w_self_far, w_neigh_far, bias, bias_far, tiles)


def final_kernel(
    back, weight_sum, far,
    sums, weights, bias_total, far_got,
    got_core, sent_row, kept, got_row, sent_pair, got_pair, w_sent, w_got,
    send_sems, recv_sems,
):
    row, col, edge, core, side = place()
    rows = lax.axis_size("row")
    x, z = lax.rem(row, 4), lax.div(row, 4)
    twin, pair = {"edge": edge + 1 - 2 * core}, {"edge": lax.rem(edge + 2, 4)}
    up, down = {"row": lax.rem(row + 1, rows)}, {"row": lax.rem(row + rows - 1, rows)}
    z_peers = [{"row": lax.rem(z + j, 4) * 4 + x} for j in (1, 2, 3)]
    e_peers = [{"edge": lax.rem(edge + j, 4)} for j in (1, 2, 3)]
    far_peers = [{"edge": lax.rem(edge + j, 4), "col": 1 - col} for j in range(4)]
    greet([up, down] + e_peers + far_peers + z_peers)
    send = Sender(send_sems, recv_sems)
    blocks = back.shape[0] // 3
    share = blocks // 4

    def piece(part, at_side, on_core):
        return pl.ds(part * blocks + (2 * at_side + on_core) * share, share)

    order = [(0, 1 - side), (2, 1 - side), (0, side), (2, side), (1, 1 - side), (1, side)]
    to_twin = [
        send(back.at[piece(part, at, 1 - core)], got_core.at[i], twin) for i, (part, at) in enumerate(order)
    ]

    def summed(i):
        to_twin[i].wait_recv()
        part, at = order[i]
        return back[piece(part, at, core)].astype(F32) + got_core[i].astype(F32)

    top = weights.shape[0]
    many, bias_at = top // 16, top // 4
    to_group = []
    for i, peer in enumerate(e_peers + far_peers):
        j, owner = (0, lax.rem(edge + 1 + i, 4)) if i < 3 else (1, lax.rem(edge + i - 3, 4))
        w_sent[i, :many] = weight_sum[j, pl.ds(pl.multiple_of(owner * many, 8), many), :]
        w_sent[i, many:] = weight_sum[j, bias_at:]
        to_group.append(send(w_sent.at[i], w_got.at[i], peer))

    to_row = []
    for i in range(4):
        sent_row[i] = summed(i).astype(BF16)
        to_row.append(send(sent_row.at[i], got_row.at[i], down if i % 2 == 0 else up))

    to_partner = send(far, far_got, far_peers[0])
    for copy in to_group:
        copy.wait_recv()
    group_total = w_got[0]
    for i in range(1, 7):
        group_total += w_got[i]
    start = pl.multiple_of(z * (top // 4) + edge * many, 8)
    weights[pl.ds(start, many), :] = weight_sum[0, pl.ds(pl.multiple_of(edge * many, 8), many), :] + group_total[:many]
    bias_total[...] = weight_sum[0, bias_at:] + group_total[many:]

    def gathered(start, many, peers):
        at = pl.ds(pl.multiple_of(start, 8), many)
        return [send(weights.at[at], weights.at[at], peer) for peer in peers]

    steps = gathered(start, many, e_peers)
    for i in range(2):
        kept[i] = summed(4 + i)
    for step in steps:
        step.wait_recv()
    steps = gathered(z * (top // 4), top // 4, z_peers)
    for i in range(2):
        to_row[i].wait_recv()
    sent_pair[...] = (kept[0] + got_row[0].astype(F32) + got_row[1].astype(F32)).astype(BF16)
    to_pair = send(sent_pair, got_pair, pair)
    for i in range(2, 4):
        to_row[i].wait_recv()
    kept[1] += got_row[2].astype(F32) + got_row[3].astype(F32)
    to_pair.wait_recv()
    sums[...] = kept[1] + got_pair[...].astype(F32)
    to_partner.wait_recv()
    for step in steps:
        step.wait_recv()
    send.finish()


def finish(back, weight_sum, far):
    share, half, size = back.shape[0] // 12, back.shape[1], back.shape[2]
    unit = half // 4 + 16
    copies = 6 + 1 + 4 + 1 + 7 + 6
    piece = (share, half, size)
    return pl.pallas_call(
        final_kernel,
        out_shape=[
            pltpu.VMEM(piece, F32),
            pltpu.VMEM((4 * half, half), F32),
            pltpu.VMEM((16, half), F32),
            pltpu.VMEM(far.shape, BF16),
        ],
        in_specs=[VMEM] * 3,
        out_specs=[VMEM] * 4,
        scratch_shapes=[
            pltpu.VMEM((6,) + piece, BF16),
            pltpu.VMEM((4,) + piece, BF16),
            pltpu.VMEM((2,) + piece, F32),
            pltpu.VMEM((4,) + piece, BF16),
            pltpu.VMEM(piece, BF16),
            pltpu.VMEM(piece, BF16),
            *[pltpu.VMEM((7, unit, half), F32)] * 2,
            pltpu.SemaphoreType.DMA((copies,)),
            pltpu.SemaphoreType.DMA((copies,)),
        ],
        compiler_params=pltpu.CompilerParams(collective_id=3, has_side_effects=True, vmem_limit_bytes=32 * MIB),
        name="finish",
    )(back, weight_sum, far)


def writing_kernel(
    scale, out_near, self_near, far, sums, weights, bias_total,
    output, features_grad, w_self_grad, w_neigh_grad, bias_grad,
):
    col = lax.axis_index("col")
    rows, half = out_near.shape
    near, away = pl.multiple_of(col * rows, 16), pl.multiple_of((1 - col) * rows, 16)
    output[pl.ds(near, rows), :] = out_near[...]
    output[pl.ds(away, rows), :] = far[:rows]
    features_grad[pl.ds(near, rows), :] = self_near[...]
    features_grad[pl.ds(away, rows), :] = far[rows:].astype(F32)
    share, _, size = sums.shape
    for b in range(share):
        features_grad[b * size : (b + 1) * size, :] += sums[b].T
    top = weights.shape[0]
    w_self_grad[...] = weights[: top // 2] * scale
    w_neigh_grad[...] = weights[top // 2 :] * scale
    bias_grad[...] = jnp.sum(bias_total[...], axis=0, keepdims=True) * scale


def written(scale, out_near, self_near, far, sums, weights, bias_total):
    rows, half = out_near.shape
    top = weights.shape[0]
    return pl.pallas_call(
        functools.partial(writing_kernel, scale),
        out_shape=[
            jax.ShapeDtypeStruct((2 * rows, half), BF16),
            jax.ShapeDtypeStruct((2 * rows, half), F32),
            jax.ShapeDtypeStruct((top // 2, half), F32),
            jax.ShapeDtypeStruct((top // 2, half), F32),
            jax.ShapeDtypeStruct((1, half), F32),
        ],
        in_specs=[VMEM] * 6,
        out_specs=[VMEM] * 5,
        compiler_params=pltpu.CompilerParams(vmem_limit_bytes=4 * MIB),
        name="written",
    )(out_near, self_near, far, sums, weights, bias_total)


def local(features, tiles, tile_rows, tile_cols, tile_count, w_self, w_neigh, bias, cotangent):
    rows_dev, half = features.shape
    size = tiles.shape[1]
    blocks = rows_dev // size
    nodes = rows_dev * lax.axis_size("row")
    scale = 1.0 / math.sqrt(nodes)

    own = features.reshape(blocks, size, half)
    cot = cotangent.reshape(-1, size, half)
    bias_row = bias.reshape(1, half)
    own, cot, w_self, w_neigh, bias_row, tile_rows, tile_cols, tiles = (
        pltpu.with_memory_space_constraint(array, pltpu.HBM)
        for array in (own, cot, w_self, w_neigh, bias_row, tile_rows, tile_cols, tiles)
    )
    window, head, own_far, cot_far, w_self_far, w_neigh_far, bias_far = exchange_inputs(
        own, cot, w_self, w_neigh, bias_row, tiles
    )
    partial = tile_sum(forward_kernel, blocks, tile_rows, tile_cols, tile_count, window, head, tiles)
    grads, out_near, self_near, weight_sum, far, head = middle(
        partial, own, own_far, cot, cot_far, w_self, w_neigh, w_self_far, w_neigh_far, bias_row, bias_far, tiles
    )
    back = tile_sum(backward_kernel, 3 * blocks, tile_rows, tile_cols, tile_count, grads, head, tiles)
    sums, weights, bias_total, far = finish(back, weight_sum, far)
    output, features_grad, w_self_grad, w_neigh_grad, bias_grad = written(
        scale, out_near, self_near, far, sums, weights, bias_total
    )
    return (output, features_grad, w_self_grad, w_neigh_grad, bias_grad.reshape(half))


def solution(mesh):
    return jax.shard_map(
        local,
        mesh=mesh,
        in_specs=(
            P("row", "col"),
            P(("row", "edge"), None, None),
            P(("row", "edge")),
            P(("row", "edge")),
            P(("row", "edge")),
            P(None, "col"),
            P(None, "col"),
            P("col"),
            P(("row", "edge"), "col"),
        ),
        out_specs=(
            P(("row", "edge"), "col"),
            P(("row", "edge"), "col"),
            P(None, "col"),
            P(None, "col"),
            P("col"),
        ),
        check_vma=False,
    )
```

```python
import functools
import math

import jax
import jax.numpy as jnp
from jax import lax
from jax.experimental import pallas as pl
from jax.experimental.pallas import tpu as pltpu
from jax.sharding import PartitionSpec as P

F32 = jnp.float32
BF16 = jnp.bfloat16
UNROLL = 88
LAG = 4
MIB = 1024 * 1024


MESH = pl.DeviceIdType.MESH


def place():
    row, col, edge = (lax.axis_index(name) for name in ("row", "col", "edge"))
    return row, col, edge, lax.rem(edge, 2), lax.div(edge, 2)


def greet(peers):
    barrier = pltpu.get_barrier_semaphore()
    for peer in peers:
        pl.semaphore_signal(barrier, inc=1, device_id=peer, device_id_type=MESH)
    pl.semaphore_wait(barrier, len(peers))


class Sender:
    def __init__(self, send_sems, recv_sems):
        self.send_sems, self.recv_sems, self.used = send_sems, recv_sems, []

    def __call__(self, src, dst, peer):
        index = len(self.used)
        copy = pltpu.make_async_remote_copy(
            src_ref=src,
            dst_ref=dst,
            send_sem=self.send_sems.at[index],
            recv_sem=self.recv_sems.at[index],
            device_id=peer,
            device_id_type=MESH,
        )
        copy.start()
        self.used.append(copy)
        return copy

    def finish(self):
        for copy in self.used:
            copy.wait_send()


def add_tiles(count, head, tiles, held, sems, total, product, target):
    spare = total.shape[0] - 1
    groups = lax.div(count + UNROLL - 1, UNROLL)

    def fetch(g):
        at = pl.ds(g * UNROLL, UNROLL)
        return pltpu.make_async_copy(tiles.at[at], held.at[pl.ds((g - 1) * UNROLL, UNROLL)], sems.at[g - 1])

    def start_step(g, carry):
        fetch(g).start()
        return carry

    lax.fori_loop(1, groups, start_step, 0)
    total[...] = jnp.zeros_like(total)

    def add_group(source, first, start):
        waiting = {}
        for u in range(UNROLL + LAG):
            if u < UNROLL:
                waiting[u] = product(start + u, source[first + u])
            if u >= LAG:
                slot = start + u - LAG
                total[jnp.where(slot < count, target(slot), spare)] += waiting.pop(u - LAG)

    add_group(head, 0, 0)

    def group_step(g, carry):
        fetch(g).wait()
        add_group(held, (g - 1) * UNROLL, g * UNROLL)
        return carry

    lax.fori_loop(1, groups, group_step, 0)


def forward_kernel(rows, cols, count_ref, window, head, tiles, out, held, total, sems):
    add_tiles(
        count_ref[0], head, tiles, held, sems, total,
        lambda slot, tile: jnp.dot(tile, window[cols[slot]], preferred_element_type=F32),
        lambda slot: rows[slot],
    )
    out[...] = total[: out.shape[0]].astype(BF16)


def backward_kernel(rows, cols, count_ref, grads, head, tiles, out, held, total, sems):
    add_tiles(
        count_ref[0], head, tiles, held, sems, total,
        lambda slot, tile: jnp.dot(grads[rows[slot]], tile, preferred_element_type=F32),
        lambda slot: cols[slot],
    )
    out[...] = total[: out.shape[0]].astype(BF16)


SMEM = pl.BlockSpec(memory_space=pltpu.SMEM)
VMEM = pl.BlockSpec(memory_space=pltpu.VMEM)
HBM = pl.BlockSpec(memory_space=pltpu.HBM)


def tile_sum(kernel, blocks, tile_rows, tile_cols, tile_count, source, head, tiles):
    slots, size, _ = tiles.shape
    return pl.pallas_call(
        kernel,
        out_shape=pltpu.VMEM((blocks, size, size), BF16),
        in_specs=[SMEM] * 3 + [VMEM, VMEM, HBM],
        out_specs=VMEM,
        scratch_shapes=[
            pltpu.VMEM((slots - UNROLL, size, size), BF16),
            pltpu.VMEM((blocks + 1, size, size), F32),
            pltpu.SemaphoreType.DMA((slots // UNROLL - 1,)),
        ],
        compiler_params=pltpu.CompilerParams(vmem_limit_bytes=32 * MIB),
        cost_estimate=pl.CostEstimate(flops=2 * slots * size**3, bytes_accessed=slots * 2 * size**2, transcendentals=0),
        name=kernel.__name__.replace("kernel", "sum"),
    )(tile_rows, tile_cols, tile_count, source, head, tiles)


HALO_CHUNKS = 4


def halo_kernel(
    features, cotangent, w_self, w_neigh, bias, tiles,
    window, head, own_far, cot_far, w_self_far, w_neigh_far, bias_far,
    load_sems, send_sems, recv_sems,
):
    row, col, edge, core, _ = place()
    rows = lax.axis_size("row")
    up, down = {"row": lax.rem(row + 1, rows)}, {"row": lax.rem(row + rows - 1, rows)}
    twin, partner = {"edge": edge + 1 - 2 * core}, {"col": 1 - col}
    blocks = features.shape[0]
    share = blocks // 8
    greet([up, down, twin, partner])
    send = Sender(send_sems, recv_sems)
    step = blocks // 2 // HALO_CHUNKS
    parts = [pl.ds(core * (blocks // 2) + i * step, step) for i in range(HALO_CHUNKS)]
    arriving = []
    for part in parts:
        for side, peer in ((0, up), (2, down)):
            landing = pl.ds(side * blocks + core * (blocks // 2) + (len(arriving) // 2) * step, step)
            arriving.append((landing, send(features.at[part], window.at[landing], peer)))
    theirs = pl.ds(edge * 2 * share + (1 - col) * share, share)
    theirs_cot = pl.ds((1 - col) * share, share)
    swaps = [
        send(features.at[theirs], own_far, partner),
        send(cotangent.at[theirs_cot], cot_far, partner),
        send(w_self, w_self_far, partner),
        send(w_neigh, w_neigh_far, partner),
        send(bias, bias_far, partner),
    ]
    loads = [
        pltpu.make_async_copy(features, window.at[pl.ds(blocks, blocks)], load_sems.at[0]),
        pltpu.make_async_copy(tiles.at[pl.ds(0, UNROLL)], head, load_sems.at[1]),
    ]
    for load in loads:
        load.start()
    handed = []
    for landing, copy in arriving:
        copy.wait_recv()
        handed.append(send(window.at[landing], window.at[landing], twin))
    for copy in swaps + handed:
        copy.wait_recv()
    for load in loads:
        load.wait()
    send.finish()


def exchange_inputs(features, cotangent, w_self, w_neigh, bias, tiles):
    blocks, size, half = features.shape
    share = blocks // 8
    shapes = [
        jax.ShapeDtypeStruct((3 * blocks, size, half), BF16),
        jax.ShapeDtypeStruct((UNROLL,) + tiles.shape[1:], BF16),
        jax.ShapeDtypeStruct((share, size, half), BF16),
        jax.ShapeDtypeStruct((share, size, half), BF16),
        w_self, w_neigh, bias,
    ]
    copies = 4 * HALO_CHUNKS + 5
    return pl.pallas_call(
        halo_kernel,
        out_shape=[pltpu.VMEM(s.shape, s.dtype) for s in shapes],
        in_specs=[HBM] * 6,
        out_specs=[VMEM] * 7,
        scratch_shapes=[
            pltpu.SemaphoreType.DMA((2,)),
            pltpu.SemaphoreType.DMA((copies,)),
            pltpu.SemaphoreType.DMA((copies,)),
        ],
        compiler_params=pltpu.CompilerParams(collective_id=1, has_side_effects=True, vmem_limit_bytes=32 * MIB),
        name="exchange_inputs",
    )(features, cotangent, w_self, w_neigh, bias, tiles)


def mid_kernel(
    partial, features, own_far, cotangent, cot_far, w_self, w_neigh, w_self_far, w_neigh_far, bias, bias_far, tiles,
    grads, out_near, self_near, weight_sum, far, head,
    got_core, sent, got, own, cot, weights, sent_grads,
    w_all, w_bias, w_sent_z, w_got_z, w_got_x,
    local_sems, send_sems, recv_sems,
):
    row, col, edge, core, pair_side = place()
    other = 1 - col
    twin, pair, partner = {"edge": edge + 1 - 2 * core}, {"edge": lax.rem(edge + 2, 4)}, {"col": other}
    diagonal = {"edge": lax.rem(edge + 2, 4), "col": other}
    x, z = lax.rem(row, 4), lax.div(row, 4)
    along_z = [lax.rem(z + j, 4) for j in (1, 2, 3)]
    x_peers = [{"row": z * 4 + lax.rem(x + j, 4)} for j in (1, 2, 3)]
    z_peers = [{"row": to * 4 + x} for to in along_z]
    blocks, size, half = partial.shape
    share = blocks // 8
    near_rows = own_far.shape[0] * size
    local = [
        pltpu.make_async_copy(features.at[pl.ds(edge * 2 * share + col * share, share)], own, local_sems.at[0]),
        pltpu.make_async_copy(cotangent.at[pl.ds(col * share, share)], cot, local_sems.at[1]),
    ]
    ahead = pltpu.make_async_copy(tiles.at[pl.ds(0, UNROLL)], head, local_sems.at[2])
    for copy in local:
        copy.start()
    ahead.start()
    greet([twin, pair, partner, diagonal] + x_peers + z_peers)
    send = Sender(send_sems, recv_sems)

    def piece(side, on_core, column):
        return pl.ds((2 * side + on_core) * 2 * share + column * share, share)

    order = [(pair_side, other), (1 - pair_side, other), (1 - pair_side, col), (pair_side, col)]
    to_twin = [
        send(partial.at[piece(side, 1 - core, column)], got_core.at[i], twin)
        for i, (side, column) in enumerate(order)
    ]
    near_w, far_w = pl.ds(pl.multiple_of(col * half, half), half), pl.ds(pl.multiple_of(other * half, half), half)
    for k, (near, away) in enumerate(((w_self, w_self_far), (w_neigh, w_neigh_far))):
        for j, rows in enumerate((near_w, far_w)):
            at = pl.ds((2 * k + j) * half, half)
            weights[at, :half] = near[rows, :]
            weights[at, half:] = away[rows, :]

    def summed(i):
        to_twin[i].wait_recv()
        side, column = order[i]
        return partial[piece(side, core, column)].astype(F32) + got_core[i].astype(F32)

    part = share // 2
    halves = [slice(h * part, (h + 1) * part) for h in range(2)]
    owners = (partner, diagonal, pair)
    for i in range(3):
        sent[i] = summed(i).astype(BF16)
        send(sent.at[i, :part], got.at[i, :part], owners[i])
    for i in range(3):
        send(sent.at[i, part:], got.at[i, part:], owners[i])
    arriving = send.used[-6:]
    kept = summed(3)
    for copy in local:
        copy.wait()

    def flat(blocks_of):
        return blocks_of.reshape(-1, half)

    own_full = jnp.concatenate([flat(own[...]), flat(own_far[...])], axis=1)
    own_pre = jnp.dot(own_full, weights[: 2 * half, :], preferred_element_type=F32) + jnp.concatenate(
        [bias[...], bias_far[...]], axis=1
    )
    cot_full = jnp.concatenate([flat(cot[...]), flat(cot_far[...])], axis=1).astype(F32)
    over_cols = (((1,), (1,)), ((), ()))
    mine = edge * 2 * share + col * share
    crossing, handed, done = [], [], []
    for h, at in enumerate(halves):
        for copy in arriving[3 * h : 3 * h + 3]:
            copy.wait_recv()
        rows = slice(h * part * size, (h + 1) * part * size)
        agg_near = (kept[at] + got[2, at].astype(F32)).astype(BF16)
        agg_far = (got[0, at].astype(F32) + got[1, at].astype(F32)).astype(BF16)
        agg = jnp.concatenate([flat(agg_near), flat(agg_far)], axis=1)
        pre = own_pre[rows] + jnp.dot(agg, weights[2 * half :, :], preferred_element_type=F32)
        sigm = jax.nn.sigmoid(pre)
        grad_pre = cot_full[rows] * sigm * (1.0 + pre * (1.0 - sigm))
        grad_low = grad_pre.astype(BF16)
        agg_back = lax.dot_general(
            weights[2 * half :, :], grad_low, over_cols, preferred_element_type=F32
        ).astype(BF16)
        for b in range(part):
            grads[mine + h * part + b] = agg_back[:half, b * size : (b + 1) * size]
            sent_grads[h * part + b] = agg_back[half:, b * size : (b + 1) * size]
        home = pl.ds(mine + h * part, part)
        crossing += [
            send(sent_grads.at[at], grads.at[home], partner),
            send(sent_grads.at[at], grads.at[home], diagonal),
            send(grads.at[home], grads.at[home], pair),
        ]
        handed.append(send(grads.at[home], grads.at[home], twin))
        done.append((agg, pre * sigm, grad_pre, grad_low))
    agg, output, grad_pre, grad_low = (jnp.concatenate(both, axis=0) for both in zip(*done))
    mixed = jnp.concatenate([own_full, agg], axis=1)

    parts = lax.dot_general(mixed, grad_low, (((0,), (0,)), ((), ())), preferred_element_type=F32)
    for k in range(2):
        for j, start in enumerate((col * half, other * half)):
            at = (2 * k + j) * half
            w_all[pl.ds(pl.multiple_of(2 * k * half + start, half), half), :] = parts[at : at + half, :]
    w_bias[...] = jnp.sum(grad_pre.reshape(near_rows // 16, 16, 2 * half), axis=0)

    z_many = 4 * half // 4
    z_start = pl.multiple_of(z * z_many, 8)
    steps = []
    for j in range(3):
        w_sent_z[j, :z_many] = w_all[pl.ds(pl.multiple_of(along_z[j] * z_many, 8), z_many), :].astype(BF16)
        w_sent_z[j, z_many:] = w_bias[...].astype(BF16)
        steps.append(send(w_sent_z.at[j], w_got_z.at[z], z_peers[j]))
    w_got_z[z, z_many:] = w_bias[...].astype(BF16)

    output = output.astype(BF16)
    out_near[...] = output[:, :half]
    far[:near_rows] = output[:, half:]
    self_back = lax.dot_general(grad_low, weights[: 2 * half, :], over_cols, preferred_element_type=F32)
    self_near[...] = self_back[:, :half]
    far[near_rows:] = self_back[:, half:].astype(BF16)

    for step in steps:
        step.wait_recv()
    quarter = w_all[pl.ds(z_start, z_many), :]
    for j in range(3):
        quarter += w_got_z[along_z[j], :z_many].astype(F32)
    bias_sum = w_got_z[0, z_many:].astype(F32)
    for j in range(1, 4):
        bias_sum += w_got_z[j, z_many:].astype(F32)
    w_got_x[x, :z_many] = quarter.astype(BF16)
    w_got_x[x, z_many:] = bias_sum.astype(BF16)
    steps = [send(w_got_x.at[x], w_got_x.at[x], peer) for peer in x_peers]

    far_edge = lax.rem(edge + 2, 4)
    homes = [
        edge * 2 * share + other * share,
        far_edge * 2 * share + other * share,
        far_edge * 2 * share + col * share,
    ]
    for h in range(2):
        for k in range(3):
            crossing[3 * h + k].wait_recv()
            home = pl.ds(homes[k] + h * part, part)
            handed.append(send(grads.at[home], grads.at[home], twin))
    for step in steps:
        step.wait_recv()
    x_total = w_got_x[0].astype(F32)
    for j in range(1, 4):
        x_total += w_got_x[j].astype(F32)
    for j in range(2):
        weight_sum[j] = x_total[:, j * half : (j + 1) * half]
    for copy in handed:
        copy.wait_recv()
    ahead.wait()
    send.finish()


def middle(partial, features, own_far, cotangent, cot_far, w_self, w_neigh, w_self_far, w_neigh_far, bias, bias_far, tiles):
    blocks, size, half = partial.shape
    share = blocks // 8
    rows = share * size
    copies = 4 + 6 + 6 + 8 + 6
    top = 4 * half
    piece = (share, size, half)
    return pl.pallas_call(
        mid_kernel,
        out_shape=[
            pltpu.VMEM((blocks, half, size), BF16),
            pltpu.VMEM((rows, half), BF16),
            pltpu.VMEM((rows, half), F32),
            pltpu.VMEM((2, top // 4 + 16, half), F32),
            pltpu.VMEM((2 * rows, half), BF16),
            pltpu.VMEM((UNROLL,) + tiles.shape[1:], BF16),
        ],
        in_specs=[VMEM, HBM, VMEM, HBM] + [VMEM] * 7 + [HBM],
        out_specs=[VMEM] * 6,
        scratch_shapes=[
            pltpu.VMEM((4,) + piece, BF16),
            pltpu.VMEM((3,) + piece, BF16),
            pltpu.VMEM((3,) + piece, BF16),
            pltpu.VMEM(piece, BF16),
            pltpu.VMEM(piece, BF16),
            pltpu.VMEM((4 * half, 2 * half), BF16),
            pltpu.VMEM((share, half, size), BF16),
            pltpu.VMEM((top, 2 * half), F32),
            pltpu.VMEM((16, 2 * half), F32),
            pltpu.VMEM((3, top // 4 + 16, 2 * half), BF16),
            pltpu.VMEM((4, top // 4 + 16, 2 * half), BF16),
            pltpu.VMEM((4, top // 4 + 16, 2 * half), BF16),
            pltpu.SemaphoreType.DMA((3,)),
            pltpu.SemaphoreType.DMA((copies,)),
            pltpu.SemaphoreType.DMA((copies,)),
        ],
        compiler_params=pltpu.CompilerParams(collective_id=2, has_side_effects=True, vmem_limit_bytes=32 * MIB),
        name="middle",
    )(partial, features, own_far, cotangent, cot_far, w_self, w_neigh, w_self_far, w_neigh_far, bias, bias_far, tiles)


def final_kernel(
    back, weight_sum, far,
    sums, weights, bias_total, far_got,
    got_core, sent_row, kept, got_row, sent_pair, got_pair, w_sent, w_got,
    send_sems, recv_sems,
):
    row, col, edge, core, side = place()
    rows = lax.axis_size("row")
    x, z = lax.rem(row, 4), lax.div(row, 4)
    twin, pair = {"edge": edge + 1 - 2 * core}, {"edge": lax.rem(edge + 2, 4)}
    up, down = {"row": lax.rem(row + 1, rows)}, {"row": lax.rem(row + rows - 1, rows)}
    z_peers = [{"row": lax.rem(z + j, 4) * 4 + x} for j in (1, 2, 3)]
    e_peers = [{"edge": lax.rem(edge + j, 4)} for j in (1, 2, 3)]
    far_peers = [{"edge": lax.rem(edge + j, 4), "col": 1 - col} for j in range(4)]
    greet([up, down] + e_peers + far_peers + z_peers)
    send = Sender(send_sems, recv_sems)
    blocks = back.shape[0] // 3
    share = blocks // 4

    def piece(part, at_side, on_core):
        return pl.ds(part * blocks + (2 * at_side + on_core) * share, share)

    order = [(0, 1 - side), (2, 1 - side), (0, side), (2, side), (1, 1 - side), (1, side)]
    to_twin = [
        send(back.at[piece(part, at, 1 - core)], got_core.at[i], twin) for i, (part, at) in enumerate(order)
    ]

    def summed(i):
        to_twin[i].wait_recv()
        part, at = order[i]
        return back[piece(part, at, core)].astype(F32) + got_core[i].astype(F32)

    top = weights.shape[0]
    many, bias_at = top // 16, top // 4
    to_group = []
    for i, peer in enumerate(e_peers + far_peers):
        j, owner = (0, lax.rem(edge + 1 + i, 4)) if i < 3 else (1, lax.rem(edge + i - 3, 4))
        w_sent[i, :many] = weight_sum[j, pl.ds(pl.multiple_of(owner * many, 8), many), :]
        w_sent[i, many:] = weight_sum[j, bias_at:]
        to_group.append(send(w_sent.at[i], w_got.at[i], peer))

    to_row = []
    for i in range(4):
        sent_row[i] = summed(i).astype(BF16)
        to_row.append(send(sent_row.at[i], got_row.at[i], down if i % 2 == 0 else up))

    to_partner = send(far, far_got, far_peers[0])
    for copy in to_group:
        copy.wait_recv()
    group_total = w_got[0]
    for i in range(1, 7):
        group_total += w_got[i]
    start = pl.multiple_of(z * (top // 4) + edge * many, 8)
    weights[pl.ds(start, many), :] = weight_sum[0, pl.ds(pl.multiple_of(edge * many, 8), many), :] + group_total[:many]
    bias_total[...] = weight_sum[0, bias_at:] + group_total[many:]

    def gathered(start, many, peers):
        at = pl.ds(pl.multiple_of(start, 8), many)
        return [send(weights.at[at], weights.at[at], peer) for peer in peers]

    steps = gathered(start, many, e_peers)
    for i in range(2):
        kept[i] = summed(4 + i)
    for step in steps:
        step.wait_recv()
    steps = gathered(z * (top // 4), top // 4, z_peers)
    for i in range(2):
        to_row[i].wait_recv()
    sent_pair[...] = (kept[0] + got_row[0].astype(F32) + got_row[1].astype(F32)).astype(BF16)
    to_pair = send(sent_pair, got_pair, pair)
    for i in range(2, 4):
        to_row[i].wait_recv()
    kept[1] += got_row[2].astype(F32) + got_row[3].astype(F32)
    to_pair.wait_recv()
    sums[...] = kept[1] + got_pair[...].astype(F32)
    to_partner.wait_recv()
    for step in steps:
        step.wait_recv()
    send.finish()


def finish(back, weight_sum, far):
    share, half, size = back.shape[0] // 12, back.shape[1], back.shape[2]
    unit = half // 4 + 16
    copies = 6 + 1 + 4 + 1 + 7 + 6
    piece = (share, half, size)
    return pl.pallas_call(
        final_kernel,
        out_shape=[
            pltpu.VMEM(piece, F32),
            pltpu.VMEM((4 * half, half), F32),
            pltpu.VMEM((16, half), F32),
            pltpu.VMEM(far.shape, BF16),
        ],
        in_specs=[VMEM] * 3,
        out_specs=[VMEM] * 4,
        scratch_shapes=[
            pltpu.VMEM((6,) + piece, BF16),
            pltpu.VMEM((4,) + piece, BF16),
            pltpu.VMEM((2,) + piece, F32),
            pltpu.VMEM((4,) + piece, BF16),
            pltpu.VMEM(piece, BF16),
            pltpu.VMEM(piece, BF16),
            *[pltpu.VMEM((7, unit, half), F32)] * 2,
            pltpu.SemaphoreType.DMA((copies,)),
            pltpu.SemaphoreType.DMA((copies,)),
        ],
        compiler_params=pltpu.CompilerParams(collective_id=3, has_side_effects=True, vmem_limit_bytes=32 * MIB),
        name="finish",
    )(back, weight_sum, far)


def writing_kernel(
    scale, out_near, self_near, far, sums, weights, bias_total,
    output, features_grad, w_self_grad, w_neigh_grad, bias_grad,
):
    col = lax.axis_index("col")
    rows, half = out_near.shape
    near, away = pl.multiple_of(col * rows, 16), pl.multiple_of((1 - col) * rows, 16)
    output[pl.ds(near, rows), :] = out_near[...]
    output[pl.ds(away, rows), :] = far[:rows]
    features_grad[pl.ds(near, rows), :] = self_near[...]
    features_grad[pl.ds(away, rows), :] = far[rows:].astype(F32)
    share, _, size = sums.shape
    for b in range(share):
        features_grad[b * size : (b + 1) * size, :] += sums[b].T
    top = weights.shape[0]
    w_self_grad[...] = weights[: top // 2] * scale
    w_neigh_grad[...] = weights[top // 2 :] * scale
    bias_grad[...] = jnp.sum(bias_total[...], axis=0, keepdims=True) * scale


def written(scale, out_near, self_near, far, sums, weights, bias_total):
    rows, half = out_near.shape
    top = weights.shape[0]
    return pl.pallas_call(
        functools.partial(writing_kernel, scale),
        out_shape=[
            jax.ShapeDtypeStruct((2 * rows, half), BF16),
            jax.ShapeDtypeStruct((2 * rows, half), F32),
            jax.ShapeDtypeStruct((top // 2, half), F32),
            jax.ShapeDtypeStruct((top // 2, half), F32),
            jax.ShapeDtypeStruct((1, half), F32),
        ],
        in_specs=[VMEM] * 6,
        out_specs=[VMEM] * 5,
        compiler_params=pltpu.CompilerParams(vmem_limit_bytes=4 * MIB),
        name="written",
    )(out_near, self_near, far, sums, weights, bias_total)


def local(features, tiles, tile_rows, tile_cols, tile_count, w_self, w_neigh, bias, cotangent):
    rows_dev, half = features.shape
    size = tiles.shape[1]
    blocks = rows_dev // size
    nodes = rows_dev * lax.axis_size("row")
    scale = 1.0 / math.sqrt(nodes)

    own = features.reshape(blocks, size, half)
    cot = cotangent.reshape(-1, size, half)
    bias_row = bias.reshape(1, half)
    own, cot, w_self, w_neigh, bias_row, tile_rows, tile_cols, tiles = (
        pltpu.with_memory_space_constraint(array, pltpu.HBM)
        for array in (own, cot, w_self, w_neigh, bias_row, tile_rows, tile_cols, tiles)
    )
    window, head, own_far, cot_far, w_self_far, w_neigh_far, bias_far = exchange_inputs(
        own, cot, w_self, w_neigh, bias_row, tiles
    )
    partial = tile_sum(forward_kernel, blocks, tile_rows, tile_cols, tile_count, window, head, tiles)
    grads, out_near, self_near, weight_sum, far, head = middle(
        partial, own, own_far, cot, cot_far, w_self, w_neigh, w_self_far, w_neigh_far, bias_row, bias_far, tiles
    )
    back = tile_sum(backward_kernel, 3 * blocks, tile_rows, tile_cols, tile_count, grads, head, tiles)
    sums, weights, bias_total, far = finish(back, weight_sum, far)
    output, features_grad, w_self_grad, w_neigh_grad, bias_grad = written(
        scale, out_near, self_near, far, sums, weights, bias_total
    )
    return (output, features_grad, w_self_grad, w_neigh_grad, bias_grad.reshape(half))


def solution(mesh):
    return jax.shard_map(
        local,
        mesh=mesh,
        in_specs=(
            P("row", "col"),
            P(("row", "edge"), None, None),
            P(("row", "edge")),
            P(("row", "edge")),
            P(("row", "edge")),
            P(None, "col"),
            P(None, "col"),
            P("col"),
            P(("row", "edge"), "col"),
        ),
        out_specs=(
            P(("row", "edge"), "col"),
            P(("row", "edge"), "col"),
            P(None, "col"),
            P(None, "col"),
            P("col"),
        ),
        check_vma=False,
    )
```

```python
import functools
import math

import jax
import jax.numpy as jnp
from jax import lax
from jax.experimental import pallas as pl
from jax.experimental.pallas import tpu as pltpu
from jax.sharding import PartitionSpec as P

F32 = jnp.float32
BF16 = jnp.bfloat16
UNROLL = 88
LAG = 4
MIB = 1024 * 1024


MESH = pl.DeviceIdType.MESH


def place():
    row, col, edge = (lax.axis_index(name) for name in ("row", "col", "edge"))
    return row, col, edge, lax.rem(edge, 2), lax.div(edge, 2)


def greet(peers):
    barrier = pltpu.get_barrier_semaphore()
    for peer in peers:
        pl.semaphore_signal(barrier, inc=1, device_id=peer, device_id_type=MESH)
    pl.semaphore_wait(barrier, len(peers))


class Sender:
    def __init__(self, send_sems, recv_sems):
        self.send_sems, self.recv_sems, self.used = send_sems, recv_sems, []

    def __call__(self, src, dst, peer):
        index = len(self.used)
        copy = pltpu.make_async_remote_copy(
            src_ref=src,
            dst_ref=dst,
            send_sem=self.send_sems.at[index],
            recv_sem=self.recv_sems.at[index],
            device_id=peer,
            device_id_type=MESH,
        )
        copy.start()
        self.used.append(copy)
        return copy

    def finish(self):
        for copy in self.used:
            copy.wait_send()


def add_tiles(count, head, tiles, held, sems, total, product, target):
    spare = total.shape[0] - 1
    groups = lax.div(count + UNROLL - 1, UNROLL)

    def fetch(g):
        at = pl.ds(g * UNROLL, UNROLL)
        return pltpu.make_async_copy(tiles.at[at], held.at[pl.ds((g - 1) * UNROLL, UNROLL)], sems.at[g - 1])

    def start_step(g, carry):
        fetch(g).start()
        return carry

    lax.fori_loop(1, groups, start_step, 0)
    total[...] = jnp.zeros_like(total)

    def add_group(source, first, start):
        waiting = {}
        for u in range(UNROLL + LAG):
            if u < UNROLL:
                waiting[u] = product(start + u, source[first + u])
            if u >= LAG:
                slot = start + u - LAG
                total[jnp.where(slot < count, target(slot), spare)] += waiting.pop(u - LAG)

    add_group(head, 0, 0)

    def group_step(g, carry):
        fetch(g).wait()
        add_group(held, (g - 1) * UNROLL, g * UNROLL)
        return carry

    lax.fori_loop(1, groups, group_step, 0)


def forward_kernel(rows, cols, count_ref, window, head, tiles, out, held, total, sems):
    add_tiles(
        count_ref[0], head, tiles, held, sems, total,
        lambda slot, tile: jnp.dot(tile, window[cols[slot]], preferred_element_type=F32),
        lambda slot: rows[slot],
    )
    out[...] = total[: out.shape[0]].astype(BF16)


def backward_kernel(rows, cols, count_ref, grads, head, tiles, out, held, total, sems):
    add_tiles(
        count_ref[0], head, tiles, held, sems, total,
        lambda slot, tile: jnp.dot(grads[rows[slot]], tile, preferred_element_type=F32),
        lambda slot: cols[slot],
    )
    out[...] = total[: out.shape[0]].astype(BF16)


SMEM = pl.BlockSpec(memory_space=pltpu.SMEM)
VMEM = pl.BlockSpec(memory_space=pltpu.VMEM)
HBM = pl.BlockSpec(memory_space=pltpu.HBM)


def tile_sum(kernel, blocks, tile_rows, tile_cols, tile_count, source, head, tiles):
    slots, size, _ = tiles.shape
    return pl.pallas_call(
        kernel,
        out_shape=pltpu.VMEM((blocks, size, size), BF16),
        in_specs=[SMEM] * 3 + [VMEM, VMEM, HBM],
        out_specs=VMEM,
        scratch_shapes=[
            pltpu.VMEM((slots - UNROLL, size, size), BF16),
            pltpu.VMEM((blocks + 1, size, size), F32),
            pltpu.SemaphoreType.DMA((slots // UNROLL - 1,)),
        ],
        compiler_params=pltpu.CompilerParams(vmem_limit_bytes=32 * MIB),
        cost_estimate=pl.CostEstimate(flops=2 * slots * size**3, bytes_accessed=slots * 2 * size**2, transcendentals=0),
        name=kernel.__name__.replace("kernel", "sum"),
    )(tile_rows, tile_cols, tile_count, source, head, tiles)


HALO_CHUNKS = 4


def halo_kernel(
    features, cotangent, w_self, w_neigh, bias, tiles,
    window, head, own_far, cot_far, w_self_far, w_neigh_far, bias_far,
    load_sems, send_sems, recv_sems,
):
    row, col, edge, core, _ = place()
    rows = lax.axis_size("row")
    up, down = {"row": lax.rem(row + 1, rows)}, {"row": lax.rem(row + rows - 1, rows)}
    twin, partner = {"edge": edge + 1 - 2 * core}, {"col": 1 - col}
    blocks = features.shape[0]
    share = blocks // 8
    greet([up, down, twin, partner])
    send = Sender(send_sems, recv_sems)
    step = blocks // 2 // HALO_CHUNKS
    parts = [pl.ds(core * (blocks // 2) + i * step, step) for i in range(HALO_CHUNKS)]
    arriving = []
    for part in parts:
        for side, peer in ((0, up), (2, down)):
            landing = pl.ds(side * blocks + core * (blocks // 2) + (len(arriving) // 2) * step, step)
            arriving.append((landing, send(features.at[part], window.at[landing], peer)))
    theirs = pl.ds(edge * 2 * share + (1 - col) * share, share)
    theirs_cot = pl.ds((1 - col) * share, share)
    swaps = [
        send(features.at[theirs], own_far, partner),
        send(cotangent.at[theirs_cot], cot_far, partner),
        send(w_self, w_self_far, partner),
        send(w_neigh, w_neigh_far, partner),
        send(bias, bias_far, partner),
    ]
    loads = [
        pltpu.make_async_copy(features, window.at[pl.ds(blocks, blocks)], load_sems.at[0]),
        pltpu.make_async_copy(tiles.at[pl.ds(0, UNROLL)], head, load_sems.at[1]),
    ]
    for load in loads:
        load.start()
    handed = []
    for landing, copy in arriving:
        copy.wait_recv()
        handed.append(send(window.at[landing], window.at[landing], twin))
    for copy in swaps + handed:
        copy.wait_recv()
    for load in loads:
        load.wait()
    send.finish()


def exchange_inputs(features, cotangent, w_self, w_neigh, bias, tiles):
    blocks, size, half = features.shape
    share = blocks // 8
    shapes = [
        jax.ShapeDtypeStruct((3 * blocks, size, half), BF16),
        jax.ShapeDtypeStruct((UNROLL,) + tiles.shape[1:], BF16),
        jax.ShapeDtypeStruct((share, size, half), BF16),
        jax.ShapeDtypeStruct((share, size, half), BF16),
        w_self, w_neigh, bias,
    ]
    copies = 4 * HALO_CHUNKS + 5
    return pl.pallas_call(
        halo_kernel,
        out_shape=[pltpu.VMEM(s.shape, s.dtype) for s in shapes],
        in_specs=[HBM] * 6,
        out_specs=[VMEM] * 7,
        scratch_shapes=[
            pltpu.SemaphoreType.DMA((2,)),
            pltpu.SemaphoreType.DMA((copies,)),
            pltpu.SemaphoreType.DMA((copies,)),
        ],
        compiler_params=pltpu.CompilerParams(collective_id=1, has_side_effects=True, vmem_limit_bytes=32 * MIB),
        name="exchange_inputs",
    )(features, cotangent, w_self, w_neigh, bias, tiles)


def mid_kernel(
    partial, features, own_far, cotangent, cot_far, w_self, w_neigh, w_self_far, w_neigh_far, bias, bias_far, tiles,
    grads, out_near, self_near, weight_sum, far, head,
    got_core, sent, got, own, cot, weights, sent_grads,
    w_all, w_bias, w_sent_z, w_got_z, w_got_x,
    local_sems, send_sems, recv_sems,
):
    row, col, edge, core, pair_side = place()
    other = 1 - col
    twin, pair, partner = {"edge": edge + 1 - 2 * core}, {"edge": lax.rem(edge + 2, 4)}, {"col": other}
    diagonal = {"edge": lax.rem(edge + 2, 4), "col": other}
    x, z = lax.rem(row, 4), lax.div(row, 4)
    along_z = [lax.rem(z + j, 4) for j in (1, 2, 3)]
    x_peers = [{"row": z * 4 + lax.rem(x + j, 4)} for j in (1, 2, 3)]
    z_peers = [{"row": to * 4 + x} for to in along_z]
    blocks, size, half = partial.shape
    share = blocks // 8
    near_rows = own_far.shape[0] * size
    local = [
        pltpu.make_async_copy(features.at[pl.ds(edge * 2 * share + col * share, share)], own, local_sems.at[0]),
        pltpu.make_async_copy(cotangent.at[pl.ds(col * share, share)], cot, local_sems.at[1]),
    ]
    ahead = pltpu.make_async_copy(tiles.at[pl.ds(0, UNROLL)], head, local_sems.at[2])
    for copy in local:
        copy.start()
    ahead.start()
    greet([twin, pair, partner, diagonal] + x_peers + z_peers)
    send = Sender(send_sems, recv_sems)

    def piece(side, on_core, column):
        return pl.ds((2 * side + on_core) * 2 * share + column * share, share)

    order = [(pair_side, other), (1 - pair_side, other), (1 - pair_side, col), (pair_side, col)]
    to_twin = [
        send(partial.at[piece(side, 1 - core, column)], got_core.at[i], twin)
        for i, (side, column) in enumerate(order)
    ]
    near_w, far_w = pl.ds(pl.multiple_of(col * half, half), half), pl.ds(pl.multiple_of(other * half, half), half)
    for k, (near, away) in enumerate(((w_self, w_self_far), (w_neigh, w_neigh_far))):
        for j, rows in enumerate((near_w, far_w)):
            at = pl.ds((2 * k + j) * half, half)
            weights[at, :half] = near[rows, :]
            weights[at, half:] = away[rows, :]

    def summed(i):
        to_twin[i].wait_recv()
        side, column = order[i]
        return partial[piece(side, core, column)].astype(F32) + got_core[i].astype(F32)

    part = share // 2
    halves = [slice(h * part, (h + 1) * part) for h in range(2)]
    owners = (partner, diagonal, pair)
    for i in range(3):
        sent[i] = summed(i).astype(BF16)
        send(sent.at[i, :part], got.at[i, :part], owners[i])
    for i in range(3):
        send(sent.at[i, part:], got.at[i, part:], owners[i])
    arriving = send.used[-6:]
    kept = summed(3)
    for copy in local:
        copy.wait()

    def flat(blocks_of):
        return blocks_of.reshape(-1, half)

    own_full = jnp.concatenate([flat(own[...]), flat(own_far[...])], axis=1)
    own_pre = jnp.dot(own_full, weights[: 2 * half, :], preferred_element_type=F32) + jnp.concatenate(
        [bias[...], bias_far[...]], axis=1
    )
    cot_full = jnp.concatenate([flat(cot[...]), flat(cot_far[...])], axis=1).astype(F32)
    over_cols = (((1,), (1,)), ((), ()))
    mine = edge * 2 * share + col * share
    crossing, handed, done = [], [], []
    for h, at in enumerate(halves):
        for copy in arriving[3 * h : 3 * h + 3]:
            copy.wait_recv()
        rows = slice(h * part * size, (h + 1) * part * size)
        agg_near = (kept[at] + got[2, at].astype(F32)).astype(BF16)
        agg_far = (got[0, at].astype(F32) + got[1, at].astype(F32)).astype(BF16)
        agg = jnp.concatenate([flat(agg_near), flat(agg_far)], axis=1)
        pre = own_pre[rows] + jnp.dot(agg, weights[2 * half :, :], preferred_element_type=F32)
        sigm = jax.nn.sigmoid(pre)
        grad_pre = cot_full[rows] * sigm * (1.0 + pre * (1.0 - sigm))
        grad_low = grad_pre.astype(BF16)
        agg_back = lax.dot_general(
            weights[2 * half :, :], grad_low, over_cols, preferred_element_type=F32
        ).astype(BF16)
        for b in range(part):
            grads[mine + h * part + b] = agg_back[:half, b * size : (b + 1) * size]
            sent_grads[h * part + b] = agg_back[half:, b * size : (b + 1) * size]
        home = pl.ds(mine + h * part, part)
        crossing += [
            send(sent_grads.at[at], grads.at[home], partner),
            send(sent_grads.at[at], grads.at[home], diagonal),
            send(grads.at[home], grads.at[home], pair),
        ]
        handed.append(send(grads.at[home], grads.at[home], twin))
        done.append((agg, pre * sigm, grad_pre, grad_low))
    agg, output, grad_pre, grad_low = (jnp.concatenate(both, axis=0) for both in zip(*done))
    mixed = jnp.concatenate([own_full, agg], axis=1)

    parts = lax.dot_general(mixed, grad_low, (((0,), (0,)), ((), ())), preferred_element_type=F32)
    for k in range(2):
        for j, start in enumerate((col * half, other * half)):
            at = (2 * k + j) * half
            w_all[pl.ds(pl.multiple_of(2 * k * half + start, half), half), :] = parts[at : at + half, :]
    w_bias[...] = jnp.sum(grad_pre.reshape(near_rows // 16, 16, 2 * half), axis=0)

    z_many = 4 * half // 4
    z_start = pl.multiple_of(z * z_many, 8)
    steps = []
    for j in range(3):
        w_sent_z[j, :z_many] = w_all[pl.ds(pl.multiple_of(along_z[j] * z_many, 8), z_many), :].astype(BF16)
        w_sent_z[j, z_many:] = w_bias[...].astype(BF16)
        steps.append(send(w_sent_z.at[j], w_got_z.at[z], z_peers[j]))
    w_got_z[z, z_many:] = w_bias[...].astype(BF16)

    output = output.astype(BF16)
    out_near[...] = output[:, :half]
    far[:near_rows] = output[:, half:]
    self_back = lax.dot_general(grad_low, weights[: 2 * half, :], over_cols, preferred_element_type=F32)
    self_near[...] = self_back[:, :half]
    far[near_rows:] = self_back[:, half:].astype(BF16)

    for step in steps:
        step.wait_recv()
    quarter = w_all[pl.ds(z_start, z_many), :]
    for j in range(3):
        quarter += w_got_z[along_z[j], :z_many].astype(F32)
    bias_sum = w_got_z[0, z_many:].astype(F32)
    for j in range(1, 4):
        bias_sum += w_got_z[j, z_many:].astype(F32)
    w_got_x[x, :z_many] = quarter.astype(BF16)
    w_got_x[x, z_many:] = bias_sum.astype(BF16)
    steps = [send(w_got_x.at[x], w_got_x.at[x], peer) for peer in x_peers]

    far_edge = lax.rem(edge + 2, 4)
    homes = [
        edge * 2 * share + other * share,
        far_edge * 2 * share + other * share,
        far_edge * 2 * share + col * share,
    ]
    for h in range(2):
        for k in range(3):
            crossing[3 * h + k].wait_recv()
            home = pl.ds(homes[k] + h * part, part)
            handed.append(send(grads.at[home], grads.at[home], twin))
    for step in steps:
        step.wait_recv()
    x_total = w_got_x[0].astype(F32)
    for j in range(1, 4):
        x_total += w_got_x[j].astype(F32)
    for j in range(2):
        weight_sum[j] = x_total[:, j * half : (j + 1) * half]
    for copy in handed:
        copy.wait_recv()
    ahead.wait()
    send.finish()


def middle(partial, features, own_far, cotangent, cot_far, w_self, w_neigh, w_self_far, w_neigh_far, bias, bias_far, tiles):
    blocks, size, half = partial.shape
    share = blocks // 8
    rows = share * size
    copies = 4 + 6 + 6 + 8 + 6
    top = 4 * half
    piece = (share, size, half)
    return pl.pallas_call(
        mid_kernel,
        out_shape=[
            pltpu.VMEM((blocks, half, size), BF16),
            pltpu.VMEM((rows, half), BF16),
            pltpu.VMEM((rows, half), F32),
            pltpu.VMEM((2, top // 4 + 16, half), F32),
            pltpu.VMEM((2 * rows, half), BF16),
            pltpu.VMEM((UNROLL,) + tiles.shape[1:], BF16),
        ],
        in_specs=[VMEM, HBM, VMEM, HBM] + [VMEM] * 7 + [HBM],
        out_specs=[VMEM] * 6,
        scratch_shapes=[
            pltpu.VMEM((4,) + piece, BF16),
            pltpu.VMEM((3,) + piece, BF16),
            pltpu.VMEM((3,) + piece, BF16),
            pltpu.VMEM(piece, BF16),
            pltpu.VMEM(piece, BF16),
            pltpu.VMEM((4 * half, 2 * half), BF16),
            pltpu.VMEM((share, half, size), BF16),
            pltpu.VMEM((top, 2 * half), F32),
            pltpu.VMEM((16, 2 * half), F32),
            pltpu.VMEM((3, top // 4 + 16, 2 * half), BF16),
            pltpu.VMEM((4, top // 4 + 16, 2 * half), BF16),
            pltpu.VMEM((4, top // 4 + 16, 2 * half), BF16),
            pltpu.SemaphoreType.DMA((3,)),
            pltpu.SemaphoreType.DMA((copies,)),
            pltpu.SemaphoreType.DMA((copies,)),
        ],
        compiler_params=pltpu.CompilerParams(collective_id=2, has_side_effects=True, vmem_limit_bytes=32 * MIB),
        name="middle",
    )(partial, features, own_far, cotangent, cot_far, w_self, w_neigh, w_self_far, w_neigh_far, bias, bias_far, tiles)


def final_kernel(
    back, weight_sum, far,
    sums, weights, bias_total, far_got,
    got_core, sent_row, kept, got_row, sent_pair, got_pair, w_sent, w_got,
    send_sems, recv_sems,
):
    row, col, edge, core, side = place()
    rows = lax.axis_size("row")
    x, z = lax.rem(row, 4), lax.div(row, 4)
    twin, pair = {"edge": edge + 1 - 2 * core}, {"edge": lax.rem(edge + 2, 4)}
    up, down = {"row": lax.rem(row + 1, rows)}, {"row": lax.rem(row + rows - 1, rows)}
    z_peers = [{"row": lax.rem(z + j, 4) * 4 + x} for j in (1, 2, 3)]
    e_peers = [{"edge": lax.rem(edge + j, 4)} for j in (1, 2, 3)]
    far_peers = [{"edge": lax.rem(edge + j, 4), "col": 1 - col} for j in range(4)]
    greet([up, down] + e_peers + far_peers + z_peers)
    send = Sender(send_sems, recv_sems)
    blocks = back.shape[0] // 3
    share = blocks // 4

    def piece(part, at_side, on_core):
        return pl.ds(part * blocks + (2 * at_side + on_core) * share, share)

    order = [(0, 1 - side), (2, 1 - side), (0, side), (2, side), (1, 1 - side), (1, side)]
    to_twin = [
        send(back.at[piece(part, at, 1 - core)], got_core.at[i], twin) for i, (part, at) in enumerate(order)
    ]

    def summed(i):
        to_twin[i].wait_recv()
        part, at = order[i]
        return back[piece(part, at, core)].astype(F32) + got_core[i].astype(F32)

    top = weights.shape[0]
    many, bias_at = top // 16, top // 4
    to_group = []
    for i, peer in enumerate(e_peers + far_peers):
        j, owner = (0, lax.rem(edge + 1 + i, 4)) if i < 3 else (1, lax.rem(edge + i - 3, 4))
        w_sent[i, :many] = weight_sum[j, pl.ds(pl.multiple_of(owner * many, 8), many), :]
        w_sent[i, many:] = weight_sum[j, bias_at:]
        to_group.append(send(w_sent.at[i], w_got.at[i], peer))

    to_row = []
    for i in range(4):
        sent_row[i] = summed(i).astype(BF16)
        to_row.append(send(sent_row.at[i], got_row.at[i], down if i % 2 == 0 else up))

    to_partner = send(far, far_got, far_peers[0])
    for copy in to_group:
        copy.wait_recv()
    group_total = w_got[0]
    for i in range(1, 7):
        group_total += w_got[i]
    start = pl.multiple_of(z * (top // 4) + edge * many, 8)
    weights[pl.ds(start, many), :] = weight_sum[0, pl.ds(pl.multiple_of(edge * many, 8), many), :] + group_total[:many]
    bias_total[...] = weight_sum[0, bias_at:] + group_total[many:]

    def gathered(start, many, peers):
        at = pl.ds(pl.multiple_of(start, 8), many)
        return [send(weights.at[at], weights.at[at], peer) for peer in peers]

    steps = gathered(start, many, e_peers)
    for i in range(2):
        kept[i] = summed(4 + i)
    for i in range(2):
        to_row[i].wait_recv()
    sent_pair[...] = (kept[0] + got_row[0].astype(F32) + got_row[1].astype(F32)).astype(BF16)
    to_pair = send(sent_pair, got_pair, pair)
    for step in steps:
        step.wait_recv()
    steps = gathered(z * (top // 4), top // 4, z_peers)
    for i in range(2, 4):
        to_row[i].wait_recv()
    kept[1] += got_row[2].astype(F32) + got_row[3].astype(F32)
    to_pair.wait_recv()
    sums[...] = kept[1] + got_pair[...].astype(F32)
    to_partner.wait_recv()
    for step in steps:
        step.wait_recv()
    send.finish()


def finish(back, weight_sum, far):
    share, half, size = back.shape[0] // 12, back.shape[1], back.shape[2]
    unit = half // 4 + 16
    copies = 6 + 1 + 4 + 1 + 7 + 6
    piece = (share, half, size)
    return pl.pallas_call(
        final_kernel,
        out_shape=[
            pltpu.VMEM(piece, F32),
            pltpu.VMEM((4 * half, half), F32),
            pltpu.VMEM((16, half), F32),
            pltpu.VMEM(far.shape, BF16),
        ],
        in_specs=[VMEM] * 3,
        out_specs=[VMEM] * 4,
        scratch_shapes=[
            pltpu.VMEM((6,) + piece, BF16),
            pltpu.VMEM((4,) + piece, BF16),
            pltpu.VMEM((2,) + piece, F32),
            pltpu.VMEM((4,) + piece, BF16),
            pltpu.VMEM(piece, BF16),
            pltpu.VMEM(piece, BF16),
            *[pltpu.VMEM((7, unit, half), F32)] * 2,
            pltpu.SemaphoreType.DMA((copies,)),
            pltpu.SemaphoreType.DMA((copies,)),
        ],
        compiler_params=pltpu.CompilerParams(collective_id=3, has_side_effects=True, vmem_limit_bytes=32 * MIB),
        name="finish",
    )(back, weight_sum, far)


def writing_kernel(
    scale, out_near, self_near, far, sums, weights, bias_total,
    output, features_grad, w_self_grad, w_neigh_grad, bias_grad,
):
    col = lax.axis_index("col")
    rows, half = out_near.shape
    near, away = pl.multiple_of(col * rows, 16), pl.multiple_of((1 - col) * rows, 16)
    output[pl.ds(near, rows), :] = out_near[...]
    output[pl.ds(away, rows), :] = far[:rows]
    features_grad[pl.ds(near, rows), :] = self_near[...]
    features_grad[pl.ds(away, rows), :] = far[rows:].astype(F32)
    share, _, size = sums.shape
    for b in range(share):
        features_grad[b * size : (b + 1) * size, :] += sums[b].T
    top = weights.shape[0]
    w_self_grad[...] = weights[: top // 2] * scale
    w_neigh_grad[...] = weights[top // 2 :] * scale
    bias_grad[...] = jnp.sum(bias_total[...], axis=0, keepdims=True) * scale


def written(scale, out_near, self_near, far, sums, weights, bias_total):
    rows, half = out_near.shape
    top = weights.shape[0]
    return pl.pallas_call(
        functools.partial(writing_kernel, scale),
        out_shape=[
            jax.ShapeDtypeStruct((2 * rows, half), BF16),
            jax.ShapeDtypeStruct((2 * rows, half), F32),
            jax.ShapeDtypeStruct((top // 2, half), F32),
            jax.ShapeDtypeStruct((top // 2, half), F32),
            jax.ShapeDtypeStruct((1, half), F32),
        ],
        in_specs=[VMEM] * 6,
        out_specs=[VMEM] * 5,
        compiler_params=pltpu.CompilerParams(vmem_limit_bytes=4 * MIB),
        name="written",
    )(out_near, self_near, far, sums, weights, bias_total)


def local(features, tiles, tile_rows, tile_cols, tile_count, w_self, w_neigh, bias, cotangent):
    rows_dev, half = features.shape
    size = tiles.shape[1]
    blocks = rows_dev // size
    nodes = rows_dev * lax.axis_size("row")
    scale = 1.0 / math.sqrt(nodes)

    own = features.reshape(blocks, size, half)
    cot = cotangent.reshape(-1, size, half)
    bias_row = bias.reshape(1, half)
    own, cot, w_self, w_neigh, bias_row, tile_rows, tile_cols, tiles = (
        pltpu.with_memory_space_constraint(array, pltpu.HBM)
        for array in (own, cot, w_self, w_neigh, bias_row, tile_rows, tile_cols, tiles)
    )
    window, head, own_far, cot_far, w_self_far, w_neigh_far, bias_far = exchange_inputs(
        own, cot, w_self, w_neigh, bias_row, tiles
    )
    partial = tile_sum(forward_kernel, blocks, tile_rows, tile_cols, tile_count, window, head, tiles)
    grads, out_near, self_near, weight_sum, far, head = middle(
        partial, own, own_far, cot, cot_far, w_self, w_neigh, w_self_far, w_neigh_far, bias_row, bias_far, tiles
    )
    back = tile_sum(backward_kernel, 3 * blocks, tile_rows, tile_cols, tile_count, grads, head, tiles)
    sums, weights, bias_total, far = finish(back, weight_sum, far)
    output, features_grad, w_self_grad, w_neigh_grad, bias_grad = written(
        scale, out_near, self_near, far, sums, weights, bias_total
    )
    return (output, features_grad, w_self_grad, w_neigh_grad, bias_grad.reshape(half))


def solution(mesh):
    return jax.shard_map(
        local,
        mesh=mesh,
        in_specs=(
            P("row", "col"),
            P(("row", "edge"), None, None),
            P(("row", "edge")),
            P(("row", "edge")),
            P(("row", "edge")),
            P(None, "col"),
            P(None, "col"),
            P("col"),
            P(("row", "edge"), "col"),
        ),
        out_specs=(
            P(("row", "edge"), "col"),
            P(("row", "edge"), "col"),
            P(None, "col"),
            P(None, "col"),
            P("col"),
        ),
        check_vma=False,
    )
```
